32 devices in a mesh: dp: 8 (over y, x, core), tensor: 4 (over z).
Axes of the slice: x: 2, y: 2, z: 4, core: 2. Of those that a mesh axis runs over, the one named last changes fastest.
Arguments:
- block_input: bfloat16 [24576, 768], P('dp'), may hold values from -6 to 6
- cotangent: bfloat16 [24576, 768], P('dp'), may hold values from -6 to 6
- heads_weight: bfloat16 [768, 2304], P('dp', 'tensor'), may hold values from -0.21875 to 0.21875
- heads_bias: bfloat16 [2304], P(('tensor', 'dp')), may hold values from -3 to 3
- merge_weight: bfloat16 [768, 768], P('tensor', 'dp'), may hold values from -0.875 to 0.875
- merge_bias: bfloat16 [768], P('dp'), may hold values from -3 to 3
- up_weight: bfloat16 [768, 3072], P('dp', 'tensor'), may hold values from -0.21875 to 0.21875
- up_bias: bfloat16 [3072], P(('tensor', 'dp')), may hold values from -3 to 3
- down_weight: bfloat16 [3072, 768], P('tensor', 'dp'), may hold values from -0.15625 to 0.15625
- down_bias: bfloat16 [768], P('dp'), may hold values from -3 to 3
- first_gain: bfloat16 [768], P('dp'), may hold values from 0.099609375 to 1.8984375
- first_shift: bfloat16 [768], P('dp'), may hold values from -2 to 2
- second_gain: bfloat16 [768], P('dp'), may hold values from 0.099609375 to 1.8984375
- second_shift: bfloat16 [768], P('dp'), may hold values from -2 to 2
Outputs:
- layer_output: bfloat16 [24576, 768], P('dp')
- input_grad: float32 [24576, 768], P('dp')
- heads_weight_grad: float32 [768, 2304], P('dp', 'tensor')
- heads_bias_grad: float32 [2304], P(('tensor', 'dp'))
- merge_weight_grad: float32 [768, 768], P('tensor', 'dp')
- merge_bias_grad: float32 [768], P('dp')
- up_weight_grad: float32 [768, 3072], P('dp', 'tensor')
- up_bias_grad: float32 [3072], P(('tensor', 'dp'))
- down_weight_grad: float32 [3072, 768], P('tensor', 'dp')
- down_bias_grad: float32 [768], P('dp')
- first_gain_grad: float32 [768], P('dp')
- first_shift_grad: float32 [768], P('dp')
- second_gain_grad: float32 [768], P('dp')
- second_shift_grad: float32 [768], P('dp')
The draws below stay inside these ranges and needn't reach their ends.
All inputs are finite; a program needn't handle non-finite values.
Results may differ from the reference program's by a relative error of at most 0.012.
Values may be sent and summed in bfloat16 or wider, within the bound.
No kernel may reach another device: no remote copies, remote signals or barrier semaphores. Data moves between devices by JAX's collectives and lax.ppermute only.
A program may use at most 192 MiB of HBM per device.

```python
import math
import jax
import jax.numpy as jnp
from jax import lax

D = 768
H = 12
HD = 64
FF = 3072
ROT = 16
SEQ = 512
TOKENS = 24576


def raised(values, rng, source, target, parts, factor):
    owner, partner = [(jnp.arange(values.shape[axis_at]) // (values.shape[axis_at] // parts)).reshape([-1 if axis == axis_at else 1 for axis in range(values.ndim)]) for axis_at in (source, target)]
    chosen = jax.random.permutation(rng, parts)[partner]
    strong = (owner == chosen) | (owner == (partner + parts // 2) % parts)
    return jnp.where(strong, factor * values, values)


def block_scale(own_key, shape, cuts, smallest, largest):
    level, own = 1.0, jax.random.fold_in(own_key, 6)
    for axis_at, parts in cuts:
        draws = jnp.exp(jax.random.uniform(jax.random.fold_in(own, axis_at), (parts,), jnp.float32, smallest / len(cuts), largest / len(cuts)))
        level = level * jnp.repeat(draws, shape[axis_at] // parts).reshape([-1 if axis == axis_at else 1 for axis in range(len(shape))])
    return level


def bell_draw(key, shape, width, limit, pieces=(), kind=jnp.bfloat16):
    level = block_scale(key, shape, pieces, -0.22, 0.18) if pieces else 1.0
    array = jax.random.normal(key, shape, jnp.float32) * width * level
    return jnp.minimum(jnp.maximum(array, -limit), limit).astype(kind)


def gaussian_with(own_key, shape, scale, bound, shards, heavy, held_as=jnp.bfloat16):
    array = scale * jax.random.normal(own_key, shape, jnp.float32)
    if shards:
        array = array * block_scale(own_key, shape, shards, -0.22, 0.18)
    return jnp.clip(raised(array, jax.random.fold_in(own_key, 3), *heavy), -bound, bound).astype(held_as)


def setup_inputs(seed: int = 0) -> dict:
    arg_keys = jax.random.split(jax.random.key(seed), 15)
    block_input = bell_draw(arg_keys[0], (TOKENS, D), 1.0, 6.0, ((0, 8),))
    cotangent = gaussian_with(arg_keys[1], (TOKENS, D), 1.0, 6.0, ((0, 8),), (0, 1, 8, 2.0))
    heads_weight = bell_draw(arg_keys[2], (D, 3 * D), D ** -0.5, 0.21875, ((0, 8), (1, 4)))
    heads_bias = bell_draw(arg_keys[3], (3 * D,), 0.5, 3.0, ((0, 32),))
    merge_weight = bell_draw(arg_keys[4], (D, D), (D // 16) ** -0.5, 0.875, ((0, 4), (1, 8)))
    merge_bias = bell_draw(arg_keys[5], (D,), 0.5, 3.0, ((0, 8),))
    up_weight = bell_draw(arg_keys[6], (D, FF), D ** -0.5, 0.21875, ((0, 8), (1, 4)))
    up_bias = bell_draw(arg_keys[7], (FF,), 0.5, 3.0, ((0, 32),))
    down_weight = bell_draw(arg_keys[8], (FF, D), (FF // 2) ** -0.5, 0.15625, ((0, 4), (1, 8)))
    down_bias = bell_draw(arg_keys[9], (D,), 0.5, 3.0, ((0, 8),))
    first_gain = jnp.clip(1.0 + 0.18 * jax.random.normal(arg_keys[10], (D,), jnp.float32), 0.099609375, 1.8984375).astype(jnp.bfloat16)
    first_shift = bell_draw(arg_keys[11], (D,), 0.3, 2.0, ((0, 8),))
    second_gain = jnp.clip(1.0 + 0.18 * jax.random.normal(arg_keys[12], (D,), jnp.float32), 0.099609375, 1.8984375).astype(jnp.bfloat16)
    second_shift = bell_draw(arg_keys[13], (D,), 0.3, 2.0, ((0, 8),))
    return {"block_input": block_input, "cotangent": cotangent, "heads_weight": heads_weight, "heads_bias": heads_bias, "merge_weight": merge_weight, "merge_bias": merge_bias, "up_weight": up_weight, "up_bias": up_bias, "down_weight": down_weight, "down_bias": down_bias, "first_gain": first_gain, "first_shift": first_shift, "second_gain": second_gain, "second_shift": second_shift}


@jax.custom_vjp
def low(v):
    return lax.optimization_barrier(v.astype(jnp.bfloat16)).astype(jnp.float32)

@jax.custom_vjp
def low_back(v):
    return v

def low_keep(v):
    return (low(v), None)

def low_pass(kept, grad):
    return (grad,)

def back_keep(v):
    return (v, None)

def back_low(kept, grad):
    return (low(grad),)
low.defvjp(low_keep, low_pass)
low_back.defvjp(back_keep, back_low)

def layer_norm(values, scale, shift):
    average = lax.optimization_barrier(jnp.mean(values, axis=-1, keepdims=True))
    centred = values - average
    spread = lax.optimization_barrier(jnp.mean(centred * centred, axis=-1, keepdims=True))
    return centred * lax.rsqrt(spread + 1e-05) * scale + shift

def rotary_tables(length, dims):
    half = dims // 2
    position = jnp.arange(length).astype(jnp.float32)
    rates = 10000.0 ** (-(2.0 * jnp.arange(half).astype(jnp.float32)) / dims)
    angles = position[:, None] * rates[None, :]
    return (jnp.cos(angles), jnp.sin(angles))

def rotate(values, cosine, sine):
    half = cosine.shape[-1]
    cosine = cosine[None, :, None, :]
    sine = sine[None, :, None, :]
    first = values[..., :half]
    second = values[..., half:2 * half]
    return jnp.concatenate([first * cosine - second * sine, second * cosine + first * sine, values[..., 2 * half:]], axis=-1)

def forward(inputs, heads_weight, heads_bias, merge_weight, merge_bias, up_weight, up_bias, down_weight, down_bias, first_gain, first_shift, second_gain, second_shift):
    highest = lax.Precision.HIGHEST
    count = inputs.shape[0] // SEQ
    cosine, sine = rotary_tables(SEQ, ROT)
    first_normed = low(layer_norm(inputs, first_gain, first_shift))
    second_normed = low(layer_norm(inputs, second_gain, second_shift))
    mixed = jnp.dot(first_normed, heads_weight, precision=highest, preferred_element_type=jnp.float32) + heads_bias
    mixed = low_back(mixed).reshape(count, SEQ, H, 3, HD)
    query = low(rotate(mixed[:, :, :, 0], cosine, sine))
    keys = low(rotate(mixed[:, :, :, 1], cosine, sine))
    values = low(mixed[:, :, :, 2])
    raw = jnp.einsum('csha,ctha->chst', query, keys, precision=highest)
    scores = low_back(raw) * (1.0 / math.sqrt(HD))
    causal = jnp.arange(SEQ)[:, None] >= jnp.arange(SEQ)[None, :]
    scores = jnp.where(causal, scores, -1e+30)
    weights = low(jax.nn.softmax(scores, axis=-1))
    attended = jnp.einsum('chst,ctha->csha', weights, values, precision=highest).reshape(inputs.shape[0], D)
    attended = low(low_back(attended))
    hidden = low_back(jnp.dot(second_normed, up_weight, precision=highest, preferred_element_type=jnp.float32) + up_bias)
    activated = low(jax.nn.gelu(hidden, approximate=False))
    branches = jnp.dot(attended, merge_weight, precision=highest, preferred_element_type=jnp.float32)
    branches = branches + jnp.dot(activated, down_weight, precision=highest, preferred_element_type=jnp.float32)
    return inputs + branches + merge_bias + down_bias

def reference(block_input, cotangent, heads_weight, heads_bias, merge_weight, merge_bias, up_weight, up_bias, down_weight, down_bias, first_gain, first_shift, second_gain, second_shift):
    params = tuple((item.astype(jnp.float32) for item in (heads_weight, heads_bias, merge_weight, merge_bias, up_weight, up_bias, down_weight, down_bias, first_gain, first_shift, second_gain, second_shift)))
    total_seqs = block_input.shape[0] // SEQ
    per_group = 1
    for option in range(1, total_seqs + 1):
        if total_seqs % option == 0 and option * SEQ <= max(4096, SEQ):
            per_group = option
    group_rows = per_group * SEQ
    blocks = block_input.reshape(total_seqs // per_group, group_rows, D)
    grad_blocks = cotangent.reshape(total_seqs // per_group, group_rows, D)

    def visit(running, pair):
        block, block_grad = pair
        result, pullback = jax.vjp(forward, block.astype(jnp.float32), *params)
        fresh = pullback(block_grad.astype(jnp.float32))
        running = tuple((old + new for old, new in zip(running, fresh[1:])))
        return (running, (result.astype(jnp.bfloat16), fresh[0]))
    start = tuple((jnp.zeros(item.shape, jnp.float32) for item in params))
    totals, (outputs, input_grads) = lax.scan(visit, start, (blocks, grad_blocks))
    layer_output = outputs.reshape(block_input.shape[0], D)
    input_grad = input_grads.reshape(block_input.shape[0], D)
    return (layer_output, input_grad, totals[0], totals[1], totals[2], totals[3], totals[4], totals[5], totals[6], totals[7], totals[8], totals[9], totals[10], totals[11])
```

```python
import math

import jax
import jax.numpy as jnp
import numpy as np
from jax import lax
from jax.experimental import pallas as pl
from jax.experimental.pallas import tpu as pltpu
from jax.sharding import PartitionSpec as P

HD = 64
ROT = 16
SEQ = 512
EPS = 1e-05
VMEM = 56 * 1024 * 1024
F32 = jnp.float32
BF16 = jnp.bfloat16


def dot(left, right, left_dim, right_dim):
    return lax.dot_general(
        left, right, (((left_dim,), (right_dim,)), ((), ())), preferred_element_type=F32
    )


def normalise(values):
    average = jnp.mean(values, axis=-1, keepdims=True)
    centred = values - average
    spread = jnp.mean(centred * centred, axis=-1, keepdims=True)
    scale = lax.rsqrt(spread + EPS)
    return centred * scale, scale


def norm_back(d, hat, scale, gain):
    dg = d * gain
    first = jnp.mean(dg, axis=-1, keepdims=True)
    second = jnp.mean(dg * hat, axis=-1, keepdims=True)
    return (dg - first - hat * second) * scale


def rotary_tables():
    half = ROT // 2
    rates = 10000.0 ** (-(2.0 * np.arange(half)) / ROT)
    angles = rates[:, None] * np.arange(SEQ)[None, :]
    return np.cos(angles).astype(np.float32), np.sin(angles).astype(np.float32)


def rotate(values, cosine, sine):
    half = ROT // 2
    first, second = values[:half], values[half:ROT]
    return jnp.concatenate(
        [first * cosine - second * sine, second * cosine + first * sine, values[ROT:]], axis=0
    )


def attention_kernel(
    place, x_ref, g_ref, wt_ref, merge_ref, bias_ref, ln_ref, cos_ref, sin_ref,
    out_ref, din_ref, n1t_ref, gt_ref, dmh_ref, atth_ref, rows_ref, hb_ref,
    mixed, datt, att, dmix,
):
    groups = wt_ref.shape[0] // (9 * HD)
    rows = 9 * HD
    half = SEQ // 2
    scaling = 1.0 / math.sqrt(HD)
    x = x_ref[...].astype(F32)
    g = g_ref[...]
    gain, shift = ln_ref[0:1, :], ln_ref[1:2, :]
    hat, scale = normalise(x)
    n1 = (hat * gain + shift).astype(BF16)
    n1t_ref[0] = n1.T
    gt_ref[0] = g.T
    datt[...] = dot(merge_ref[...], g, 1, 1).astype(BF16)
    cosine, sine = cos_ref[...], sin_ref[...]
    below = lax.broadcasted_iota(jnp.int32, (half, half), 0) <= lax.broadcasted_iota(
        jnp.int32, (half, half), 1
    )

    def softmax(scores):
        top = jnp.max(scores, axis=0, keepdims=True)
        raised = jnp.exp(scores - top)
        return raised * (1.0 / jnp.sum(raised, axis=0, keepdims=True))

    def group(index, carry):
        base = pl.multiple_of(index * rows, rows)
        part = dot(wt_ref[pl.ds(base, rows), :], n1, 1, 1)
        bias = bias_ref[pl.ds(base, rows), :]
        part = part + jnp.concatenate([bias] * (SEQ // 128), axis=1)
        for head in range(3):
            at = head * 3 * HD
            query = rotate(part[at : at + HD], cosine, sine).astype(BF16)
            keys = rotate(part[at + HD : at + 2 * HD], cosine, sine).astype(BF16)
            values = part[at + 2 * HD : at + 3 * HD].astype(BF16)
            spot = pl.multiple_of(index * 3 * HD + head * HD, HD)
            given = datt[pl.ds(spot, HD), :]
            keys_t, values_t = keys.T, values.T
            s0 = dot(keys_t[:half], query[:, :half], 1, 0) * scaling
            s1a = dot(keys_t[:half], query[:, half:], 1, 0) * scaling
            s1b = dot(keys_t[half:], query[:, half:], 1, 0) * scaling
            s0 = jnp.where(below, s0, -1e30)
            s1b = jnp.where(below, s1b, -1e30)
            p0 = softmax(s0)
            p1 = softmax(jnp.concatenate([s1a, s1b], axis=0))
            w0, w1 = p0.astype(BF16), p1.astype(BF16)
            attended = jnp.concatenate(
                [dot(values[:, :half], w0, 1, 0), dot(values, w1, 1, 0)], axis=1
            )
            att[pl.ds(spot, HD), :] = attended.astype(BF16)
            q0 = dot(values_t[:half], given[:, :half], 1, 0)
            q1 = dot(values_t, given[:, half:], 1, 0)
            d0 = (p0 * (q0 - jnp.sum(q0 * p0, axis=0, keepdims=True)) * scaling).astype(BF16)
            d1 = (p1 * (q1 - jnp.sum(q1 * p1, axis=0, keepdims=True)) * scaling).astype(BF16)
            d_values = dot(given[:, half:], w1, 1, 1)
            d_values = jnp.concatenate(
                [d_values[:, :half] + dot(given[:, :half], w0, 1, 1), d_values[:, half:]], axis=1
            )
            d_keys = dot(query[:, half:], d1, 1, 1)
            d_keys = jnp.concatenate(
                [d_keys[:, :half] + dot(query[:, :half], d0, 1, 1), d_keys[:, half:]], axis=1
            )
            d_query = jnp.concatenate(
                [dot(keys[:, :half], d0, 1, 0), dot(keys, d1, 1, 0)], axis=1
            )
            to = pl.multiple_of(base + at, HD)
            dmix[pl.ds(to, HD), :] = rotate(d_query, cosine, -sine).astype(BF16)
            dmix[pl.ds(to + HD, HD), :] = rotate(d_keys, cosine, -sine).astype(BF16)
            dmix[pl.ds(to + 2 * HD, HD), :] = d_values.astype(BF16)
        return carry

    lax.fori_loop(0, groups, group, 0)
    out_ref[...] = dot(att[...].T, merge_ref[...], 1, 0)
    d_first = dot(dmix[...].T, wt_ref[...], 1, 0)
    pair = place[1]
    mine = dmix[pl.ds(pl.multiple_of(pair * 2 * rows, 2 * rows), 2 * rows), :]
    dmh_ref[0] = mine
    atth_ref[0] = att[pl.ds(pl.multiple_of(pair * 6 * HD, 6 * HD), 6 * HD), :]
    hb_ref[0] = dot(jnp.ones((8, SEQ), BF16), mine, 1, 1)
    rows_ref[0] = jnp.concatenate(
        [
            jnp.sum(d_first * hat, axis=0, keepdims=True),
            jnp.sum(d_first, axis=0, keepdims=True),
            jnp.sum(g.astype(F32), axis=0, keepdims=True),
            jnp.zeros((5, x.shape[1]), F32),
        ],
        axis=0,
    )
    din_ref[...] = norm_back(d_first, hat, scale, gain)


def gelu_parts(h):
    near = 0.7071067811865476 * jnp.abs(h)
    below = 1.0 + 0.3275911 * near
    t = pl.reciprocal(below, approx=True)
    t = t * (2.0 - below * t)
    bell = jnp.exp(-0.5 * h * h)
    series = 1.061405429 * t - 1.453152027
    series = series * t + 1.421413741
    series = series * t - 0.284496736
    series = series * t + 0.254829592
    tail = 0.5 * series * t * bell
    phi = jnp.where(h >= 0, 1.0 - tail, tail)
    return h * phi, phi + h * bell * 0.3989422804014327


def feed_kernel(
    place, x_ref, g_ref, up_ref, down_ref, bias_ref, ln_ref, aout_ref, din_ref,
    out_ref, t_ref, n2t_ref, act_ref, dh_ref, rows_ref,
    n2, hat_s, scale_s, acc, dacc, sums,
):
    step = pl.program_id(1)
    pair = place[1]
    gain, shift = ln_ref[2:3, :], ln_ref[3:4, :]

    @pl.when(step == 0)
    def _():
        hat, scale = normalise(x_ref[...].astype(F32))
        hat_s[...] = hat
        scale_s[...] = jnp.broadcast_to(scale, scale_s.shape)
        n2[...] = (hat * gain + shift).astype(BF16)
        n2t_ref[0] = n2[...].T
        sums[...] = jnp.zeros_like(sums)
        acc[...] = x_ref[...].astype(F32) + aout_ref[...] + ln_ref[4:5, :]
        dacc[...] = jnp.zeros_like(dacc)

    up, down = up_ref[0], down_ref[0]
    h = dot(n2[...], up, 1, 0) + bias_ref[0, 0:1, :]
    activated, slope = gelu_parts(h)
    activated = activated.astype(BF16)
    d_hidden = (dot(g_ref[...], down, 1, 0) * slope).astype(BF16)
    acc[...] += dot(activated, down, 1, 1)
    dacc[...] += dot(d_hidden, up, 1, 1)

    @pl.when(step // 2 == pair)
    def _():
        act_ref[0] = activated
        dh_ref[0] = d_hidden
        sums[pl.ds(step % 2, 1), :] = jnp.sum(d_hidden.astype(F32), axis=0, keepdims=True)

    @pl.when(step == pl.num_programs(1) - 1)
    def _():
        d_second = dacc[...]
        hat = hat_s[...]
        out_ref[...] = acc[...].astype(BF16)
        total = norm_back(d_second, hat, scale_s[:, 0:1], gain) + din_ref[...]
        t_ref[...] = total.astype(BF16)
        rows_ref[0] = jnp.concatenate(
            [
                jnp.sum(d_second * hat, axis=0, keepdims=True),
                jnp.sum(d_second, axis=0, keepdims=True),
                sums[0:2, :],
                jnp.zeros((4, hat.shape[1]), F32),
            ],
            axis=0,
        )


def heads_grad_kernel(n1t_ref, gt_ref, dmh_ref, atth_ref, out_ref, acc):
    step = pl.program_id(0)
    width = dmh_ref.shape[1]

    @pl.when(step == 0)
    def _():
        acc[...] = jnp.zeros_like(acc)

    acc[:, :width] += dot(n1t_ref[0], dmh_ref[0], 1, 1)
    acc[:, width:] += dot(gt_ref[0], atth_ref[0], 1, 1)

    @pl.when(step == pl.num_programs(0) - 1)
    def _():
        out_ref[...] = acc[...].astype(BF16)


def feed_grad_kernel(n2t_ref, gt_ref, dh_ref, act_ref, small_ref, out_ref, acc):
    step = pl.program_id(0)
    width = dh_ref.shape[2]

    @pl.when(step == 0)
    def _():
        acc[...] = jnp.zeros_like(acc)

    acc[:, :width] += dot(n2t_ref[0], dh_ref[0], 1, 0)
    acc[:, width:] += dot(gt_ref[0], act_ref[0], 1, 0)

    @pl.when(step == pl.num_programs(0) - 1)
    def _():
        out_ref[:, : 2 * width] = acc[...].astype(BF16)
        out_ref[:, 2 * width :] = small_ref[...].astype(BF16)


def params(*kinds):
    return pltpu.CompilerParams(dimension_semantics=kinds, vmem_limit_bytes=VMEM)


def whole(shape):
    zeros = (0,) * len(shape)
    return pl.BlockSpec(shape, lambda *_: zeros)


def attention(place, x, g, wt, merge, bias, ln, cosine, sine, count):
    width = x.shape[1]
    rows = 9 * HD
    given = pl.BlockSpec((SEQ, width), lambda i, place: (place[0] + i, 0))
    taken = pl.BlockSpec((SEQ, width), lambda i, place: (i, 0))

    def per(a, b):
        return pl.BlockSpec((1, a, b), lambda i, place: (i, 0, 0))

    return pl.pallas_call(
        attention_kernel,
        grid_spec=pltpu.PrefetchScalarGridSpec(
            num_scalar_prefetch=1,
            grid=(count,),
            in_specs=[
                given, given, whole(wt.shape), whole(merge.shape), whole(bias.shape),
                whole(ln.shape), whole(cosine.shape), whole(sine.shape),
            ],
            out_specs=[
                taken, taken, per(width, SEQ), per(width, SEQ), per(2 * rows, SEQ),
                per(6 * HD, SEQ), per(8, width), per(8, 2 * rows),
            ],
            scratch_shapes=[
                pltpu.VMEM((8, 128), BF16),
                pltpu.VMEM((width, SEQ), BF16),
                pltpu.VMEM((width, SEQ), BF16),
                pltpu.VMEM((wt.shape[0], SEQ), BF16),
            ],
        ),
        out_shape=[
            jax.ShapeDtypeStruct((count * SEQ, width), F32),
            jax.ShapeDtypeStruct((count * SEQ, width), F32),
            jax.ShapeDtypeStruct((count, width, SEQ), BF16),
            jax.ShapeDtypeStruct((count, width, SEQ), BF16),
            jax.ShapeDtypeStruct((count, 2 * rows, SEQ), BF16),
            jax.ShapeDtypeStruct((count, 6 * HD, SEQ), BF16),
            jax.ShapeDtypeStruct((count, 8, width), F32),
            jax.ShapeDtypeStruct((count, 8, 2 * rows), F32),
        ],
        compiler_params=params("arbitrary"),
        name="attention",
        cost_estimate=pl.CostEstimate(
            flops=count * 20_000_000_000, bytes_accessed=count * 12_000_000, transcendentals=0
        ),
    )(place, x, g, wt, merge, bias, ln, cosine, sine)


def feed(place, x, g, up, down, bias, ln, aout, din, count):
    width = x.shape[1]
    groups, _, ff = up.shape
    given = pl.BlockSpec((SEQ, width), lambda i, t, place: (place[0] + i, 0))
    taken = pl.BlockSpec((SEQ, width), lambda i, t, place: (i, 0))
    weight = pl.BlockSpec((1, width, ff), lambda i, t, place: (t, 0, 0))
    kept = pl.BlockSpec(
        (1, SEQ, ff), lambda i, t, place: (i, 0, jnp.clip(t - 2 * place[1], 0, 1))
    )
    return pl.pallas_call(
        feed_kernel,
        grid_spec=pltpu.PrefetchScalarGridSpec(
            num_scalar_prefetch=1,
            grid=(count, groups),
            in_specs=[
                given, given, weight, weight,
                pl.BlockSpec((1, 1, ff), lambda i, t, place: (t, 0, 0)),
                whole(ln.shape), taken, taken,
            ],
            out_specs=[
                taken, taken,
                pl.BlockSpec((1, width, SEQ), lambda i, t, place: (i, 0, 0)),
                kept, kept,
                pl.BlockSpec((1, 8, width), lambda i, t, place: (i, 0, 0)),
            ],
            scratch_shapes=[
                pltpu.VMEM((SEQ, width), BF16),
                pltpu.VMEM((SEQ, width), F32),
                pltpu.VMEM((SEQ, 128), F32),
                pltpu.VMEM((SEQ, width), F32),
                pltpu.VMEM((SEQ, width), F32),
                pltpu.VMEM((8, ff), F32),
            ],
        ),
        out_shape=[
            jax.ShapeDtypeStruct((count * SEQ, width), BF16),
            jax.ShapeDtypeStruct((count * SEQ, width), BF16),
            jax.ShapeDtypeStruct((count, width, SEQ), BF16),
            jax.ShapeDtypeStruct((count, SEQ, 2 * ff), BF16),
            jax.ShapeDtypeStruct((count, SEQ, 2 * ff), BF16),
            jax.ShapeDtypeStruct((count, 8, width), F32),
        ],
        compiler_params=params("arbitrary", "arbitrary"),
        name="feed",
        cost_estimate=pl.CostEstimate(
            flops=count * 15_000_000_000, bytes_accessed=count * 18_000_000, transcendentals=0
        ),
    )(place, x, g, up, down, bias, ln, aout, din)


def heads_grad(n1t, gt, dmh, atth):
    count, width, _ = n1t.shape
    columns = dmh.shape[1] + atth.shape[1]

    def per(array):
        return pl.BlockSpec((1,) + array.shape[1:], lambda i: (i, 0, 0))

    return pl.pallas_call(
        heads_grad_kernel,
        grid=(count,),
        in_specs=[per(n1t), per(gt), per(dmh), per(atth)],
        out_specs=whole((width, columns)),
        out_shape=jax.ShapeDtypeStruct((width, columns), BF16),
        scratch_shapes=[pltpu.VMEM((width, columns), F32)],
        compiler_params=params("arbitrary"),
        name="heads_grad",
        cost_estimate=pl.CostEstimate(
            flops=2 * count * SEQ * width * columns, bytes_accessed=8_000_000, transcendentals=0
        ),
    )(n1t, gt, dmh, atth)


def feed_grad(n2t, gt, dh, act, small):
    count, width, _ = n2t.shape
    columns = 2 * dh.shape[2]

    def per(array):
        return pl.BlockSpec((1,) + array.shape[1:], lambda i: (i, 0, 0))

    return pl.pallas_call(
        feed_grad_kernel,
        grid=(count,),
        in_specs=[per(n2t), per(gt), per(dh), per(act), whole(small.shape)],
        out_specs=whole((width, columns + small.shape[1])),
        out_shape=jax.ShapeDtypeStruct((width, columns + small.shape[1]), BF16),
        scratch_shapes=[pltpu.VMEM((width, columns), F32)],
        compiler_params=params("arbitrary"),
        name="feed_grad",
        cost_estimate=pl.CostEstimate(
            flops=2 * count * SEQ * width * columns, bytes_accessed=18_000_000, transcendentals=0
        ),
    )(n2t, gt, dh, act, small)


def body(
    block_input, cotangent, heads_weight, heads_bias, merge_weight, merge_bias, up_weight, up_bias,
    down_weight, down_bias, first_gain, first_shift, second_gain, second_shift,
):
    chunk = heads_weight.shape[0]
    owners = lax.axis_size("dp")
    groups = lax.axis_size("tensor")
    width = block_input.shape[1]
    spot = lax.axis_index("tensor")
    odd, pair = spot % 2, spot // 2
    total = block_input.shape[0] // SEQ
    count = total // 2
    place = jnp.stack([odd * count, pair]).astype(jnp.int32)

    bias_part = heads_bias.shape[0]
    vectors = jnp.stack(
        [
            jnp.pad(heads_bias, (0, chunk - bias_part)), up_bias, merge_bias, down_bias,
            first_gain, first_shift, second_gain, second_shift,
        ],
        axis=1,
    )
    early = jnp.concatenate(
        [heads_weight, merge_weight.T, jnp.pad(vectors, ((0, 0), (0, 120)))], axis=1
    )
    late = jnp.concatenate([up_weight, down_weight.T], axis=1)
    early = lax.all_gather(lax.all_gather(early, "dp", axis=0, tiled=True), "tensor", axis=0)
    late = lax.all_gather(lax.all_gather(late, "dp", axis=0, tiled=True), "tensor", axis=0)
    rows = 9 * HD
    wt = early[:, :, :rows].transpose(0, 2, 1).reshape(groups * rows, width)
    merge = early[:, :, rows : rows + 3 * HD].transpose(0, 2, 1).reshape(groups * 3 * HD, width)
    vecs = early[:, :, rows + 3 * HD : rows + 3 * HD + 8].astype(F32).transpose(0, 2, 1)
    hbias = vecs[:, 0].reshape(groups, owners, chunk)[:, :, :bias_part].reshape(groups * rows, 1)
    hbias = jnp.broadcast_to(hbias, (groups * rows, 128))
    ubias = vecs[:, 1:2, :]
    ln = jnp.concatenate(
        [vecs[0, 4:8], (vecs[0, 2] + vecs[0, 3])[None], jnp.zeros((3, width), F32)], axis=0
    )
    ff = up_weight.shape[1]
    up, down = late[:, :, :ff], late[:, :, ff:]

    cosine, sine = rotary_tables()
    aout, din, n1t, gt, dmh, atth, rows_a, hb = attention(
        place, block_input, cotangent, wt, merge, hbias, ln, cosine, sine, count
    )
    out16, t16, n2t, act, dh, rows_f = feed(
        place, block_input, cotangent, up, down, ubias, ln, aout, din, count
    )
    swap = [(i, i ^ 1) for i in range(groups)]
    out_other = lax.ppermute(out16, "tensor", swap)
    t_other = lax.ppermute(t16, "tensor", swap)

    first_cols = heads_grad(n1t, gt, dmh, atth)
    rows_a, rows_f, hb = rows_a.sum(0), rows_f.sum(0), hb.sum(0)[0]
    hb = jnp.pad(hb.reshape(2, owners, bias_part), ((0, 0), (0, 0), (0, chunk - bias_part)))
    small = jnp.concatenate(
        [rows_a[0:2], rows_f[0:2], rows_a[2:3], rows_f[2:4], hb.reshape(2, width)], axis=0
    )
    small = jnp.pad(small.T, ((0, 0), (0, 128 - 9)))
    second_cols = feed_grad(n2t, gt, dh, act, small)

    first_cols = lax.psum_scatter(first_cols, "dp", scatter_dimension=0, tiled=True)
    second_cols = lax.psum_scatter(second_cols, "dp", scatter_dimension=0, tiled=True)
    hw = first_cols[:, : 2 * rows].reshape(chunk, 2, rows)
    mw = first_cols[:, 2 * rows :].reshape(chunk, 2, 3 * HD)
    uw = second_cols[:, : 2 * ff].reshape(chunk, 2, ff)
    dw = second_cols[:, 2 * ff : 4 * ff].reshape(chunk, 2, ff)
    tiny = second_cols[:, 4 * ff :]
    halves = [
        jnp.concatenate(
            [hw[:, k], mw[:, k], uw[:, k], dw[:, k], tiny[:, 0:5], tiny[:, 5 + k : 6 + k], tiny[:, 7 + k : 8 + k]],
            axis=1,
        )
        for k in range(2)
    ]
    mine = jnp.where(odd == 0, halves[0], halves[1])
    other = jnp.where(odd == 0, halves[1], halves[0])
    full = mine.astype(F32) + lax.ppermute(other, "tensor", swap).astype(F32)
    a, b, c, d = rows, rows + 3 * HD, rows + 3 * HD + ff, rows + 3 * HD + 2 * ff

    layer_output = jnp.where(
        odd == 0,
        jnp.concatenate([out16, out_other], axis=0),
        jnp.concatenate([out_other, out16], axis=0),
    )
    terms = jnp.where(
        odd == 0,
        jnp.concatenate([t16, t_other], axis=0),
        jnp.concatenate([t_other, t16], axis=0),
    )
    input_grad = terms.astype(F32) + cotangent.astype(F32)
    return (
        layer_output,
        input_grad,
        full[:, :a],
        full[:bias_part, d + 6],
        full[:, a:b].T,
        full[:, d + 4],
        full[:, b:c],
        full[:, d + 5],
        full[:, c:d].T,
        full[:, d + 4],
        full[:, d],
        full[:, d + 1],
        full[:, d + 2],
        full[:, d + 3],
    )


def solution(mesh):
    placed = (
        P("dp", None),
        P("dp", None),
        P("dp", "tensor"),
        P(("tensor", "dp")),
        P("tensor", "dp"),
        P("dp"),
        P("dp", "tensor"),
        P(("tensor", "dp")),
        P("tensor", "dp"),
        P("dp"),
        P("dp"),
        P("dp"),
        P("dp"),
        P("dp"),
    )
    return jax.shard_map(
        body,
        mesh=mesh,
        in_specs=placed,
        out_specs=placed,
        check_vma=False,
    )
```

```python
import functools
import math

import jax
import jax.numpy as jnp
import numpy as np
from jax import lax
from jax.experimental import pallas as pl
from jax.experimental.pallas import tpu as pltpu
from jax.sharding import PartitionSpec as P

HD = 64
ROT = 16
SEQ = 512
EPS = 1e-05
VMEM = 56 * 1024 * 1024
F32 = jnp.float32
BF16 = jnp.bfloat16


def dot(left, right, left_dim, right_dim):
    return lax.dot_general(
        left, right, (((left_dim,), (right_dim,)), ((), ())), preferred_element_type=F32
    )


def normalise(values):
    average = jnp.mean(values, axis=-1, keepdims=True)
    centred = values - average
    spread = jnp.mean(centred * centred, axis=-1, keepdims=True)
    scale = lax.rsqrt(spread + EPS)
    return centred * scale, scale


def norm_back(d, hat, scale, gain):
    dg = d * gain
    first = jnp.mean(dg, axis=-1, keepdims=True)
    second = jnp.mean(dg * hat, axis=-1, keepdims=True)
    return (dg - first - hat * second) * scale


def rotary_tables():
    half = ROT // 2
    rates = 10000.0 ** (-(2.0 * np.arange(half)) / ROT)
    angles = rates[:, None] * np.arange(SEQ)[None, :]
    return np.cos(angles).astype(np.float32), np.sin(angles).astype(np.float32)


def rotate(values, cosine, sine):
    half = ROT // 2
    first, second = values[:half], values[half:ROT]
    return jnp.concatenate(
        [first * cosine - second * sine, second * cosine + first * sine, values[ROT:]], axis=0
    )


def piece_rows(place, index, pieces, chunk):
    if pieces == 1:
        return pl.ds(0, chunk)
    across, core = index // 2, index % 2
    owner = (across ^ place[3]) * 2 + (core ^ place[4])
    return pl.ds(pl.multiple_of(owner * chunk, 16), chunk)


def assemble(place, refs, target):
    chunk = refs[0].shape[1]
    for index, ref in enumerate(refs):
        target[piece_rows(place, index, len(refs), chunk), :] = ref[0]


def prepare_kernel(place, *refs):
    *pieces, wt_ref, merge_ref, vec_ref, full = refs
    assemble(place, pieces, full)
    rows = wt_ref.shape[0]
    end = rows + merge_ref.shape[0]
    wt_ref[...] = full[:, :rows].T
    merge_ref[...] = full[:, rows:end].T
    vec_ref[0] = full[:, end:].astype(F32).T[: vec_ref.shape[1]]


def attention_kernel(
    place, x_ref, g_ref, wt_ref, merge_ref, bias_ref, ln_ref, cos_ref, sin_ref,
    out_ref, din_ref, gt_ref, grad_ref, rows_ref, hb_ref,
    datt, att, dmix, acc,
):
    groups = wt_ref.shape[0] // (9 * HD)
    rows = 9 * HD
    half = SEQ // 2
    scaling = 1.0 / math.sqrt(HD)
    x = x_ref[...].astype(F32)
    g = g_ref[...]
    gain, shift = ln_ref[0:1, :], ln_ref[1:2, :]
    hat, scale = normalise(x)
    n1 = (hat * gain + shift).astype(BF16)
    datt[...] = dot(merge_ref[...], g, 1, 1).astype(BF16)
    cosine, sine = cos_ref[...], sin_ref[...]
    below = lax.broadcasted_iota(jnp.int32, (half, half), 0) <= lax.broadcasted_iota(
        jnp.int32, (half, half), 1
    )

    def raise_columns(scores):
        raised = jnp.exp(scores - jnp.max(scores, axis=0, keepdims=True))
        return raised, jnp.sum(raised, axis=0, keepdims=True)

    def group(index, carry):
        base = pl.multiple_of(index * rows, rows)
        part = dot(wt_ref[pl.ds(base, rows), :], n1, 1, 1)
        part = part + bias_ref[index].T[:, 0:1]
        for head in range(3):
            at = head * 3 * HD
            query = (rotate(part[at : at + HD], cosine, sine) * scaling).astype(BF16)
            keys = rotate(part[at + HD : at + 2 * HD], cosine, sine).astype(BF16)
            values = part[at + 2 * HD : at + 3 * HD].astype(BF16)
            spot = pl.multiple_of(index * 3 * HD + head * HD, HD)
            given = datt[pl.ds(spot, HD), :].astype(F32)
            keys_t, values_t = keys.T, values.T
            s0 = dot(keys_t[:half], query[:, :half], 1, 0)
            s1a = dot(keys_t[:half], query[:, half:], 1, 0)
            s1b = dot(keys_t[half:], query[:, half:], 1, 0)
            e0, l0 = raise_columns(jnp.where(below, s0, -1e30))
            e1, l1 = raise_columns(
                jnp.concatenate([s1a, jnp.where(below, s1b, -1e30)], axis=0)
            )
            w0, w1 = e0.astype(BF16), e1.astype(BF16)
            share = 1.0 / jnp.concatenate([l0, l1], axis=1)
            attended = share * jnp.concatenate(
                [dot(values[:, :half], w0, 1, 0), dot(values, w1, 1, 0)], axis=1
            )
            att[pl.ds(spot, HD), :] = attended.astype(BF16)
            given = (given * share).astype(BF16)
            level = jnp.sum(given.astype(F32) * attended, axis=0, keepdims=True)
            q0 = dot(values_t[:half], given[:, :half], 1, 0)
            q1 = dot(values_t, given[:, half:], 1, 0)
            d0 = (e0 * (q0 - level[:, :half])).astype(BF16)
            d1 = (e1 * (q1 - level[:, half:])).astype(BF16)
            d_values = dot(given[:, half:], w1, 1, 1)
            d_values = jnp.concatenate(
                [d_values[:, :half] + dot(given[:, :half], w0, 1, 1), d_values[:, half:]], axis=1
            )
            d_keys = dot(query[:, half:], d1, 1, 1)
            d_keys = jnp.concatenate(
                [d_keys[:, :half] + dot(query[:, :half], d0, 1, 1), d_keys[:, half:]], axis=1
            )
            d_query = jnp.concatenate(
                [dot(keys[:, :half], d0, 1, 0), dot(keys, d1, 1, 0)], axis=1
            ) * scaling
            to = pl.multiple_of(base + at, HD)
            dmix[pl.ds(to, HD), :] = rotate(d_query, cosine, -sine).astype(BF16)
            dmix[pl.ds(to + HD, HD), :] = rotate(d_keys, cosine, -sine).astype(BF16)
            dmix[pl.ds(to + 2 * HD, HD), :] = d_values.astype(BF16)
        return carry

    lax.fori_loop(0, groups, group, 0)
    out_ref[...] = dot(att[...].T, merge_ref[...], 1, 0).astype(BF16)
    d_first = dot(dmix[...].T, wt_ref[...], 1, 0)
    pair = place[1]
    mine = dmix[pl.ds(pl.multiple_of(pair * 2 * rows, 2 * rows), 2 * rows), :]
    mine_att = att[pl.ds(pl.multiple_of(pair * 6 * HD, 6 * HD), 6 * HD), :]
    hb_ref[0] = dot(jnp.ones((8, SEQ), BF16), mine, 1, 1)
    gt = g.T
    gt_ref[0] = gt
    step = pl.program_id(0)

    @pl.when(step == 0)
    def _():
        acc[...] = jnp.zeros_like(acc)

    acc[:, : 2 * rows] += dot(n1.T, mine, 1, 1)
    acc[:, 2 * rows :] += dot(gt, mine_att, 1, 1)

    @pl.when(step == pl.num_programs(0) - 1)
    def _():
        grad_ref[...] = acc[...].astype(BF16)

    rows_ref[0] = jnp.concatenate(
        [
            jnp.sum(d_first * hat, axis=0, keepdims=True),
            jnp.sum(d_first, axis=0, keepdims=True),
            jnp.sum(g.astype(F32), axis=0, keepdims=True),
            jnp.zeros((5, x.shape[1]), F32),
        ],
        axis=0,
    )
    din_ref[...] = norm_back(d_first, hat, scale, gain).astype(BF16)


def gelu_parts(h):
    near = 0.7071067811865476 * jnp.abs(h)
    below = 1.0 + 0.3275911 * near
    t = pl.reciprocal(below, approx=True)
    t = t * (2.0 - below * t)
    bell = jnp.exp(-0.5 * h * h)
    series = 1.061405429 * t - 1.453152027
    series = series * t + 1.421413741
    series = series * t - 0.284496736
    series = series * t + 0.254829592
    tail = 0.5 * series * t * bell
    phi = jnp.where(h >= 0, 1.0 - tail, tail)
    return h * phi, phi + h * bell * 0.3989422804014327


def feed_kernel(
    place, x_ref, g_ref, gt_ref, bias_ref, ln_ref, aout_ref, din_ref, *refs, pieces, earlier,
):
    weights, refs = refs[:pieces], refs[pieces:]
    sides = min(pieces, 2)
    held, refs = refs[: sides * earlier], refs[(sides + 2) * earlier :]
    out_ref, grad_ref, send_ref, rows_ref = refs[:4]
    made = refs[4 : 4 + sides]
    n2, n2t, hat_s, scale_s, acc, dacc, sums, full, fresh = refs[4 + sides :]
    ff = full.shape[1] // 2
    step = pl.program_id(1)
    pair = place[1]
    gain, shift = ln_ref[2:3, :], ln_ref[3:4, :]

    @pl.when(step == 0)
    def _():
        hat, scale = normalise(x_ref[...].astype(F32))
        hat_s[...] = hat
        scale_s[...] = jnp.broadcast_to(scale, scale_s.shape)
        n2[...] = (hat * gain + shift).astype(BF16)
        n2t[...] = n2[...].T
        sums[...] = jnp.zeros_like(sums)
        acc[...] = x_ref[...].astype(F32) + aout_ref[...].astype(F32) + ln_ref[4:5, :]
        dacc[...] = jnp.zeros_like(dacc)

    assemble(place, weights, full)
    up, down = full[:, :ff], full[:, ff:]
    h = dot(n2[...], up, 1, 0) + bias_ref[0, 0:1, :]
    activated, slope = gelu_parts(h)
    activated = activated.astype(BF16)
    d_hidden = (dot(g_ref[...], down, 1, 0) * slope).astype(BF16)
    acc[...] += dot(activated, down, 1, 1)
    dacc[...] += dot(d_hidden, up, 1, 1)

    @pl.when(step // 2 == pair)
    def _():
        fresh[:, :ff] = dot(n2t[...], d_hidden, 1, 0)
        fresh[:, ff:] = dot(gt_ref[0], activated, 1, 0)
        chunk = made[0].shape[1]
        for index in range(pieces):
            value = fresh[piece_rows(place, index, pieces, chunk), :]
            spot = index // 2
            if earlier:
                value = value + held[index % 2][spot].astype(F32)
            made[index % 2][spot] = value.astype(BF16)
        sums[pl.ds(step % 2, 1), :] = jnp.sum(d_hidden.astype(F32), axis=0, keepdims=True)

    @pl.when(step == pl.num_programs(1) - 1)
    def _():
        d_second = dacc[...]
        hat = hat_s[...]
        finished = acc[...].astype(BF16)
        out_ref[...] = finished
        send_ref[0] = finished
        total = norm_back(d_second, hat, scale_s[:, 0:1], gain) + din_ref[...].astype(F32)
        total = total.astype(BF16)
        send_ref[1] = total
        grad_ref[...] = total.astype(F32) + g_ref[...].astype(F32)
        rows_ref[...] = jnp.concatenate(
            [
                jnp.sum(d_second * hat, axis=0, keepdims=True),
                jnp.sum(d_second, axis=0, keepdims=True),
                sums[0:2, :],
                jnp.zeros((4, hat.shape[1]), F32),
            ],
            axis=0,
        )


def heads_grad_kernel(n1t_ref, gt_ref, dmh_ref, atth_ref, out_ref, acc):
    step = pl.program_id(0)
    width = dmh_ref.shape[1]

    @pl.when(step == 0)
    def _():
        acc[...] = jnp.zeros_like(acc)

    acc[:, :width] += dot(n1t_ref[0], dmh_ref[0], 1, 1)
    acc[:, width:] += dot(gt_ref[0], atth_ref[0], 1, 1)

    @pl.when(step == pl.num_programs(0) - 1)
    def _():
        out_ref[...] = acc[...].astype(BF16)


def params(*kinds):
    return pltpu.CompilerParams(dimension_semantics=kinds, vmem_limit_bytes=VMEM)


def whole(shape):
    zeros = (0,) * len(shape)
    return pl.BlockSpec(shape, lambda *_: zeros)


def attention(place, x, g, wt, merge, bias, ln, cosine, sine, count):
    width = x.shape[1]
    rows = 9 * HD
    columns = 2 * rows + 6 * HD
    given = pl.BlockSpec((SEQ, width), lambda i, place: (place[0] + i, 0))
    taken = pl.BlockSpec((SEQ, width), lambda i, place: (i, 0))

    def per(a, b):
        return pl.BlockSpec((1, a, b), lambda i, place: (i, 0, 0))

    return pl.pallas_call(
        attention_kernel,
        grid_spec=pltpu.PrefetchScalarGridSpec(
            num_scalar_prefetch=1,
            grid=(count,),
            in_specs=[
                given, given, whole(wt.shape), whole(merge.shape), whole(bias.shape),
                whole(ln.shape), whole(cosine.shape), whole(sine.shape),
            ],
            out_specs=[
                taken, taken, per(width, SEQ), whole((width, columns)), per(8, width),
                per(8, 2 * rows),
            ],
            scratch_shapes=[
                pltpu.VMEM((width, SEQ), BF16),
                pltpu.VMEM((width, SEQ), BF16),
                pltpu.VMEM((wt.shape[0], SEQ), BF16),
                pltpu.VMEM((width, columns), F32),
            ],
        ),
        out_shape=[
            jax.ShapeDtypeStruct((count * SEQ, width), BF16),
            jax.ShapeDtypeStruct((count * SEQ, width), BF16),
            jax.ShapeDtypeStruct((count, width, SEQ), BF16),
            jax.ShapeDtypeStruct((width, columns), BF16),
            jax.ShapeDtypeStruct((count, 8, width), F32),
            jax.ShapeDtypeStruct((count, 8, 2 * rows), F32),
        ],
        compiler_params=params("arbitrary"),
        name="attention",
        cost_estimate=pl.CostEstimate(
            flops=count * 16_000_000_000, bytes_accessed=count * 12_000_000, transcendentals=0
        ),
    )(place, x, g, wt, merge, bias, ln, cosine, sine)


def feed(place, x, g, gt, bias, ln, aout, din, at, weights, earlier, big):
    width = x.shape[1]
    groups, chunk, columns = weights[0].shape
    ff = columns // 2
    pieces = len(weights)
    sides = min(pieces, 2)
    given = pl.BlockSpec((SEQ, width), lambda i, t, place: (place[0], 0))
    taken = pl.BlockSpec((SEQ, width), lambda i, t, place: (at, 0))
    weight = pl.BlockSpec((1, chunk, columns), lambda i, t, place: (t ^ place[2], 0, 0))
    part = pl.BlockSpec(
        (pieces // sides, chunk, columns),
        lambda i, t, place: (0, 0, jnp.clip(t - 2 * place[1], 0, 1)),
    )
    anywhere = pl.BlockSpec(memory_space=pl.ANY)
    first = 8 + pieces
    alias = {first + k: 4 + k for k in range(len(earlier))}
    alias |= {first + len(earlier) + k: k for k in range(len(big))}
    return pl.pallas_call(
        functools.partial(feed_kernel, pieces=pieces, earlier=1 if earlier else 0),
        grid_spec=pltpu.PrefetchScalarGridSpec(
            num_scalar_prefetch=1,
            grid=(1, groups),
            in_specs=[
                given, given,
                pl.BlockSpec((1, width, SEQ), lambda i, t, place: (at, 0, 0)),
                pl.BlockSpec((1, 1, ff), lambda i, t, place: (t, 0, 0)),
                whole(ln.shape), taken, taken,
            ]
            + [weight] * pieces
            + [part] * len(earlier)
            + [anywhere] * len(big),
            out_specs=[
                given, given,
                whole((2, SEQ, width)),
                whole((8, width)),
            ]
            + [part] * sides,
            scratch_shapes=[
                pltpu.VMEM((SEQ, width), BF16),
                pltpu.VMEM((width, SEQ), BF16),
                pltpu.VMEM((SEQ, width), F32),
                pltpu.VMEM((SEQ, 128), F32),
                pltpu.VMEM((SEQ, width), F32),
                pltpu.VMEM((SEQ, width), F32),
                pltpu.VMEM((8, ff), F32),
                pltpu.VMEM((width, columns), BF16),
                pltpu.VMEM((width, columns), F32),
            ],
        ),
        out_shape=[
            jax.ShapeDtypeStruct(x.shape, BF16),
            jax.ShapeDtypeStruct(x.shape, F32),
            jax.ShapeDtypeStruct((2, SEQ, width), BF16),
            jax.ShapeDtypeStruct((8, width), F32),
        ]
        + [jax.ShapeDtypeStruct((pieces // sides, chunk, 2 * columns), BF16)] * sides,
        input_output_aliases=alias,
        compiler_params=params("arbitrary", "arbitrary"),
        name="feed",
        cost_estimate=pl.CostEstimate(
            flops=16_000_000_000, bytes_accessed=18_000_000, transcendentals=0
        ),
    )(place, x, g, gt, bias, ln, aout, din, *weights, *earlier, *big)


def prepare(place, weights):
    groups, chunk, columns = weights[0].shape
    pieces = len(weights)
    width = pieces * chunk
    rows = 9 * HD
    return pl.pallas_call(
        prepare_kernel,
        grid_spec=pltpu.PrefetchScalarGridSpec(
            num_scalar_prefetch=1,
            grid=(groups,),
            in_specs=[
                pl.BlockSpec((1, chunk, columns), lambda t, place: (t ^ place[2], 0, 0))
            ]
            * pieces,
            out_specs=[
                pl.BlockSpec((rows, width), lambda t, place: (t, 0)),
                pl.BlockSpec((3 * HD, width), lambda t, place: (t, 0)),
                pl.BlockSpec((1, 8, width), lambda t, place: (t, 0, 0)),
            ],
            scratch_shapes=[pltpu.VMEM((width, columns), BF16)],
        ),
        out_shape=[
            jax.ShapeDtypeStruct((groups * rows, width), BF16),
            jax.ShapeDtypeStruct((groups * 3 * HD, width), BF16),
            jax.ShapeDtypeStruct((groups, 8, width), F32),
        ],
        compiler_params=params("arbitrary"),
        name="prepare",
    )(place, *weights)


def trade(array, axis, mask):
    size = lax.axis_size(axis)
    return lax.ppermute(array, axis, [(i, i ^ mask) for i in range(size)])


def along(block):
    return jnp.stack([block] + [trade(block, "tensor", mask) for mask in (1, 2, 3)])


def across(block):
    return [block] + [trade(block, "dp", mask) for mask in (2, 4, 6)]


def both_cores(blocks):
    return [item for block in blocks for item in (block, trade(block, "dp", 1))]


def tie(array, after):
    return lax.optimization_barrier((array, after))[0]


def gather_both(early, late):
    early = along(early)
    late = along(tie(late, early))
    early = across(early)
    late = across(tie(late, early))
    early = both_cores(early)
    return early, late


def body(
    block_input, cotangent, heads_weight, heads_bias, merge_weight, merge_bias, up_weight, up_bias,
    down_weight, down_bias, first_gain, first_shift, second_gain, second_shift,
):
    chunk = heads_weight.shape[0]
    owners = lax.axis_size("dp")
    groups = lax.axis_size("tensor")
    width = block_input.shape[1]
    spot = lax.axis_index("tensor")
    odd, pair = spot % 2, spot // 2
    total = block_input.shape[0] // SEQ
    count = total // 2
    fast = owners == 8 and groups == 4
    if fast:
        me = lax.axis_index("dp")
        facts = [odd * count, pair, spot, me // 2, me % 2]
    else:
        facts = [odd * count, pair] + [jnp.zeros_like(spot)] * 3
    place = jnp.stack(facts).astype(jnp.int32)

    bias_part = heads_bias.shape[0]
    vectors = jnp.stack(
        [
            jnp.pad(heads_bias, (0, chunk - bias_part)), up_bias, merge_bias, down_bias,
            first_gain, first_shift, second_gain, second_shift,
        ],
        axis=1,
    )
    early = jnp.concatenate(
        [heads_weight, merge_weight.T, jnp.pad(vectors, ((0, 0), (0, 120)))], axis=1
    )
    late = jnp.concatenate([up_weight, down_weight.T], axis=1)
    if fast:
        early, late = gather_both(early, late)
    else:
        early, late = (
            [lax.all_gather(item, ("tensor", "dp"), axis=0, tiled=True).reshape(groups, width, -1)]
            for item in (early, late)
        )
    rows = 9 * HD
    wt, merge, vecs = prepare(place, early)
    hbias = vecs[:, 0].reshape(groups, owners, chunk)[:, :, :bias_part].reshape(groups, 1, rows)
    hbias = jnp.broadcast_to(hbias, (groups, 8, rows))
    ubias = vecs[:, 1:2, :]
    ln = jnp.concatenate(
        [vecs[0, 4:8], (vecs[0, 2] + vecs[0, 3])[None], jnp.zeros((3, width), F32)], axis=0
    )
    ff = up_weight.shape[1]
    cosine, sine = rotary_tables()
    swap = [(i, i ^ 1) for i in range(groups)]
    def shifted(i):
        return place.at[0].add(i)

    def attend(i, number, after):
        return attention(
            tie(shifted(i), after), block_input, cotangent, wt, merge, hbias, ln, cosine, sine,
            number,
        )

    def advance(i, source, at, done, after):
        aout, din, gt = source[:3]
        result = feed(
            tie(shifted(i), after), block_input, cotangent, gt, ubias, ln, aout, din, at, late,
            done[4:], done[:2],
        )
        return result, trade(result[2], "tensor", 1)

    lead = count - 1
    first = attend(0, lead, ())
    if fast:
        late = both_cores(tie(late, first[0]))
    done, other = advance(0, first, 0, (), ())
    others, totals = [other], [done[3]]
    second = attend(lead, 1, done[3])
    first_cols = first[3] + second[3]
    first_cols = lax.psum_scatter(first_cols, "dp", scatter_dimension=0, tiled=True)
    for i in range(1, count):
        source, at = (first, i) if i < lead else (second, 0)
        done, other = advance(i, source, at, done, others[i - 2] if i > 1 else second[4])
        others.append(other)
        totals.append(done[3])

    rows_a = first[4].sum(0) + second[4].sum(0)
    hb = (first[5].sum(0) + second[5].sum(0))[0]
    rows_f = sum(totals)
    hb = jnp.pad(hb.reshape(2, owners, bias_part), ((0, 0), (0, 0), (0, chunk - bias_part)))
    small = jnp.concatenate(
        [rows_a[0:2], rows_f[0:2], rows_a[2:3], rows_f[2:4], hb.reshape(2, width)], axis=0
    )
    small = lax.psum_scatter(small.T, "dp", scatter_dimension=0, tiled=True)
    if fast:
        kept, away = done[4:]
        kept = kept.astype(F32) + trade(away, "dp", 1).astype(F32)
        kept = tie(kept.astype(BF16), others[-2])
        second_cols = sum(
            item.astype(F32)
            for item in [kept[0]] + [trade(kept[k], "dp", 2 * k) for k in (1, 2, 3)]
        ).astype(BF16)
    else:
        second_cols = lax.psum_scatter(done[4][0], "dp", scatter_dimension=0, tiled=True)

    def settle(cols):
        mine = jnp.where(odd == 0, cols[0], cols[1])
        other = jnp.where(odd == 0, cols[1], cols[0])
        return mine.astype(F32) + trade(other.astype(BF16), "tensor", 1).astype(F32)

    hw = first_cols[:, : 2 * rows].reshape(chunk, 2, rows)
    mw = first_cols[:, 2 * rows :].reshape(chunk, 2, 3 * HD)
    early_sum = settle([jnp.concatenate([hw[:, k], mw[:, k]], axis=1) for k in range(2)])
    late_sum = settle(
        [
            jnp.concatenate(
                [
                    second_cols[:, 2 * ff * k : 2 * ff * (k + 1)].astype(F32),
                    small[:, 0:5], small[:, 5 + k : 6 + k], small[:, 7 + k : 8 + k],
                ],
                axis=1,
            )
            for k in range(2)
        ]
    )
    d = 2 * ff

    layer_output, input_grad = done[:2]
    start = (1 - odd) * count * SEQ
    for i, other in enumerate(others):
        at = start + i * SEQ
        layer_output = lax.dynamic_update_slice(layer_output, other[0], (at, 0))
        given = lax.dynamic_slice(cotangent, (at, 0), (SEQ, width))
        input_grad = lax.dynamic_update_slice(
            input_grad, other[1].astype(F32) + given.astype(F32), (at, 0)
        )
    return (
        layer_output,
        input_grad,
        early_sum[:, :rows],
        late_sum[:bias_part, d + 6],
        early_sum[:, rows:].T,
        late_sum[:, d + 4],
        late_sum[:, :ff],
        late_sum[:, d + 5],
        late_sum[:, ff:d].T,
        late_sum[:, d + 4],
        late_sum[:, d],
        late_sum[:, d + 1],
        late_sum[:, d + 2],
        late_sum[:, d + 3],
    )


def solution(mesh):
    placed = (
        P("dp", None),
        P("dp", None),
        P("dp", "tensor"),
        P(("tensor", "dp")),
        P("tensor", "dp"),
        P("dp"),
        P("dp", "tensor"),
        P(("tensor", "dp")),
        P("tensor", "dp"),
        P("dp"),
        P("dp"),
        P("dp"),
        P("dp"),
        P("dp"),
    )
    return jax.shard_map(
        body,
        mesh=mesh,
        in_specs=placed,
        out_specs=placed,
        check_vma=False,
    )
```

```python
import functools
import math

import jax
import jax.numpy as jnp
import numpy as np
from jax import lax
from jax.experimental import pallas as pl
from jax.experimental.pallas import tpu as pltpu
from jax.sharding import PartitionSpec as P

HD = 64
ROT = 16
SEQ = 512
EPS = 1e-05
VMEM = 56 * 1024 * 1024
F32 = jnp.float32
BF16 = jnp.bfloat16


def dot(left, right, left_dim, right_dim):
    return lax.dot_general(
        left, right, (((left_dim,), (right_dim,)), ((), ())), preferred_element_type=F32
    )


def normalise(values):
    average = jnp.mean(values, axis=-1, keepdims=True)
    centred = values - average
    spread = jnp.mean(centred * centred, axis=-1, keepdims=True)
    scale = lax.rsqrt(spread + EPS)
    return centred * scale, scale


def norm_back(d, hat, scale, gain):
    dg = d * gain
    first = jnp.mean(dg, axis=-1, keepdims=True)
    second = jnp.mean(dg * hat, axis=-1, keepdims=True)
    return (dg - first - hat * second) * scale


def rotary_tables():
    half = ROT // 2
    rates = 10000.0 ** (-(2.0 * np.arange(half)) / ROT)
    angles = rates[:, None] * np.arange(SEQ)[None, :]
    return np.cos(angles).astype(np.float32), np.sin(angles).astype(np.float32)


def rotate(values, cosine, sine):
    half = ROT // 2
    first, second = values[:half], values[half:ROT]
    return jnp.concatenate(
        [first * cosine - second * sine, second * cosine + first * sine, values[ROT:]], axis=0
    )


def piece_rows(place, index, pieces, chunk):
    if pieces == 1:
        return pl.ds(0, chunk)
    across, core = index // 2, index % 2
    owner = (across ^ place[3]) * 2 + (core ^ place[4])
    return pl.ds(pl.multiple_of(owner * chunk, 16), chunk)


def assemble(place, refs, target):
    chunk = refs[0].shape[1]
    for index, ref in enumerate(refs):
        target[piece_rows(place, index, len(refs), chunk), :] = ref[0]


def share_out(place, source, held, made, pieces):
    for index in range(pieces):
        value = source[piece_rows(place, index, pieces, made[0].shape[1]), :]
        if held:
            value = value + held[index % 2][index // 2].astype(F32)
        made[index % 2][index // 2] = value.astype(BF16)


def prepare_kernel(place, *refs, part):
    *pieces, wt_ref, merge_ref, vec_ref, bias_ref, full = refs
    assemble(place, pieces, full)
    rows = wt_ref.shape[0]
    end = rows + merge_ref.shape[0]
    wt_ref[...] = full[:, :rows].T
    merge_ref[...] = full[:, rows:end].T
    vectors = full[:, end:].astype(F32)
    vec_ref[0] = vectors.T[: vec_ref.shape[1]]
    chunk = pieces[0].shape[1]
    if len(pieces) > 1:
        packed = [vectors[at : at + part] for at in range(0, vectors.shape[0], chunk)]
        bias_ref[0] = jnp.concatenate(packed, axis=0).T[: bias_ref.shape[1]]
    else:
        bias_ref[...] = jnp.zeros_like(bias_ref)


def attention_kernel(
    place, x_ref, g_ref, wt_ref, merge_ref, bias_ref, vec_ref, cos_ref, sin_ref, *refs,
    pieces, earlier,
):
    sides = min(pieces, 2)
    held, refs = refs[: sides * earlier], refs[sides * earlier :]
    out_ref, din_ref, gt_ref, rows_ref, hb_ref = refs[:5]
    made = refs[5 : 5 + sides]
    datt, att, dmix, acc = refs[5 + sides :]
    groups = wt_ref.shape[0] // (9 * HD)
    rows = 9 * HD
    half = SEQ // 2
    scaling = 1.0 / math.sqrt(HD)
    x = x_ref[...].astype(F32)
    g = g_ref[...]
    gain, shift = vec_ref[0, 4:5, :], vec_ref[0, 5:6, :]
    hat, scale = normalise(x)
    n1 = (hat * gain + shift).astype(BF16)
    datt[...] = dot(merge_ref[...], g, 1, 1).astype(BF16)
    cosine, sine = cos_ref[...], sin_ref[...]
    below = lax.broadcasted_iota(jnp.int32, (half, half), 0) <= lax.broadcasted_iota(
        jnp.int32, (half, half), 1
    )

    def raise_columns(scores):
        raised = jnp.exp(scores - jnp.max(scores, axis=0, keepdims=True))
        return raised, jnp.sum(raised, axis=0, keepdims=True)

    def group(index, carry):
        base = pl.multiple_of(index * rows, rows)
        part = dot(wt_ref[pl.ds(base, rows), :], n1, 1, 1)
        part = part + bias_ref[index].T[:, 0:1]
        for head in range(3):
            at = head * 3 * HD
            query = (rotate(part[at : at + HD], cosine, sine) * scaling).astype(BF16)
            keys = rotate(part[at + HD : at + 2 * HD], cosine, sine).astype(BF16)
            values = part[at + 2 * HD : at + 3 * HD].astype(BF16)
            spot = pl.multiple_of(index * 3 * HD + head * HD, HD)
            given = datt[pl.ds(spot, HD), :].astype(F32)
            keys_t, values_t = keys.T, values.T
            s0 = dot(keys_t[:half], query[:, :half], 1, 0)
            s1a = dot(keys_t[:half], query[:, half:], 1, 0)
            s1b = dot(keys_t[half:], query[:, half:], 1, 0)
            e0, l0 = raise_columns(jnp.where(below, s0, -1e30))
            e1, l1 = raise_columns(
                jnp.concatenate([s1a, jnp.where(below, s1b, -1e30)], axis=0)
            )
            w0, w1 = e0.astype(BF16), e1.astype(BF16)
            share = 1.0 / jnp.concatenate([l0, l1], axis=1)
            attended = share * jnp.concatenate(
                [dot(values[:, :half], w0, 1, 0), dot(values, w1, 1, 0)], axis=1
            )
            att[pl.ds(spot, HD), :] = attended.astype(BF16)
            given = (given * share).astype(BF16)
            level = jnp.sum(given.astype(F32) * attended, axis=0, keepdims=True)
            q0 = dot(values_t[:half], given[:, :half], 1, 0)
            q1 = dot(values_t, given[:, half:], 1, 0)
            d0 = (e0 * (q0 - level[:, :half])).astype(BF16)
            d1 = (e1 * (q1 - level[:, half:])).astype(BF16)
            d_values = dot(given[:, half:], w1, 1, 1)
            d_values = jnp.concatenate(
                [d_values[:, :half] + dot(given[:, :half], w0, 1, 1), d_values[:, half:]], axis=1
            )
            d_keys = dot(query[:, half:], d1, 1, 1)
            d_keys = jnp.concatenate(
                [d_keys[:, :half] + dot(query[:, :half], d0, 1, 1), d_keys[:, half:]], axis=1
            )
            d_query = jnp.concatenate(
                [dot(keys[:, :half], d0, 1, 0), dot(keys, d1, 1, 0)], axis=1
            ) * scaling
            to = pl.multiple_of(base + at, HD)
            dmix[pl.ds(to, HD), :] = rotate(d_query, cosine, -sine).astype(BF16)
            dmix[pl.ds(to + HD, HD), :] = rotate(d_keys, cosine, -sine).astype(BF16)
            dmix[pl.ds(to + 2 * HD, HD), :] = d_values.astype(BF16)
        return carry

    lax.fori_loop(0, groups, group, 0)
    out_ref[...] = dot(att[...].T, merge_ref[...], 1, 0).astype(BF16)
    d_first = dot(dmix[...].T, wt_ref[...], 1, 0)
    pair = place[1]
    mine = dmix[pl.ds(pl.multiple_of(pair * 2 * rows, 2 * rows), 2 * rows), :]
    mine_att = att[pl.ds(pl.multiple_of(pair * 6 * HD, 6 * HD), 6 * HD), :]
    hb_ref[0] = dot(jnp.ones((8, SEQ), BF16), mine, 1, 1)
    gt = g.T
    gt_ref[0] = gt
    step = pl.program_id(0)

    @pl.when(step == 0)
    def _():
        acc[...] = jnp.zeros_like(acc)

    acc[:, : 2 * rows] += dot(n1.T, mine, 1, 1)
    acc[:, 2 * rows :] += dot(gt, mine_att, 1, 1)

    @pl.when(step == pl.num_programs(0) - 1)
    def _():
        share_out(place, acc, held, made, pieces)

    rows_ref[0] = jnp.concatenate(
        [
            jnp.sum(d_first * hat, axis=0, keepdims=True),
            jnp.sum(d_first, axis=0, keepdims=True),
            jnp.sum(g.astype(F32), axis=0, keepdims=True),
            jnp.zeros((5, x.shape[1]), F32),
        ],
        axis=0,
    )
    din_ref[...] = norm_back(d_first, hat, scale, gain).astype(BF16)


def gelu_parts(h):
    near = 0.7071067811865476 * jnp.abs(h)
    below = 1.0 + 0.3275911 * near
    t = pl.reciprocal(below, approx=True)
    t = t * (2.0 - below * t)
    bell = jnp.exp(-0.5 * h * h)
    series = 1.061405429 * t - 1.453152027
    series = series * t + 1.421413741
    series = series * t - 0.284496736
    series = series * t + 0.254829592
    tail = 0.5 * series * t * bell
    phi = jnp.where(h >= 0, 1.0 - tail, tail)
    return h * phi, phi + h * bell * 0.3989422804014327


def feed_kernel(
    place, x_ref, g_ref, gt_ref, bias_ref, vec_ref, aout_ref, din_ref, *refs, pieces, earlier,
):
    weights, refs = refs[:pieces], refs[pieces:]
    sides = min(pieces, 2)
    held, refs = refs[: sides * earlier], refs[(sides + 2) * earlier :]
    out_ref, grad_ref, send_ref, rows_ref = refs[:4]
    made = refs[4 : 4 + sides]
    n2, n2t, hat_s, scale_s, acc, dacc, sums, full, fresh = refs[4 + sides :]
    ff = full.shape[1] // 2
    step = pl.program_id(1)
    pair = place[1]
    gain, shift = vec_ref[0, 6:7, :], vec_ref[0, 7:8, :]

    @pl.when(step == 0)
    def _():
        hat, scale = normalise(x_ref[...].astype(F32))
        hat_s[...] = hat
        scale_s[...] = jnp.broadcast_to(scale, scale_s.shape)
        n2[...] = (hat * gain + shift).astype(BF16)
        n2t[...] = n2[...].T
        sums[...] = jnp.zeros_like(sums)
        acc[...] = x_ref[...].astype(F32) + aout_ref[...].astype(F32)
        acc[...] += vec_ref[0, 2:3, :] + vec_ref[0, 3:4, :]
        dacc[...] = jnp.zeros_like(dacc)

    assemble(place, weights, full)
    up, down = full[:, :ff], full[:, ff:]
    h = dot(n2[...], up, 1, 0) + bias_ref[0, 1:2, :]
    activated, slope = gelu_parts(h)
    activated = activated.astype(BF16)
    d_hidden = (dot(g_ref[...], down, 1, 0) * slope).astype(BF16)
    acc[...] += dot(activated, down, 1, 1)
    dacc[...] += dot(d_hidden, up, 1, 1)

    @pl.when(step // 2 == pair)
    def _():
        fresh[:, :ff] = dot(n2t[...], d_hidden, 1, 0)
        fresh[:, ff:] = dot(gt_ref[0], activated, 1, 0)
        share_out(place, fresh, held, made, pieces)
        sums[pl.ds(step % 2, 1), :] = jnp.sum(d_hidden.astype(F32), axis=0, keepdims=True)

    @pl.when(step == pl.num_programs(1) - 1)
    def _():
        d_second = dacc[...]
        hat = hat_s[...]
        finished = acc[...].astype(BF16)
        out_ref[...] = finished
        send_ref[0] = finished
        total = norm_back(d_second, hat, scale_s[:, 0:1], gain) + din_ref[...].astype(F32)
        total = total.astype(BF16)
        send_ref[1] = total
        grad_ref[...] = total.astype(F32) + g_ref[...].astype(F32)
        rows_ref[...] = jnp.concatenate(
            [
                jnp.sum(d_second * hat, axis=0, keepdims=True),
                jnp.sum(d_second, axis=0, keepdims=True),
                sums[0:2, :],
                jnp.zeros((4, hat.shape[1]), F32),
            ],
            axis=0,
        )


def heads_grad_kernel(n1t_ref, gt_ref, dmh_ref, atth_ref, out_ref, acc):
    step = pl.program_id(0)
    width = dmh_ref.shape[1]

    @pl.when(step == 0)
    def _():
        acc[...] = jnp.zeros_like(acc)

    acc[:, :width] += dot(n1t_ref[0], dmh_ref[0], 1, 1)
    acc[:, width:] += dot(gt_ref[0], atth_ref[0], 1, 1)

    @pl.when(step == pl.num_programs(0) - 1)
    def _():
        out_ref[...] = acc[...].astype(BF16)


def params(*kinds):
    return pltpu.CompilerParams(dimension_semantics=kinds, vmem_limit_bytes=VMEM)


def whole(shape):
    zeros = (0,) * len(shape)
    return pl.BlockSpec(shape, lambda *_: zeros)


def attention(place, x, g, wt, merge, bias, vecs, cosine, sine, count, pieces, earlier):
    width = x.shape[1]
    rows = 9 * HD
    columns = 2 * rows + 6 * HD
    given = pl.BlockSpec((SEQ, width), lambda i, place: (place[0] + i, 0))
    taken = pl.BlockSpec((SEQ, width), lambda i, place: (i, 0))

    def per(a, b):
        return pl.BlockSpec((1, a, b), lambda i, place: (i, 0, 0))

    sides = min(pieces, 2)
    part = (pieces // sides, width // pieces, columns)
    return pl.pallas_call(
        functools.partial(attention_kernel, pieces=pieces, earlier=1 if earlier else 0),
        grid_spec=pltpu.PrefetchScalarGridSpec(
            num_scalar_prefetch=1,
            grid=(count,),
            in_specs=[
                given, given, whole(wt.shape), whole(merge.shape), whole(bias.shape),
                whole((1, 8, width)), whole(cosine.shape), whole(sine.shape),
            ]
            + [whole(part)] * len(earlier),
            out_specs=[taken, taken, per(width, SEQ), per(8, width), per(8, 2 * rows)]
            + [whole(part)] * sides,
            scratch_shapes=[
                pltpu.VMEM((width, SEQ), BF16),
                pltpu.VMEM((width, SEQ), BF16),
                pltpu.VMEM((wt.shape[0], SEQ), BF16),
                pltpu.VMEM((width, columns), F32),
            ],
        ),
        out_shape=[
            jax.ShapeDtypeStruct((count * SEQ, width), BF16),
            jax.ShapeDtypeStruct((count * SEQ, width), BF16),
            jax.ShapeDtypeStruct((count, width, SEQ), BF16),
            jax.ShapeDtypeStruct((count, 8, width), F32),
            jax.ShapeDtypeStruct((count, 8, 2 * rows), F32),
        ]
        + [jax.ShapeDtypeStruct(part, BF16)] * sides,
        compiler_params=params("arbitrary"),
        name="attention",
        cost_estimate=pl.CostEstimate(
            flops=count * 16_000_000_000, bytes_accessed=count * 12_000_000, transcendentals=0
        ),
    )(place, x, g, wt, merge, bias, vecs, cosine, sine, *earlier)


def feed(place, x, g, gt, vecs, aout, din, at, weights, earlier, big):
    width = x.shape[1]
    groups, chunk, columns = weights[0].shape
    ff = columns // 2
    pieces = len(weights)
    sides = min(pieces, 2)
    given = pl.BlockSpec((SEQ, width), lambda i, t, place: (place[0], 0))
    taken = pl.BlockSpec((SEQ, width), lambda i, t, place: (at, 0))
    weight = pl.BlockSpec((1, chunk, columns), lambda i, t, place: (t ^ place[2], 0, 0))
    part = pl.BlockSpec(
        (pieces // sides, chunk, columns),
        lambda i, t, place: (0, 0, jnp.clip(t - 2 * place[1], 0, 1)),
    )
    anywhere = pl.BlockSpec(memory_space=pl.ANY)
    first = 8 + pieces
    alias = {first + k: 4 + k for k in range(len(earlier))}
    alias |= {first + len(earlier) + k: k for k in range(len(big))}
    return pl.pallas_call(
        functools.partial(feed_kernel, pieces=pieces, earlier=1 if earlier else 0),
        grid_spec=pltpu.PrefetchScalarGridSpec(
            num_scalar_prefetch=1,
            grid=(1, groups),
            in_specs=[
                given, given,
                pl.BlockSpec((1, width, SEQ), lambda i, t, place: (at, 0, 0)),
                pl.BlockSpec((1, 8, ff), lambda i, t, place: (t, 0, 0)),
                whole((1, 8, width)), taken, taken,
            ]
            + [weight] * pieces
            + [part] * len(earlier)
            + [anywhere] * len(big),
            out_specs=[
                given, given,
                whole((2, SEQ, width)),
                whole((8, width)),
            ]
            + [part] * sides,
            scratch_shapes=[
                pltpu.VMEM((SEQ, width), BF16),
                pltpu.VMEM((width, SEQ), BF16),
                pltpu.VMEM((SEQ, width), F32),
                pltpu.VMEM((SEQ, 128), F32),
                pltpu.VMEM((SEQ, width), F32),
                pltpu.VMEM((SEQ, width), F32),
                pltpu.VMEM((8, ff), F32),
                pltpu.VMEM((width, columns), BF16),
                pltpu.VMEM((width, columns), F32),
            ],
        ),
        out_shape=[
            jax.ShapeDtypeStruct(x.shape, BF16),
            jax.ShapeDtypeStruct(x.shape, F32),
            jax.ShapeDtypeStruct((2, SEQ, width), BF16),
            jax.ShapeDtypeStruct((8, width), F32),
        ]
        + [jax.ShapeDtypeStruct((pieces // sides, chunk, 2 * columns), BF16)] * sides,
        input_output_aliases=alias,
        compiler_params=params("arbitrary", "arbitrary"),
        name="feed",
        cost_estimate=pl.CostEstimate(
            flops=16_000_000_000, bytes_accessed=18_000_000, transcendentals=0
        ),
    )(place, x, g, gt, vecs, vecs, aout, din, *weights, *earlier, *big)


def prepare(place, weights, part):
    groups, chunk, columns = weights[0].shape
    pieces = len(weights)
    width = pieces * chunk
    rows = 9 * HD
    return pl.pallas_call(
        functools.partial(prepare_kernel, part=part),
        grid_spec=pltpu.PrefetchScalarGridSpec(
            num_scalar_prefetch=1,
            grid=(groups,),
            in_specs=[
                pl.BlockSpec((1, chunk, columns), lambda t, place: (t ^ place[2], 0, 0))
            ]
            * pieces,
            out_specs=[
                pl.BlockSpec((rows, width), lambda t, place: (t, 0)),
                pl.BlockSpec((3 * HD, width), lambda t, place: (t, 0)),
                pl.BlockSpec((1, 8, width), lambda t, place: (t, 0, 0)),
                pl.BlockSpec((1, 8, rows), lambda t, place: (t, 0, 0)),
            ],
            scratch_shapes=[pltpu.VMEM((width, columns), BF16)],
        ),
        out_shape=[
            jax.ShapeDtypeStruct((groups * rows, width), BF16),
            jax.ShapeDtypeStruct((groups * 3 * HD, width), BF16),
            jax.ShapeDtypeStruct((groups, 8, width), F32),
            jax.ShapeDtypeStruct((groups, 8, rows), F32),
        ],
        compiler_params=params("arbitrary"),
        name="prepare",
    )(place, *weights)


def trade(array, axis, mask):
    size = lax.axis_size(axis)
    return lax.ppermute(array, axis, [(i, i ^ mask) for i in range(size)])


def along(block):
    return jnp.stack([block] + [trade(block, "tensor", mask) for mask in (1, 2, 3)])


def across(block):
    return [block] + [trade(block, "dp", mask) for mask in (2, 4, 6)]


def both_cores(blocks):
    return [item for block in blocks for item in (block, trade(block, "dp", 1))]


def tie(array, after):
    return lax.optimization_barrier((array, after))[0]


def gather_both(early, late):
    early = along(early)
    late = along(tie(late, early))
    early = across(early)
    ahead = late
    late = across(tie(late, early))
    early = both_cores([tie(item, ahead) for item in early])
    return early, late


def reduce_cores(kept, away):
    return kept.astype(F32) + trade(away, "dp", 1).astype(F32)


def reduce_across(pieces, after=()):
    received = tie([trade(pieces[k], "dp", 2 * k) for k in (1, 2, 3)], after)
    return sum(item.astype(F32) for item in [pieces[0]] + received)


def body(
    block_input, cotangent, heads_weight, heads_bias, merge_weight, merge_bias, up_weight, up_bias,
    down_weight, down_bias, first_gain, first_shift, second_gain, second_shift,
):
    chunk = heads_weight.shape[0]
    owners = lax.axis_size("dp")
    groups = lax.axis_size("tensor")
    width = block_input.shape[1]
    spot = lax.axis_index("tensor")
    odd, pair = spot % 2, spot // 2
    total = block_input.shape[0] // SEQ
    count = total // 2
    fast = owners == 8 and groups == 4
    if fast:
        me = lax.axis_index("dp")
        facts = [odd * count, pair, spot, me // 2, me % 2]
    else:
        facts = [odd * count, pair] + [jnp.zeros_like(spot)] * 3
    place = jnp.stack(facts).astype(jnp.int32)

    bias_part = heads_bias.shape[0]
    vectors = jnp.stack(
        [
            jnp.pad(heads_bias, (0, chunk - bias_part)), up_bias, merge_bias, down_bias,
            first_gain, first_shift, second_gain, second_shift,
        ],
        axis=1,
    )
    early = jnp.concatenate(
        [heads_weight, merge_weight.T, jnp.pad(vectors, ((0, 0), (0, 120)))], axis=1
    )
    late = jnp.concatenate([up_weight, down_weight.T], axis=1)
    if fast:
        early, late = gather_both(early, late)
    else:
        early, late = (
            [lax.all_gather(item, ("tensor", "dp"), axis=0, tiled=True).reshape(groups, width, -1)]
            for item in (early, late)
        )
    rows = 9 * HD
    wt, merge, vecs, hbias = prepare(place, early, bias_part)
    if not fast:
        hbias = vecs[:, 0].reshape(groups, owners, chunk)[:, :, :bias_part]
        hbias = jnp.broadcast_to(hbias.reshape(groups, 1, rows), (groups, 8, rows))
    ff = up_weight.shape[1]
    cosine, sine = rotary_tables()
    swap = [(i, i ^ 1) for i in range(groups)]
    def shifted(i):
        return place.at[0].add(i)

    def attend(i, number, earlier, after):
        return attention(
            tie(shifted(i), after), block_input, cotangent, wt, merge, hbias, vecs, cosine, sine,
            number, len(early), earlier,
        )

    def advance(i, source, at, done, after):
        aout, din, gt = source[:3]
        result = feed(
            tie(shifted(i), after), block_input, cotangent, gt, vecs, aout, din, at, late,
            done[4:], done[:2],
        )
        return result, trade(result[2], "tensor", 1)

    lead = count - 1
    first = attend(0, lead, [], ())
    if fast:
        late = both_cores(tie(late, first[0]))
    done, other = advance(0, first, 0, [], ())
    others, totals = [other], [done[3]]
    second = attend(lead, 1, first[5:], done[3])
    wait = second[3]
    for i in range(1, count):
        source, at = (first, i) if i < lead else (second, 0)
        done, other = advance(i, source, at, done, wait)
        others.append(other)
        totals.append(done[3])
        if i == 1:
            if fast:
                heads_part = reduce_cores(*second[5:]).astype(BF16)
                wait = others[0], heads_part
            else:
                wait = others[0]
    if fast:
        heads_cols = reduce_across(heads_part, done[3]).astype(BF16)
    else:
        heads_cols = lax.psum_scatter(second[5][0], "dp", scatter_dimension=0, tiled=True)

    rows_a = first[3].sum(0) + second[3].sum(0)
    hb = (first[4].sum(0) + second[4].sum(0))[0]
    rows_f = sum(totals)
    hb = jnp.pad(hb.reshape(2, owners, bias_part), ((0, 0), (0, 0), (0, chunk - bias_part)))
    small = jnp.concatenate(
        [
            rows_a[0:2], rows_f[0:2], rows_a[2:3], rows_f[2:4], hb.reshape(2, width),
            jnp.zeros((3, width), F32),
        ],
        axis=0,
    )
    small = small + trade(small, "tensor", 1)
    if fast:
        kept, away = done[4:]
        kept = reduce_cores(kept, away).astype(BF16)
        small = (small + trade(small, "dp", 1)).reshape(-1, 4 * ff)
        tail = small.shape[0]
        small = jnp.pad(small, ((0, 8 - tail), (0, 0))).astype(BF16)
        kept = tie(kept, (others[-2], heads_cols))
        feed_cols = reduce_across([jnp.concatenate([item, small]) for item in kept])
        small = feed_cols[chunk : chunk + tail].reshape(-1, width)
        small = lax.dynamic_slice(small, (0, me * chunk), (small.shape[0], chunk))
        feed_cols = feed_cols[:chunk].astype(BF16)
    else:
        feed_cols = lax.psum_scatter(done[4][0], "dp", scatter_dimension=0, tiled=True)
        small = lax.psum_scatter(small, "dp", scatter_dimension=1, tiled=True)

    def settle(cols):
        half = cols.shape[1] // 2
        mine = jnp.where(odd == 0, cols[:, :half], cols[:, half:])
        other = jnp.where(odd == 0, cols[:, half:], cols[:, :half])
        return mine.astype(F32) + trade(other, "tensor", 1).astype(F32)

    wide = 2 * rows
    heads_cols = jnp.concatenate(
        [
            heads_cols[:, :rows], heads_cols[:, wide : wide + 3 * HD],
            heads_cols[:, rows:wide], heads_cols[:, wide + 3 * HD :],
        ],
        axis=1,
    )
    heads_sum = settle(heads_cols)
    feed_sum = settle(feed_cols)

    layer_output, input_grad = done[:2]
    start = (1 - odd) * count * SEQ
    for i, other in enumerate(others):
        at = start + i * SEQ
        layer_output = lax.dynamic_update_slice(layer_output, other[0], (at, 0))
        given = lax.dynamic_slice(cotangent, (at, 0), (SEQ, width))
        input_grad = lax.dynamic_update_slice(
            input_grad, other[1].astype(F32) + given.astype(F32), (at, 0)
        )
    return (
        layer_output,
        input_grad,
        heads_sum[:, :rows],
        jnp.where(odd == 0, small[7], small[8])[:bias_part],
        heads_sum[:, rows:].T,
        small[4],
        feed_sum[:, :ff],
        jnp.where(odd == 0, small[5], small[6]),
        feed_sum[:, ff:].T,
        small[4],
        small[0],
        small[1],
        small[2],
        small[3],
    )


def solution(mesh):
    placed = (
        P("dp", None),
        P("dp", None),
        P("dp", "tensor"),
        P(("tensor", "dp")),
        P("tensor", "dp"),
        P("dp"),
        P("dp", "tensor"),
        P(("tensor", "dp")),
        P("tensor", "dp"),
        P("dp"),
        P("dp"),
        P("dp"),
        P("dp"),
        P("dp"),
    )
    return jax.shard_map(
        body,
        mesh=mesh,
        in_specs=placed,
        out_specs=placed,
        check_vma=False,
    )
```

```python
import functools
import math

import jax
import jax.numpy as jnp
import numpy as np
from jax import lax
from jax.experimental import pallas as pl
from jax.experimental.pallas import tpu as pltpu
from jax.sharding import PartitionSpec as P

HD = 64
ROT = 16
SEQ = 512
EPS = 1e-05
VMEM = 60 * 1024 * 1024
F32 = jnp.float32
BF16 = jnp.bfloat16


def dot(left, right, left_dim, right_dim):
    return lax.dot_general(
        left, right, (((left_dim,), (right_dim,)), ((), ())), preferred_element_type=F32
    )


def normalise(values):
    average = jnp.mean(values, axis=-1, keepdims=True)
    centred = values - average
    spread = jnp.mean(centred * centred, axis=-1, keepdims=True)
    scale = lax.rsqrt(spread + EPS)
    return centred * scale, scale


def norm_back(d, hat, scale, gain):
    dg = d * gain
    first = jnp.mean(dg, axis=-1, keepdims=True)
    second = jnp.mean(dg * hat, axis=-1, keepdims=True)
    return (dg - first - hat * second) * scale


def rotary_tables():
    half = ROT // 2
    rates = 10000.0 ** (-(2.0 * np.arange(half)) / ROT)
    angles = rates[:, None] * np.arange(SEQ)[None, :]
    return np.cos(angles).astype(np.float32), np.sin(angles).astype(np.float32)


def rotate(values, cosine, sine):
    half = ROT // 2
    first, second = values[:half], values[half:ROT]
    return jnp.concatenate(
        [first * cosine - second * sine, second * cosine + first * sine, values[ROT:]], axis=0
    )


def piece_rows(place, index, pieces, chunk):
    if pieces == 1:
        return pl.ds(0, chunk)
    across, core = index // 2, index % 2
    owner = (across ^ place[3]) * 2 + (core ^ place[4])
    return pl.ds(pl.multiple_of(owner * chunk, 16), chunk)


def assemble(place, refs, target):
    chunk = refs[0].shape[1]
    for index, ref in enumerate(refs):
        target[piece_rows(place, index, len(refs), chunk), :] = ref[0]


def share_out(place, source, held, made, pieces):
    for index in range(pieces):
        value = source[piece_rows(place, index, pieces, made[0].shape[1]), :]
        if held:
            value = value + held[index % 2][index // 2].astype(F32)
        made[index % 2][index // 2] = value.astype(BF16)


def prepare_kernel(place, *refs, part):
    *pieces, wt_ref, merge_ref, vec_ref, bias_ref, full = refs
    assemble(place, pieces, full)
    rows = wt_ref.shape[0]
    end = rows + merge_ref.shape[0]
    wt_ref[...] = full[:, :rows].T
    merge_ref[...] = full[:, rows:end].T
    vectors = full[:, end:].astype(F32)
    vec_ref[0] = vectors.T[: vec_ref.shape[1]]
    chunk = pieces[0].shape[1]
    if len(pieces) > 1:
        packed = [vectors[at : at + part] for at in range(0, vectors.shape[0], chunk)]
        bias_ref[0] = jnp.concatenate(packed, axis=0).T[: bias_ref.shape[1]]
    else:
        bias_ref[...] = jnp.zeros_like(bias_ref)


def attention_kernel(
    place, x_ref, g_ref, wt_ref, merge_ref, bias_ref, vec_ref, cos_ref, sin_ref, *refs,
    pieces, earlier,
):
    sides = min(pieces, 2)
    held, refs = refs[: sides * earlier], refs[sides * earlier :]
    out_ref, din_ref, rows_ref, hb_ref = refs[:4]
    made = refs[4 : 4 + sides]
    datt, att, dmix, acc = refs[4 + sides :]
    groups = wt_ref.shape[0] // (9 * HD)
    rows = 9 * HD
    half = SEQ // 2
    scaling = 1.0 / math.sqrt(HD)
    x = x_ref[...].astype(F32)
    g = g_ref[...]
    gain, shift = vec_ref[0, 4:5, :], vec_ref[0, 5:6, :]
    hat, scale = normalise(x)
    n1 = (hat * gain + shift).astype(BF16)
    datt[...] = dot(merge_ref[...], g, 1, 1).astype(BF16)
    cosine, sine = cos_ref[...], sin_ref[...]
    below = lax.broadcasted_iota(jnp.int32, (half, half), 0) <= lax.broadcasted_iota(
        jnp.int32, (half, half), 1
    )

    def raise_columns(scores):
        raised = jnp.exp(scores - jnp.max(scores, axis=0, keepdims=True))
        return raised, jnp.sum(raised, axis=0, keepdims=True)

    def group(index, carry):
        base = pl.multiple_of(index * rows, rows)
        part = dot(wt_ref[pl.ds(base, rows), :], n1, 1, 1)
        part = part + bias_ref[index].T[:, 0:1]
        for head in range(3):
            at = head * 3 * HD
            query = (rotate(part[at : at + HD], cosine, sine) * scaling).astype(BF16)
            keys = rotate(part[at + HD : at + 2 * HD], cosine, sine).astype(BF16)
            values = part[at + 2 * HD : at + 3 * HD].astype(BF16)
            spot = pl.multiple_of(index * 3 * HD + head * HD, HD)
            given = datt[pl.ds(spot, HD), :].astype(F32)
            keys_t, values_t = keys.T, values.T
            s0 = dot(keys_t[:half], query[:, :half], 1, 0)
            s1a = dot(keys_t[:half], query[:, half:], 1, 0)
            s1b = dot(keys_t[half:], query[:, half:], 1, 0)
            e0, l0 = raise_columns(jnp.where(below, s0, -1e30))
            e1, l1 = raise_columns(
                jnp.concatenate([s1a, jnp.where(below, s1b, -1e30)], axis=0)
            )
            w0, w1 = e0.astype(BF16), e1.astype(BF16)
            share = 1.0 / jnp.concatenate([l0, l1], axis=1)
            attended = share * jnp.concatenate(
                [dot(values[:, :half], w0, 1, 0), dot(values, w1, 1, 0)], axis=1
            )
            att[pl.ds(spot, HD), :] = attended.astype(BF16)
            given = (given * share).astype(BF16)
            level = jnp.sum(given.astype(F32) * attended, axis=0, keepdims=True)
            q0 = dot(values_t[:half], given[:, :half], 1, 0)
            q1 = dot(values_t, given[:, half:], 1, 0)
            d0 = (e0 * (q0 - level[:, :half])).astype(BF16)
            d1 = (e1 * (q1 - level[:, half:])).astype(BF16)
            d_values = dot(given[:, half:], w1, 1, 1)
            d_values = jnp.concatenate(
                [d_values[:, :half] + dot(given[:, :half], w0, 1, 1), d_values[:, half:]], axis=1
            )
            d_keys = dot(query[:, half:], d1, 1, 1)
            d_keys = jnp.concatenate(
                [d_keys[:, :half] + dot(query[:, :half], d0, 1, 1), d_keys[:, half:]], axis=1
            )
            d_query = jnp.concatenate(
                [dot(keys[:, :half], d0, 1, 0), dot(keys, d1, 1, 0)], axis=1
            ) * scaling
            to = pl.multiple_of(base + at, HD)
            dmix[pl.ds(to, HD), :] = rotate(d_query, cosine, -sine).astype(BF16)
            dmix[pl.ds(to + HD, HD), :] = rotate(d_keys, cosine, -sine).astype(BF16)
            dmix[pl.ds(to + 2 * HD, HD), :] = d_values.astype(BF16)
        return carry

    lax.fori_loop(0, groups, group, 0)
    out_ref[...] = dot(att[...].T, merge_ref[...], 1, 0).astype(BF16)
    d_first = dot(dmix[...].T, wt_ref[...], 1, 0)
    pair = place[1]
    mine = dmix[pl.ds(pl.multiple_of(pair * 2 * rows, 2 * rows), 2 * rows), :]
    mine_att = att[pl.ds(pl.multiple_of(pair * 6 * HD, 6 * HD), 6 * HD), :]
    hb_ref[0] = dot(jnp.ones((8, SEQ), BF16), mine, 1, 1)
    step = pl.program_id(0)

    @pl.when(step == 0)
    def _():
        acc[...] = jnp.zeros_like(acc)

    acc[:, : 2 * rows] += dot(n1.T, mine, 1, 1)
    acc[:, 2 * rows :] += dot(g.T, mine_att, 1, 1)

    @pl.when(step == pl.num_programs(0) - 1)
    def _():
        share_out(place, acc, held, made, pieces)

    rows_ref[0] = jnp.concatenate(
        [
            jnp.sum(d_first * hat, axis=0, keepdims=True),
            jnp.sum(d_first, axis=0, keepdims=True),
            jnp.sum(g.astype(F32), axis=0, keepdims=True),
            jnp.zeros((5, x.shape[1]), F32),
        ],
        axis=0,
    )
    din_ref[...] = norm_back(d_first, hat, scale, gain).astype(BF16)


def gelu_parts(h):
    near = 0.7071067811865476 * jnp.abs(h)
    below = 1.0 + 0.3275911 * near
    t = pl.reciprocal(below, approx=True)
    t = t * (2.0 - below * t)
    bell = jnp.exp(-0.5 * h * h)
    series = 1.061405429 * t - 1.453152027
    series = series * t + 1.421413741
    series = series * t - 0.284496736
    series = series * t + 0.254829592
    tail = 0.5 * series * t * bell
    phi = jnp.where(h >= 0, 1.0 - tail, tail)
    return h * phi, phi + h * bell * 0.3989422804014327


def feed_kernel(
    place, x_ref, g_ref, bias_ref, vec_ref, aout_ref, din_ref, *refs, pieces, earlier, at,
):
    weights, refs = refs[:pieces], refs[pieces:]
    sides = min(pieces, 2)
    held, refs = refs[: sides * earlier], refs[sides * earlier :]
    send_ref, rows_ref = refs[:2]
    made = refs[2 : 2 + sides]
    n2, turned, n2t, gt, up, down, extra, part_s, load_sem, held_sem, extra_sem, out_sem = refs[
        2 + sides :
    ]
    chunk = weights[0].shape[1]
    ff = up.shape[2] // 2
    loads = [[], []]
    for step in range(2):
        for index, ref in enumerate(weights):
            rows = piece_rows(place, index, pieces, chunk)
            for side in range(2):
                spot = slice(side * ff, (side + 1) * ff)
                for kind, target in enumerate((up, down)):
                    copy = pltpu.make_async_copy(
                        ref.at[2 * step + side, :, kind * ff : (kind + 1) * ff],
                        target.at[step, rows, spot],
                        load_sem.at[step, index, side, kind],
                    )
                    copy.start()
                    loads[step].append(copy)
    fetched = [
        pltpu.make_async_copy(held[k], part_s.at[k], held_sem.at[k])
        for k in range(sides * earlier)
    ]
    fetched += [
        pltpu.make_async_copy(ref.at[at * SEQ : (at + 1) * SEQ], extra.at[k], extra_sem.at[k])
        for k, ref in enumerate((aout_ref, din_ref))
    ]
    for copy in fetched:
        copy.start()

    gain, shift = vec_ref[0, 6:7, :], vec_ref[0, 7:8, :]
    hat, scale = normalise(x_ref[...].astype(F32))
    n2[...] = (hat * gain + shift).astype(BF16)
    for source, target in ((n2, n2t), (g_ref, gt)):
        turned[...] = source[...].T
        for index in range(pieces):
            rows = piece_rows(place, index, pieces, chunk)
            target[index * chunk : (index + 1) * chunk, :] = turned[rows, :]

    def pair_of_groups(step):
        for copy in loads[step]:
            copy.wait()
        which, parity = place[1] ^ step, place[2] % 2
        bias = jnp.concatenate(
            [bias_ref[2 * which + parity, 1:2, :], bias_ref[2 * which + 1 - parity, 1:2, :]],
            axis=1,
        )
        activated, slope = gelu_parts(dot(n2[...], up[step], 1, 0) + bias)
        activated = activated.astype(BF16)
        d_hidden = (dot(g_ref[...], down[step], 1, 0) * slope).astype(BF16)
        return (
            activated,
            d_hidden,
            dot(activated, down[step], 1, 1),
            dot(d_hidden, up[step], 1, 1),
        )

    activated, d_hidden, part, d_part = pair_of_groups(0)
    for copy in fetched[: sides * earlier]:
        copy.wait()
    for left, right, spot in ((n2t, d_hidden, 0), (gt, activated, 2 * ff)):
        fresh = dot(left[...], right, 1, 0)
        for index in range(pieces):
            value = fresh[index * chunk : (index + 1) * chunk, :]
            spots = (index % 2, index // 2, slice(None), slice(spot, spot + 2 * ff))
            if earlier:
                value = value + part_s[spots].astype(F32)
            part_s[spots] = value.astype(BF16)
    stores = [pltpu.make_async_copy(part_s.at[k], made[k], out_sem.at[k]) for k in range(sides)]
    for copy in stores:
        copy.start()
    sums = jnp.sum(d_hidden.astype(F32), axis=0, keepdims=True)

    _, _, more, d_more = pair_of_groups(1)
    d_second = d_part + d_more
    for copy in fetched[sides * earlier :]:
        copy.wait()
    base = x_ref[...].astype(F32) + extra[0].astype(F32)
    base = base + vec_ref[0, 2:3, :] + vec_ref[0, 3:4, :]
    send_ref[0] = (part + more + base).astype(BF16)
    total = norm_back(d_second, hat, scale, gain) + extra[1].astype(F32)
    send_ref[1] = total.astype(BF16)
    rows_ref[...] = jnp.concatenate(
        [
            jnp.sum(d_second * hat, axis=0, keepdims=True),
            jnp.sum(d_second, axis=0, keepdims=True),
            sums[:, :ff],
            sums[:, ff:],
            jnp.zeros((4, hat.shape[1]), F32),
        ],
        axis=0,
    )
    for copy in stores:
        copy.wait()


def params(*kinds):
    return pltpu.CompilerParams(dimension_semantics=kinds, vmem_limit_bytes=VMEM)


def whole(shape):
    zeros = (0,) * len(shape)
    return pl.BlockSpec(shape, lambda *_: zeros)


def attention(place, x, g, wt, merge, bias, vecs, cosine, sine, count, pieces, earlier):
    width = x.shape[1]
    rows = 9 * HD
    columns = 2 * rows + 6 * HD
    given = pl.BlockSpec((SEQ, width), lambda i, place: (place[0] + i, 0))
    taken = pl.BlockSpec((SEQ, width), lambda i, place: (i, 0))

    def per(a, b):
        return pl.BlockSpec((1, a, b), lambda i, place: (i, 0, 0))

    sides = min(pieces, 2)
    part = (pieces // sides, width // pieces, columns)
    return pl.pallas_call(
        functools.partial(attention_kernel, pieces=pieces, earlier=1 if earlier else 0),
        grid_spec=pltpu.PrefetchScalarGridSpec(
            num_scalar_prefetch=1,
            grid=(count,),
            in_specs=[
                given, given, whole(wt.shape), whole(merge.shape), whole(bias.shape),
                whole((1, 8, width)), whole(cosine.shape), whole(sine.shape),
            ]
            + [whole(part)] * len(earlier),
            out_specs=[taken, taken, per(8, width), per(8, 2 * rows)]
            + [whole(part)] * sides,
            scratch_shapes=[
                pltpu.VMEM((width, SEQ), BF16),
                pltpu.VMEM((width, SEQ), BF16),
                pltpu.VMEM((wt.shape[0], SEQ), BF16),
                pltpu.VMEM((width, columns), F32),
            ],
        ),
        out_shape=[
            jax.ShapeDtypeStruct((count * SEQ, width), BF16),
            jax.ShapeDtypeStruct((count * SEQ, width), BF16),
            jax.ShapeDtypeStruct((count, 8, width), F32),
            jax.ShapeDtypeStruct((count, 8, 2 * rows), F32),
        ]
        + [jax.ShapeDtypeStruct(part, BF16)] * sides,
        compiler_params=params("arbitrary"),
        name="attention",
        cost_estimate=pl.CostEstimate(
            flops=count * 16_000_000_000, bytes_accessed=count * 12_000_000, transcendentals=0
        ),
    )(place, x, g, wt, merge, bias, vecs, cosine, sine, *earlier)


def feed(place, x, g, vecs, aout, din, at, weights, earlier):
    width = x.shape[1]
    groups, chunk, columns = weights[0].shape
    ff = columns // 2
    pieces = len(weights)
    sides = min(pieces, 2)
    given = pl.BlockSpec((SEQ, width), lambda s, place: (place[0], 0))
    part = (pieces // sides, chunk, 2 * columns)
    anywhere = pl.BlockSpec(memory_space=pl.ANY)
    first = 7 + pieces
    return pl.pallas_call(
        functools.partial(feed_kernel, pieces=pieces, earlier=1 if earlier else 0, at=at),
        grid_spec=pltpu.PrefetchScalarGridSpec(
            num_scalar_prefetch=1,
            grid=(1,),
            in_specs=[given, given, whole(vecs.shape), whole((1, 8, width))]
            + [anywhere] * (2 + pieces + len(earlier)),
            out_specs=[whole((2, SEQ, width)), whole((8, width))] + [anywhere] * sides,
            scratch_shapes=[
                pltpu.VMEM((SEQ, width), BF16),
                pltpu.VMEM((width, SEQ), BF16),
                pltpu.VMEM((width, SEQ), BF16),
                pltpu.VMEM((width, SEQ), BF16),
                pltpu.VMEM((2, width, columns), BF16),
                pltpu.VMEM((2, width, columns), BF16),
                pltpu.VMEM((2, SEQ, width), BF16),
                pltpu.VMEM((sides, *part), BF16),
                pltpu.SemaphoreType.DMA((2, pieces, 2, 2)),
                pltpu.SemaphoreType.DMA((2,)),
                pltpu.SemaphoreType.DMA((2,)),
                pltpu.SemaphoreType.DMA((2,)),
            ],
        ),
        out_shape=[
            jax.ShapeDtypeStruct((2, SEQ, width), BF16),
            jax.ShapeDtypeStruct((8, width), F32),
        ]
        + [jax.ShapeDtypeStruct(part, BF16)] * sides,
        input_output_aliases={first + k: 2 + k for k in range(len(earlier))},
        compiler_params=params("arbitrary"),
        name="feed",
        cost_estimate=pl.CostEstimate(
            flops=16_000_000_000, bytes_accessed=18_000_000, transcendentals=0
        ),
    )(place, x, g, vecs, vecs, aout, din, *weights, *earlier)


def prepare(place, weights, part):
    groups, chunk, columns = weights[0].shape
    pieces = len(weights)
    width = pieces * chunk
    rows = 9 * HD
    return pl.pallas_call(
        functools.partial(prepare_kernel, part=part),
        grid_spec=pltpu.PrefetchScalarGridSpec(
            num_scalar_prefetch=1,
            grid=(groups,),
            in_specs=[
                pl.BlockSpec((1, chunk, columns), lambda t, place: (t ^ place[2], 0, 0))
            ]
            * pieces,
            out_specs=[
                pl.BlockSpec((rows, width), lambda t, place: (t, 0)),
                pl.BlockSpec((3 * HD, width), lambda t, place: (t, 0)),
                pl.BlockSpec((1, 8, width), lambda t, place: (t, 0, 0)),
                pl.BlockSpec((1, 8, rows), lambda t, place: (t, 0, 0)),
            ],
            scratch_shapes=[pltpu.VMEM((width, columns), BF16)],
        ),
        out_shape=[
            jax.ShapeDtypeStruct((groups * rows, width), BF16),
            jax.ShapeDtypeStruct((groups * 3 * HD, width), BF16),
            jax.ShapeDtypeStruct((groups, 8, width), F32),
            jax.ShapeDtypeStruct((groups, 8, rows), F32),
        ],
        compiler_params=params("arbitrary"),
        name="prepare",
    )(place, *weights)


def trade(array, axis, mask):
    size = lax.axis_size(axis)
    return lax.ppermute(array, axis, [(i, i ^ mask) for i in range(size)])


def along(block):
    return jnp.stack([block] + [trade(block, "tensor", mask) for mask in (1, 2, 3)])


def across(block):
    return [block] + [trade(block, "dp", mask) for mask in (2, 4, 6)]


def both_cores(blocks):
    return [item for block in blocks for item in (block, trade(block, "dp", 1))]


def tie(array, after):
    return lax.optimization_barrier((array, after))[0]


def gather_both(early, late):
    early = along(early)
    late = along(tie(late, early))
    early = across(early)
    ahead = late
    late = across(tie(late, early))
    early = both_cores([tie(item, ahead) for item in early])
    return early, late


def reduce_cores(kept, away):
    return kept.astype(F32) + trade(away, "dp", 1).astype(F32)


def exchange_across(pieces):
    return [pieces[0]] + [trade(pieces[k], "dp", 2 * k) for k in (1, 2, 3)]


def add_up(items):
    return sum(item.astype(F32) for item in items)


def body(
    block_input, cotangent, heads_weight, heads_bias, merge_weight, merge_bias, up_weight, up_bias,
    down_weight, down_bias, first_gain, first_shift, second_gain, second_shift,
):
    chunk = heads_weight.shape[0]
    owners = lax.axis_size("dp")
    groups = lax.axis_size("tensor")
    width = block_input.shape[1]
    spot = lax.axis_index("tensor")
    odd, pair = spot % 2, spot // 2
    total = block_input.shape[0] // SEQ
    count = total // 2
    fast = owners == 8 and groups == 4
    if fast:
        me = lax.axis_index("dp")
        facts = [odd * count, pair, spot, me // 2, me % 2]
    else:
        facts = [odd * count, pair, spot] + [jnp.zeros_like(spot)] * 2
    place = jnp.stack(facts).astype(jnp.int32)

    bias_part = heads_bias.shape[0]
    vectors = jnp.stack(
        [
            jnp.pad(heads_bias, (0, chunk - bias_part)), up_bias, merge_bias, down_bias,
            first_gain, first_shift, second_gain, second_shift,
        ],
        axis=1,
    )
    early = jnp.concatenate(
        [heads_weight, merge_weight.T, jnp.pad(vectors, ((0, 0), (0, 120)))], axis=1
    )
    late = jnp.concatenate([up_weight, down_weight.T], axis=1)
    if fast:
        early, late = gather_both(early, late)
    else:
        early, late = (
            lax.all_gather(item, ("tensor", "dp"), axis=0, tiled=True).reshape(groups, width, -1)
            for item in (early, late)
        )
        early, late = ([item[spot ^ jnp.arange(groups)]] for item in (early, late))
    rows = 9 * HD
    wt, merge, vecs, hbias = prepare(place, early, bias_part)
    if not fast:
        hbias = vecs[:, 0].reshape(groups, owners, chunk)[:, :, :bias_part]
        hbias = jnp.broadcast_to(hbias.reshape(groups, 1, rows), (groups, 8, rows))
    ff = up_weight.shape[1]
    cosine, sine = rotary_tables()
    swap = [(i, i ^ 1) for i in range(groups)]
    def shifted(i):
        return place.at[0].add(i)

    def attend(i, number, earlier, after):
        return attention(
            tie(shifted(i), after), block_input, cotangent, wt, merge, hbias, vecs, cosine, sine,
            number, len(early), earlier,
        )

    def advance(i, source, at, done, after):
        result = feed(
            tie(shifted(i), after), block_input, cotangent, vecs, *source[:2], at, late, done[2:]
        )
        return result, trade(result[0], "tensor", 1)

    lead = count - 1
    first = attend(0, lead, [], ())
    if fast:
        late = both_cores(tie(late, first[0]))
    second = attend(lead, 1, first[4:], late[0])
    done, others, totals = [], [], []
    wait = second[2]
    for i in range(count):
        source, at = (first, i) if i < lead else (second, 0)
        done, other = advance(i, source, at, done, wait)
        others.append((done[0], other))
        totals.append(done[1])
        if i == 0 and fast:
            heads_part = reduce_cores(*second[4:]).astype(BF16)
            wait = heads_part
        if i == 1:
            wait = others[0]
            if fast:
                heads_items = exchange_across(heads_part)
                wait = wait, heads_items
    if fast:
        heads_cols = add_up(tie(heads_items, done[1])).astype(BF16)
    else:
        heads_cols = lax.psum_scatter(second[4][0], "dp", scatter_dimension=0, tiled=True)

    rows_a = first[2].sum(0) + second[2].sum(0)
    hb = (first[3].sum(0) + second[3].sum(0))[0]
    rows_f = sum(totals)
    hb = jnp.pad(hb.reshape(2, owners, bias_part), ((0, 0), (0, 0), (0, chunk - bias_part)))
    small = jnp.concatenate(
        [
            rows_a[0:2], rows_f[0:2], rows_a[2:3], rows_f[2:4], hb.reshape(2, width),
            jnp.zeros((3, width), F32),
        ],
        axis=0,
    )
    if fast:
        kept, away = done[2:]
        kept = reduce_cores(kept, away).astype(BF16)
        small = (small + trade(small, "dp", 1)).reshape(-1, 4 * ff)
        tail = small.shape[0]
        small = jnp.pad(small, ((0, 8 - tail), (0, 0))).astype(BF16)
        kept = tie(kept, others[-2][1])
        ready = kept
        feed_cols = add_up(exchange_across([jnp.concatenate([item, small]) for item in kept]))
        small = feed_cols[chunk : chunk + tail].reshape(-1, width)
        small = lax.dynamic_slice(small, (0, me * chunk), (small.shape[0], chunk))
        feed_cols = feed_cols[:chunk].astype(BF16)
    else:
        ready = done[1]
        feed_cols = lax.psum_scatter(done[2][0], "dp", scatter_dimension=0, tiled=True)
        small = lax.psum_scatter(small, "dp", scatter_dimension=1, tiled=True)

    def settle(mine, other):
        return mine.astype(F32) + trade(other, "tensor", 1).astype(F32)

    small = small + trade(
        jnp.concatenate([small[:5], small[6:7], small[5:6], small[7:]], axis=0), "tensor", 1
    )
    feed_sum = settle(
        *(
            jnp.concatenate([feed_cols[:, k : k + ff], feed_cols[:, k + 2 * ff : k + 3 * ff]], axis=1)
            for k in (0, ff)
        )
    )
    wide = 2 * rows
    heads_cols = jnp.concatenate(
        [
            heads_cols[:, :rows], heads_cols[:, wide : wide + 3 * HD],
            heads_cols[:, rows:wide], heads_cols[:, wide + 3 * HD :],
        ],
        axis=1,
    )
    heads_cols = tie(heads_cols, ready)
    others[-1] = others[-1][0], tie(others[-1][1], ready)
    half = rows + 3 * HD
    left, right = heads_cols[:, :half], heads_cols[:, half:]
    heads_sum = settle(jnp.where(odd == 0, left, right), jnp.where(odd == 0, right, left))

    layer_output = tie(jnp.zeros(block_input.shape, BF16), done[1])
    input_grad = tie(jnp.zeros(block_input.shape, F32), ready)
    for i, both in enumerate(others):
        for item, base in zip(both, (odd, 1 - odd)):
            at = (base * count + i) * SEQ
            layer_output = lax.dynamic_update_slice(layer_output, item[0], (at, 0))
            given = lax.dynamic_slice(cotangent, (at, 0), (SEQ, width))
            input_grad = lax.dynamic_update_slice(
                input_grad, item[1].astype(F32) + given.astype(F32), (at, 0)
            )
    return (
        layer_output,
        input_grad,
        heads_sum[:, :rows],
        jnp.where(odd == 0, small[7], small[8])[:bias_part],
        heads_sum[:, rows:].T,
        small[4],
        feed_sum[:, :ff],
        small[5],
        feed_sum[:, ff:].T,
        small[4],
        small[0],
        small[1],
        small[2],
        small[3],
    )


def solution(mesh):
    placed = (
        P("dp", None),
        P("dp", None),
        P("dp", "tensor"),
        P(("tensor", "dp")),
        P("tensor", "dp"),
        P("dp"),
        P("dp", "tensor"),
        P(("tensor", "dp")),
        P("tensor", "dp"),
        P("dp"),
        P("dp"),
        P("dp"),
        P("dp"),
        P("dp"),
    )
    return jax.shard_map(
        body,
        mesh=mesh,
        in_specs=placed,
        out_specs=placed,
        check_vma=False,
    )
```

```python
import functools
import math

import jax
import jax.numpy as jnp
import numpy as np
from jax import lax
from jax.experimental import pallas as pl
from jax.experimental.pallas import tpu as pltpu
from jax.sharding import PartitionSpec as P

HD = 64
ROT = 16
SEQ = 512
EPS = 1e-05
VMEM = 60 * 1024 * 1024
F32 = jnp.float32
BF16 = jnp.bfloat16


def dot(left, right, left_dim, right_dim):
    return lax.dot_general(
        left, right, (((left_dim,), (right_dim,)), ((), ())), preferred_element_type=F32
    )


def normalise(values):
    average = jnp.mean(values, axis=-1, keepdims=True)
    centred = values - average
    spread = jnp.mean(centred * centred, axis=-1, keepdims=True)
    scale = lax.rsqrt(spread + EPS)
    return centred * scale, scale


def norm_back(d, hat, scale, gain):
    dg = d * gain
    first = jnp.mean(dg, axis=-1, keepdims=True)
    second = jnp.mean(dg * hat, axis=-1, keepdims=True)
    return (dg - first - hat * second) * scale


def rotary_tables():
    half = ROT // 2
    rates = 10000.0 ** (-(2.0 * np.arange(half)) / ROT)
    angles = rates[:, None] * np.arange(SEQ)[None, :]
    return np.cos(angles).astype(np.float32), np.sin(angles).astype(np.float32)


def rotate(values, cosine, sine):
    half = ROT // 2
    first, second = values[:half], values[half:ROT]
    return jnp.concatenate(
        [first * cosine - second * sine, second * cosine + first * sine, values[ROT:]], axis=0
    )


def piece_rows(place, index, pieces, chunk):
    if pieces == 1:
        return pl.ds(0, chunk)
    across, core = index // 2, index % 2
    owner = (across ^ place[3]) * 2 + (core ^ place[4])
    return pl.ds(pl.multiple_of(owner * chunk, 16), chunk)


def assemble(place, refs, target):
    chunk = refs[0].shape[1]
    for index, ref in enumerate(refs):
        target[piece_rows(place, index, len(refs), chunk), :] = ref[0]


def share_out(place, source, held, made, pieces):
    for index in range(pieces):
        value = source[piece_rows(place, index, pieces, made[0].shape[1]), :]
        if held:
            value = value + held[index % 2][index // 2].astype(F32)
        made[index % 2][index // 2] = value.astype(BF16)


def prepare_kernel(place, *refs, part):
    *pieces, wt_ref, merge_ref, vec_ref, bias_ref, full = refs
    assemble(place, pieces, full)
    rows = wt_ref.shape[0]
    end = rows + merge_ref.shape[0]
    wt_ref[...] = full[:, :rows].T
    merge_ref[...] = full[:, rows:end].T
    vectors = full[:, end:].astype(F32)
    vec_ref[0] = vectors.T[: vec_ref.shape[1]]
    chunk = pieces[0].shape[1]
    if len(pieces) > 1:
        packed = [vectors[at : at + part] for at in range(0, vectors.shape[0], chunk)]
        bias_ref[0] = jnp.concatenate(packed, axis=0).T[: bias_ref.shape[1]]
    else:
        bias_ref[...] = jnp.zeros_like(bias_ref)


def attention_kernel(
    place, x_ref, g_ref, wt_ref, merge_ref, bias_ref, vec_ref, cos_ref, sin_ref, *refs,
    pieces, earlier,
):
    sides = min(pieces, 2)
    held, refs = refs[: sides * earlier], refs[sides * earlier :]
    out_ref, din_ref, rows_ref, hb_ref = refs[:4]
    made = refs[4 : 4 + sides]
    datt, att, dmix, acc = refs[4 + sides :]
    groups = wt_ref.shape[0] // (9 * HD)
    rows = 9 * HD
    half = SEQ // 2
    scaling = 1.0 / math.sqrt(HD)
    x = x_ref[...].astype(F32)
    g = g_ref[...]
    gain, shift = vec_ref[0, 4:5, :], vec_ref[0, 5:6, :]
    hat, scale = normalise(x)
    n1 = (hat * gain + shift).astype(BF16)
    datt[...] = dot(merge_ref[...], g, 1, 1).astype(BF16)
    cosine, sine = cos_ref[...], sin_ref[...]
    below = lax.broadcasted_iota(jnp.int32, (half, half), 0) <= lax.broadcasted_iota(
        jnp.int32, (half, half), 1
    )

    def raise_columns(scores):
        raised = jnp.exp(scores - jnp.max(scores, axis=0, keepdims=True))
        return raised, jnp.sum(raised, axis=0, keepdims=True)

    def group(index, carry):
        base = pl.multiple_of(index * rows, rows)
        part = dot(wt_ref[pl.ds(base, rows), :], n1, 1, 1)
        part = part + bias_ref[index].T[:, 0:1]
        for head in range(3):
            at = head * 3 * HD
            query = (rotate(part[at : at + HD], cosine, sine) * scaling).astype(BF16)
            keys = rotate(part[at + HD : at + 2 * HD], cosine, sine).astype(BF16)
            values = part[at + 2 * HD : at + 3 * HD].astype(BF16)
            spot = pl.multiple_of(index * 3 * HD + head * HD, HD)
            given = datt[pl.ds(spot, HD), :].astype(F32)
            keys_t, values_t = keys.T, values.T
            s0 = dot(keys_t[:half], query[:, :half], 1, 0)
            s1a = dot(keys_t[:half], query[:, half:], 1, 0)
            s1b = dot(keys_t[half:], query[:, half:], 1, 0)
            e0, l0 = raise_columns(jnp.where(below, s0, -1e30))
            e1, l1 = raise_columns(
                jnp.concatenate([s1a, jnp.where(below, s1b, -1e30)], axis=0)
            )
            w0, w1 = e0.astype(BF16), e1.astype(BF16)
            share = 1.0 / jnp.concatenate([l0, l1], axis=1)
            attended = share * jnp.concatenate(
                [dot(values[:, :half], w0, 1, 0), dot(values, w1, 1, 0)], axis=1
            )
            att[pl.ds(spot, HD), :] = attended.astype(BF16)
            given = (given * share).astype(BF16)
            level = jnp.sum(given.astype(F32) * attended, axis=0, keepdims=True)
            q0 = dot(values_t[:half], given[:, :half], 1, 0)
            q1 = dot(values_t, given[:, half:], 1, 0)
            d0 = (e0 * (q0 - level[:, :half])).astype(BF16)
            d1 = (e1 * (q1 - level[:, half:])).astype(BF16)
            d_values = dot(given[:, half:], w1, 1, 1)
            d_values = jnp.concatenate(
                [d_values[:, :half] + dot(given[:, :half], w0, 1, 1), d_values[:, half:]], axis=1
            )
            d_keys = dot(query[:, half:], d1, 1, 1)
            d_keys = jnp.concatenate(
                [d_keys[:, :half] + dot(query[:, :half], d0, 1, 1), d_keys[:, half:]], axis=1
            )
            d_query = jnp.concatenate(
                [dot(keys[:, :half], d0, 1, 0), dot(keys, d1, 1, 0)], axis=1
            ) * scaling
            to = pl.multiple_of(base + at, HD)
            dmix[pl.ds(to, HD), :] = rotate(d_query, cosine, -sine).astype(BF16)
            dmix[pl.ds(to + HD, HD), :] = rotate(d_keys, cosine, -sine).astype(BF16)
            dmix[pl.ds(to + 2 * HD, HD), :] = d_values.astype(BF16)
        return carry

    lax.fori_loop(0, groups, group, 0)
    out_ref[...] = dot(att[...].T, merge_ref[...], 1, 0).astype(BF16)
    d_first = dot(dmix[...].T, wt_ref[...], 1, 0)
    pair = place[1]
    mine = dmix[pl.ds(pl.multiple_of(pair * 2 * rows, 2 * rows), 2 * rows), :]
    mine_att = att[pl.ds(pl.multiple_of(pair * 6 * HD, 6 * HD), 6 * HD), :]
    hb_ref[0] = dot(jnp.ones((8, SEQ), BF16), mine, 1, 1)
    step = pl.program_id(0)

    @pl.when(step == 0)
    def _():
        acc[...] = jnp.zeros_like(acc)

    acc[:, : 2 * rows] += dot(n1.T, mine, 1, 1)
    acc[:, 2 * rows :] += dot(g.T, mine_att, 1, 1)

    @pl.when(step == pl.num_programs(0) - 1)
    def _():
        share_out(place, acc, held, made, pieces)

    rows_ref[0] = jnp.concatenate(
        [
            jnp.sum(d_first * hat, axis=0, keepdims=True),
            jnp.sum(d_first, axis=0, keepdims=True),
            jnp.sum(g.astype(F32), axis=0, keepdims=True),
            jnp.zeros((5, x.shape[1]), F32),
        ],
        axis=0,
    )
    din_ref[...] = norm_back(d_first, hat, scale, gain).astype(BF16)


def gelu_parts(h):
    near = 0.7071067811865476 * jnp.abs(h)
    below = 1.0 + 0.3275911 * near
    t = pl.reciprocal(below, approx=True)
    t = t * (2.0 - below * t)
    bell = jnp.exp(-0.5 * h * h)
    series = 1.061405429 * t - 1.453152027
    series = series * t + 1.421413741
    series = series * t - 0.284496736
    series = series * t + 0.254829592
    tail = 0.5 * series * t * bell
    phi = jnp.where(h >= 0, 1.0 - tail, tail)
    return h * phi, phi + h * bell * 0.3989422804014327


def feed_kernel(
    place, x_ref, g_ref, bias_ref, vec_ref, aout_ref, din_ref, *refs, pieces, earlier, at, phases,
):
    opens, closes = phases[0] == 0, phases[-1] == 1
    weights, refs = refs[:pieces], refs[pieces:]
    sides = min(pieces, 2)
    held, refs = refs[: sides * earlier], refs[sides * earlier :]
    begun, refs = refs[: 1 - opens], refs[1 - opens :]
    rows_ref, main_ref = refs[:2]
    made, refs = refs[2 : 2 + sides * opens], refs[2 + sides * opens :]
    n2, turned, n2t, gt, up, down, extra, part_s, acc, load_sem, held_sem, extra_sem, out_sem = refs
    chunk = weights[0].shape[1]
    ff = up.shape[2] // 2
    loads = {step: [] for step in phases}
    for step in phases:
        for index, ref in enumerate(weights):
            rows = piece_rows(place, index, pieces, chunk)
            for side in range(2):
                spot = slice(side * ff, (side + 1) * ff)
                for kind, target in enumerate((up, down)):
                    copy = pltpu.make_async_copy(
                        ref.at[2 * step + side, :, kind * ff : (kind + 1) * ff],
                        target.at[step, rows, spot],
                        load_sem.at[step, index, side, kind],
                    )
                    copy.start()
                    loads[step].append(copy)
    fetched = [
        pltpu.make_async_copy(held[k], part_s.at[k], held_sem.at[k])
        for k in range(sides * earlier)
    ]
    fetched += [
        pltpu.make_async_copy(ref.at[at * SEQ : (at + 1) * SEQ], extra.at[k], extra_sem.at[k])
        for k, ref in enumerate((aout_ref, din_ref))
    ]
    for copy in fetched:
        copy.start()

    gain, shift = vec_ref[0, 6:7, :], vec_ref[0, 7:8, :]
    hat, scale = normalise(x_ref[...].astype(F32))
    n2[...] = (hat * gain + shift).astype(BF16)
    if opens:
        for source, target in ((n2, n2t), (g_ref, gt)):
            turned[...] = source[...].T
            for index in range(pieces):
                rows = piece_rows(place, index, pieces, chunk)
                target[index * chunk : (index + 1) * chunk, :] = turned[rows, :]
    rows_ref[...] = jnp.zeros_like(rows_ref)
    stores = [pltpu.make_async_copy(part_s.at[k], made[k], out_sem.at[k]) for k in range(len(made))]

    def keep_gradients(activated, d_hidden):
        for copy in fetched[: sides * earlier]:
            copy.wait()
        for left, right, spot in ((n2t, d_hidden, 0), (gt, activated, 2 * ff)):
            fresh = dot(left[...], right, 1, 0)
            for index in range(pieces):
                value = fresh[index * chunk : (index + 1) * chunk, :]
                spots = (index % 2, index // 2, slice(None), slice(spot, spot + 2 * ff))
                if earlier:
                    value = value + part_s[spots].astype(F32)
                part_s[spots] = value.astype(BF16)
        for copy in stores:
            copy.start()
        sums = jnp.sum(d_hidden.astype(F32), axis=0, keepdims=True)
        rows_ref[2:3, :] = sums[:, :ff]
        rows_ref[3:4, :] = sums[:, ff:]

    def pair_of_groups(step, carry):
        for index, ref in enumerate(weights):
            for side in range(2):
                for kind, target in enumerate((up, down)):
                    pltpu.make_async_copy(
                        ref.at[side, :, :ff],
                        target.at[step, pl.ds(0, chunk), :ff],
                        load_sem.at[step, index, side, kind],
                    ).wait()
        which, parity = place[1] ^ step, place[2] % 2
        bias = jnp.concatenate(
            [bias_ref[2 * which + parity, 1:2, :], bias_ref[2 * which + 1 - parity, 1:2, :]],
            axis=1,
        )
        activated, slope = gelu_parts(dot(n2[...], up[step], 1, 0) + bias)
        activated = activated.astype(BF16)
        d_hidden = (dot(g_ref[...], down[step], 1, 0) * slope).astype(BF16)
        acc[0] += dot(activated, down[step], 1, 1)
        acc[1] += dot(d_hidden, up[step], 1, 1)
        if opens:
            pl.when(step == 0)(functools.partial(keep_gradients, activated, d_hidden))
        return carry

    acc[...] = begun[0][...] if begun else jnp.zeros_like(acc)
    lax.fori_loop(phases[0], phases[-1] + 1, pair_of_groups, 0)
    for copy in fetched[sides * earlier :]:
        copy.wait()
    if closes:
        d_second = acc[1]
        base = x_ref[...].astype(F32) + extra[0].astype(F32)
        base = base + vec_ref[0, 2:3, :] + vec_ref[0, 3:4, :]
        main_ref[0] = (acc[0] + base).astype(BF16)
        total = norm_back(d_second, hat, scale, gain) + extra[1].astype(F32)
        main_ref[1] = total.astype(BF16)
        rows_ref[0:1, :] = jnp.sum(d_second * hat, axis=0, keepdims=True)
        rows_ref[1:2, :] = jnp.sum(d_second, axis=0, keepdims=True)
    else:
        main_ref[...] = acc[...]
    for copy in stores:
        copy.wait()


def params(*kinds):
    return pltpu.CompilerParams(dimension_semantics=kinds, vmem_limit_bytes=VMEM)


def whole(shape):
    zeros = (0,) * len(shape)
    return pl.BlockSpec(shape, lambda *_: zeros)


def attention(place, x, g, wt, merge, bias, vecs, cosine, sine, count, pieces, earlier):
    width = x.shape[1]
    rows = 9 * HD
    columns = 2 * rows + 6 * HD
    given = pl.BlockSpec((SEQ, width), lambda i, place: (place[0] + i, 0))
    taken = pl.BlockSpec((SEQ, width), lambda i, place: (i, 0))

    def per(a, b):
        return pl.BlockSpec((1, a, b), lambda i, place: (i, 0, 0))

    sides = min(pieces, 2)
    part = (pieces // sides, width // pieces, columns)
    return pl.pallas_call(
        functools.partial(attention_kernel, pieces=pieces, earlier=1 if earlier else 0),
        grid_spec=pltpu.PrefetchScalarGridSpec(
            num_scalar_prefetch=1,
            grid=(count,),
            in_specs=[
                given, given, whole(wt.shape), whole(merge.shape), whole(bias.shape),
                whole((1, 8, width)), whole(cosine.shape), whole(sine.shape),
            ]
            + [whole(part)] * len(earlier),
            out_specs=[taken, taken, per(8, width), per(8, 2 * rows)]
            + [whole(part)] * sides,
            scratch_shapes=[
                pltpu.VMEM((width, SEQ), BF16),
                pltpu.VMEM((width, SEQ), BF16),
                pltpu.VMEM((wt.shape[0], SEQ), BF16),
                pltpu.VMEM((width, columns), F32),
            ],
        ),
        out_shape=[
            jax.ShapeDtypeStruct((count * SEQ, width), BF16),
            jax.ShapeDtypeStruct((count * SEQ, width), BF16),
            jax.ShapeDtypeStruct((count, 8, width), F32),
            jax.ShapeDtypeStruct((count, 8, 2 * rows), F32),
        ]
        + [jax.ShapeDtypeStruct(part, BF16)] * sides,
        compiler_params=params("arbitrary"),
        name="attention",
        cost_estimate=pl.CostEstimate(
            flops=count * 16_000_000_000, bytes_accessed=count * 12_000_000, transcendentals=0
        ),
    )(place, x, g, wt, merge, bias, vecs, cosine, sine, *earlier)


def feed(place, x, g, vecs, aout, din, at, weights, earlier, phases=(0, 1), begun=()):
    width = x.shape[1]
    groups, chunk, columns = weights[0].shape
    ff = columns // 2
    pieces = len(weights)
    sides = min(pieces, 2)
    given = pl.BlockSpec((SEQ, width), lambda s, place: (place[0], 0))
    part = (pieces // sides, chunk, 2 * columns)
    anywhere = pl.BlockSpec(memory_space=pl.ANY)
    first = 7 + pieces
    kept = 0 if begun else sides
    return pl.pallas_call(
        functools.partial(
            feed_kernel, pieces=pieces, earlier=1 if earlier else 0, at=at, phases=phases
        ),
        grid_spec=pltpu.PrefetchScalarGridSpec(
            num_scalar_prefetch=1,
            grid=(1,),
            in_specs=[given, given, whole(vecs.shape), whole((1, 8, width))]
            + [anywhere] * (2 + pieces + len(earlier))
            + [whole((2, SEQ, width))] * len(begun),
            out_specs=[whole((8, width)), whole((2, SEQ, width))] + [anywhere] * kept,
            scratch_shapes=[
                pltpu.VMEM((SEQ, width), BF16),
                pltpu.VMEM((width, SEQ), BF16),
                pltpu.VMEM((width, SEQ), BF16),
                pltpu.VMEM((width, SEQ), BF16),
                pltpu.VMEM((2, width, columns), BF16),
                pltpu.VMEM((2, width, columns), BF16),
                pltpu.VMEM((2, SEQ, width), BF16),
                pltpu.VMEM((sides, *part), BF16),
                pltpu.VMEM((2, SEQ, width), F32),
                pltpu.SemaphoreType.DMA((2, pieces, 2, 2)),
                pltpu.SemaphoreType.DMA((2,)),
                pltpu.SemaphoreType.DMA((2,)),
                pltpu.SemaphoreType.DMA((2,)),
            ],
        ),
        out_shape=[
            jax.ShapeDtypeStruct((8, width), F32),
            jax.ShapeDtypeStruct((2, SEQ, width), BF16 if phases[-1] == 1 else F32),
        ]
        + [jax.ShapeDtypeStruct(part, BF16)] * kept,
        input_output_aliases={first + k: 2 + k for k in range(len(earlier))},
        compiler_params=params("arbitrary"),
        name="feed",
        cost_estimate=pl.CostEstimate(
            flops=8_000_000_000 * len(phases), bytes_accessed=9_000_000, transcendentals=0
        ),
    )(place, x, g, vecs, vecs, aout, din, *weights, *earlier, *begun)


def prepare(place, weights, part):
    groups, chunk, columns = weights[0].shape
    pieces = len(weights)
    width = pieces * chunk
    rows = 9 * HD
    return pl.pallas_call(
        functools.partial(prepare_kernel, part=part),
        grid_spec=pltpu.PrefetchScalarGridSpec(
            num_scalar_prefetch=1,
            grid=(groups,),
            in_specs=[
                pl.BlockSpec((1, chunk, columns), lambda t, place: (t ^ place[2], 0, 0))
            ]
            * pieces,
            out_specs=[
                pl.BlockSpec((rows, width), lambda t, place: (t, 0)),
                pl.BlockSpec((3 * HD, width), lambda t, place: (t, 0)),
                pl.BlockSpec((1, 8, width), lambda t, place: (t, 0, 0)),
                pl.BlockSpec((1, 8, rows), lambda t, place: (t, 0, 0)),
            ],
            scratch_shapes=[pltpu.VMEM((width, columns), BF16)],
        ),
        out_shape=[
            jax.ShapeDtypeStruct((groups * rows, width), BF16),
            jax.ShapeDtypeStruct((groups * 3 * HD, width), BF16),
            jax.ShapeDtypeStruct((groups, 8, width), F32),
            jax.ShapeDtypeStruct((groups, 8, rows), F32),
        ],
        compiler_params=params("arbitrary"),
        name="prepare",
    )(place, *weights)


def trade(array, axis, mask):
    size = lax.axis_size(axis)
    return lax.ppermute(array, axis, [(i, i ^ mask) for i in range(size)])


def along(block):
    return jnp.stack([block] + [trade(block, "tensor", mask) for mask in (1, 2, 3)])


def across(block):
    return [block] + [trade(block, "dp", mask) for mask in (2, 4, 6)]


def both_cores(blocks):
    return [item for block in blocks for item in (block, trade(block, "dp", 1))]


def tie(array, after):
    return lax.optimization_barrier((array, after))[0]


def gather_both(early, late):
    early = along(early)
    late = along(tie(late, early))
    early = across(early)
    ahead = late
    late = across(tie(late, early))
    early = both_cores([tie(item, ahead) for item in early])
    return early, late


def reduce_cores(kept, away):
    return kept.astype(F32) + trade(away, "dp", 1).astype(F32)


def exchange_across(pieces):
    return [pieces[0]] + [trade(pieces[k], "dp", 2 * k) for k in (1, 2, 3)]


def add_up(items):
    return sum(item.astype(F32) for item in items)


def body(
    block_input, cotangent, heads_weight, heads_bias, merge_weight, merge_bias, up_weight, up_bias,
    down_weight, down_bias, first_gain, first_shift, second_gain, second_shift,
):
    chunk = heads_weight.shape[0]
    owners = lax.axis_size("dp")
    groups = lax.axis_size("tensor")
    width = block_input.shape[1]
    spot = lax.axis_index("tensor")
    odd, pair = spot % 2, spot // 2
    total = block_input.shape[0] // SEQ
    count = total // 2
    fast = owners == 8 and groups == 4
    if fast:
        me = lax.axis_index("dp")
        facts = [odd * count, pair, spot, me // 2, me % 2]
    else:
        facts = [odd * count, pair, spot] + [jnp.zeros_like(spot)] * 2
    place = jnp.stack(facts).astype(jnp.int32)

    bias_part = heads_bias.shape[0]
    vectors = jnp.stack(
        [
            jnp.pad(heads_bias, (0, chunk - bias_part)), up_bias, merge_bias, down_bias,
            first_gain, first_shift, second_gain, second_shift,
        ],
        axis=1,
    )
    early = jnp.concatenate(
        [heads_weight, merge_weight.T, jnp.pad(vectors, ((0, 0), (0, 120)))], axis=1
    )
    late = jnp.concatenate([up_weight, down_weight.T], axis=1)
    if fast:
        early, late = gather_both(early, late)
    else:
        early, late = (
            lax.all_gather(item, ("tensor", "dp"), axis=0, tiled=True).reshape(groups, width, -1)
            for item in (early, late)
        )
        early, late = ([item[spot ^ jnp.arange(groups)]] for item in (early, late))
    rows = 9 * HD
    wt, merge, vecs, hbias = prepare(place, early, bias_part)
    if not fast:
        hbias = vecs[:, 0].reshape(groups, owners, chunk)[:, :, :bias_part]
        hbias = jnp.broadcast_to(hbias.reshape(groups, 1, rows), (groups, 8, rows))
    ff = up_weight.shape[1]
    cosine, sine = rotary_tables()
    swap = [(i, i ^ 1) for i in range(groups)]
    def shifted(i):
        return place.at[0].add(i)

    def attend(i, number, earlier, after):
        return attention(
            tie(shifted(i), after), block_input, cotangent, wt, merge, hbias, vecs, cosine, sine,
            number, len(early), earlier,
        )

    def advance(i, source, at, done, after):
        common = tie(shifted(i), after), block_input, cotangent, vecs, *source[:2], at, late
        sums, rows16, *grads = feed(*common, done[2:])
        return [rows16, sums, *grads], trade(rows16, "tensor", 1)

    lead = count - 1
    first = attend(0, lead, [], ())
    if fast:
        late = both_cores(tie(late, first[0]))
    second = attend(lead, 1, first[4:], late[0])
    done, others, totals = [], [], []
    wait = second[2]
    for i in range(count):
        source, at = (first, i) if i < lead else (second, 0)
        done, other = advance(i, source, at, done, wait)
        others.append((done[0], other))
        totals.append(done[1])
        if i == 0 and fast:
            heads_part = reduce_cores(*second[4:]).astype(BF16)
            wait = heads_part
        if i == 1:
            wait = others[0]
            if fast:
                heads_items = exchange_across(heads_part)
                wait = wait, heads_items
    if fast:
        heads_cols = add_up(tie(heads_items, done[1])).astype(BF16)
    else:
        heads_cols = lax.psum_scatter(second[4][0], "dp", scatter_dimension=0, tiled=True)

    rows_a = first[2].sum(0) + second[2].sum(0)
    hb = (first[3].sum(0) + second[3].sum(0))[0]
    rows_f = sum(totals)
    hb = jnp.pad(hb.reshape(2, owners, bias_part), ((0, 0), (0, 0), (0, chunk - bias_part)))
    small = jnp.concatenate(
        [
            rows_a[0:2], rows_f[0:2], rows_a[2:3], rows_f[2:4], hb.reshape(2, width),
            jnp.zeros((3, width), F32),
        ],
        axis=0,
    )
    if fast:
        kept, away = done[2:]
        kept = reduce_cores(kept, away).astype(BF16)
        small = (small + trade(small, "dp", 1)).reshape(-1, 4 * ff)
        tail = small.shape[0]
        small = jnp.pad(small, ((0, 8 - tail), (0, 0))).astype(BF16)
        kept = tie(kept, others[-2][1])
        ready = kept
        feed_cols = add_up(exchange_across([jnp.concatenate([item, small]) for item in kept]))
        small = feed_cols[chunk : chunk + tail].reshape(-1, width)
        small = lax.dynamic_slice(small, (0, me * chunk), (small.shape[0], chunk))
        feed_cols = feed_cols[:chunk].astype(BF16)
    else:
        ready = done[1]
        feed_cols = lax.psum_scatter(done[2][0], "dp", scatter_dimension=0, tiled=True)
        small = lax.psum_scatter(small, "dp", scatter_dimension=1, tiled=True)

    def settle(mine, other):
        return mine.astype(F32) + trade(other, "tensor", 1).astype(F32)

    small = small + trade(
        jnp.concatenate([small[:5], small[6:7], small[5:6], small[7:]], axis=0), "tensor", 1
    )
    feed_sum = settle(
        *(
            jnp.concatenate([feed_cols[:, k : k + ff], feed_cols[:, k + 2 * ff : k + 3 * ff]], axis=1)
            for k in (0, ff)
        )
    )
    wide = 2 * rows
    heads_cols = jnp.concatenate(
        [
            heads_cols[:, :rows], heads_cols[:, wide : wide + 3 * HD],
            heads_cols[:, rows:wide], heads_cols[:, wide + 3 * HD :],
        ],
        axis=1,
    )
    heads_cols = tie(heads_cols, ready)
    others[-1] = others[-1][0], tie(others[-1][1], ready)
    half = rows + 3 * HD
    left, right = heads_cols[:, :half], heads_cols[:, half:]
    heads_sum = settle(jnp.where(odd == 0, left, right), jnp.where(odd == 0, right, left))

    layer_output = tie(jnp.zeros(block_input.shape, BF16), done[1])
    input_grad = tie(jnp.zeros(block_input.shape, F32), ready)
    for i, both in enumerate(others):
        for item, base in zip(both, (odd, 1 - odd)):
            at = (base * count + i) * SEQ
            layer_output = lax.dynamic_update_slice(layer_output, item[0], (at, 0))
            given = lax.dynamic_slice(cotangent, (at, 0), (SEQ, width))
            input_grad = lax.dynamic_update_slice(
                input_grad, item[1].astype(F32) + given.astype(F32), (at, 0)
            )
    return (
        layer_output,
        input_grad,
        heads_sum[:, :rows],
        jnp.where(odd == 0, small[7], small[8])[:bias_part],
        heads_sum[:, rows:].T,
        small[4],
        feed_sum[:, :ff],
        small[5],
        feed_sum[:, ff:].T,
        small[4],
        small[0],
        small[1],
        small[2],
        small[3],
    )


def solution(mesh):
    placed = (
        P("dp", None),
        P("dp", None),
        P("dp", "tensor"),
        P(("tensor", "dp")),
        P("tensor", "dp"),
        P("dp"),
        P("dp", "tensor"),
        P(("tensor", "dp")),
        P("tensor", "dp"),
        P("dp"),
        P("dp"),
        P("dp"),
        P("dp"),
        P("dp"),
    )
    return jax.shard_map(
        body,
        mesh=mesh,
        in_specs=placed,
        out_specs=placed,
        check_vma=False,
    )
```

```python
import functools
import math

import jax
import jax.numpy as jnp
import numpy as np
from jax import lax
from jax.experimental import pallas as pl
from jax.experimental.pallas import tpu as pltpu
from jax.sharding import PartitionSpec as P

HD = 64
ROT = 16
SEQ = 512
EPS = 1e-05
VMEM = 60 * 1024 * 1024
F32 = jnp.float32
BF16 = jnp.bfloat16


def dot(left, right, left_dim, right_dim):
    return lax.dot_general(
        left, right, (((left_dim,), (right_dim,)), ((), ())), preferred_element_type=F32
    )


def normalise(values):
    average = jnp.mean(values, axis=-1, keepdims=True)
    centred = values - average
    spread = jnp.mean(centred * centred, axis=-1, keepdims=True)
    scale = lax.rsqrt(spread + EPS)
    return centred * scale, scale


def norm_back(d, hat, scale, gain):
    dg = d * gain
    first = jnp.mean(dg, axis=-1, keepdims=True)
    second = jnp.mean(dg * hat, axis=-1, keepdims=True)
    return (dg - first - hat * second) * scale


def rotary_tables():
    half = ROT // 2
    rates = 10000.0 ** (-(2.0 * np.arange(half)) / ROT)
    angles = rates[:, None] * np.arange(SEQ)[None, :]
    return np.cos(angles).astype(np.float32), np.sin(angles).astype(np.float32)


def rotate(values, cosine, sine):
    half = ROT // 2
    first, second = values[:half], values[half:ROT]
    return jnp.concatenate(
        [first * cosine - second * sine, second * cosine + first * sine, values[ROT:]], axis=0
    )


def piece_rows(place, index, pieces, chunk):
    if pieces == 1:
        return pl.ds(0, chunk)
    across, core = index // 2, index % 2
    owner = (across ^ place[3]) * 2 + (core ^ place[4])
    return pl.ds(pl.multiple_of(owner * chunk, 16), chunk)


def assemble(place, refs, target):
    chunk = refs[0].shape[1]
    for index, ref in enumerate(refs):
        target[piece_rows(place, index, len(refs), chunk), :] = ref[0]


def share_out(place, source, held, made, pieces):
    for index in range(pieces):
        value = source[piece_rows(place, index, pieces, made[0].shape[1]), :]
        if held:
            value = value + held[index % 2][index // 2].astype(F32)
        made[index % 2][index // 2] = value.astype(BF16)


def prepare_kernel(place, *refs, part):
    *pieces, wt_ref, merge_ref, vec_ref, bias_ref, full = refs
    assemble(place, pieces, full)
    rows = wt_ref.shape[0]
    end = rows + merge_ref.shape[0]
    wt_ref[...] = full[:, :rows].T
    merge_ref[...] = full[:, rows:end].T
    vectors = full[:, end:].astype(F32)
    vec_ref[0] = vectors.T[: vec_ref.shape[1]]
    chunk = pieces[0].shape[1]
    if len(pieces) > 1:
        packed = [vectors[at : at + part] for at in range(0, vectors.shape[0], chunk)]
        bias_ref[0] = jnp.concatenate(packed, axis=0).T[: bias_ref.shape[1]]
    else:
        bias_ref[...] = jnp.zeros_like(bias_ref)


def attention_kernel(
    place, x_ref, g_ref, wt_ref, merge_ref, bias_ref, vec_ref, cos_ref, sin_ref, *refs,
    pieces, earlier,
):
    sides = min(pieces, 2)
    held, refs = refs[: sides * earlier], refs[sides * earlier :]
    out_ref, din_ref, rows_ref, hb_ref = refs[:4]
    made = refs[4 : 4 + sides]
    datt, att, dmix, acc = refs[4 + sides :]
    groups = wt_ref.shape[0] // (9 * HD)
    rows = 9 * HD
    half = SEQ // 2
    scaling = 1.0 / math.sqrt(HD)
    x = x_ref[...].astype(F32)
    g = g_ref[...]
    gain, shift = vec_ref[0, 4:5, :], vec_ref[0, 5:6, :]
    hat, scale = normalise(x)
    n1 = (hat * gain + shift).astype(BF16)
    datt[...] = dot(merge_ref[...], g, 1, 1).astype(BF16)
    cosine, sine = cos_ref[...], sin_ref[...]
    below = lax.broadcasted_iota(jnp.int32, (half, half), 0) <= lax.broadcasted_iota(
        jnp.int32, (half, half), 1
    )

    def raise_columns(scores):
        raised = jnp.exp(scores - jnp.max(scores, axis=0, keepdims=True))
        return raised, jnp.sum(raised, axis=0, keepdims=True)

    def group(index, carry):
        base = pl.multiple_of(index * rows, rows)
        part = dot(wt_ref[pl.ds(base, rows), :], n1, 1, 1)
        part = part + bias_ref[index].T[:, 0:1]
        for head in range(3):
            at = head * 3 * HD
            query = (rotate(part[at : at + HD], cosine, sine) * scaling).astype(BF16)
            keys = rotate(part[at + HD : at + 2 * HD], cosine, sine).astype(BF16)
            values = part[at + 2 * HD : at + 3 * HD].astype(BF16)
            spot = pl.multiple_of(index * 3 * HD + head * HD, HD)
            given = datt[pl.ds(spot, HD), :].astype(F32)
            keys_t, values_t = keys.T, values.T
            s0 = dot(keys_t[:half], query[:, :half], 1, 0)
            s1a = dot(keys_t[:half], query[:, half:], 1, 0)
            s1b = dot(keys_t[half:], query[:, half:], 1, 0)
            e0, l0 = raise_columns(jnp.where(below, s0, -1e30))
            e1, l1 = raise_columns(
                jnp.concatenate([s1a, jnp.where(below, s1b, -1e30)], axis=0)
            )
            w0, w1 = e0.astype(BF16), e1.astype(BF16)
            share = 1.0 / jnp.concatenate([l0, l1], axis=1)
            attended = share * jnp.concatenate(
                [dot(values[:, :half], w0, 1, 0), dot(values, w1, 1, 0)], axis=1
            )
            att[pl.ds(spot, HD), :] = attended.astype(BF16)
            given = (given * share).astype(BF16)
            level = jnp.sum(given.astype(F32) * attended, axis=0, keepdims=True)
            q0 = dot(values_t[:half], given[:, :half], 1, 0)
            q1 = dot(values_t, given[:, half:], 1, 0)
            d0 = (e0 * (q0 - level[:, :half])).astype(BF16)
            d1 = (e1 * (q1 - level[:, half:])).astype(BF16)
            d_values = dot(given[:, half:], w1, 1, 1)
            d_values = jnp.concatenate(
                [d_values[:, :half] + dot(given[:, :half], w0, 1, 1), d_values[:, half:]], axis=1
            )
            d_keys = dot(query[:, half:], d1, 1, 1)
            d_keys = jnp.concatenate(
                [d_keys[:, :half] + dot(query[:, :half], d0, 1, 1), d_keys[:, half:]], axis=1
            )
            d_query = jnp.concatenate(
                [dot(keys[:, :half], d0, 1, 0), dot(keys, d1, 1, 0)], axis=1
            ) * scaling
            to = pl.multiple_of(base + at, HD)
            dmix[pl.ds(to, HD), :] = rotate(d_query, cosine, -sine).astype(BF16)
            dmix[pl.ds(to + HD, HD), :] = rotate(d_keys, cosine, -sine).astype(BF16)
            dmix[pl.ds(to + 2 * HD, HD), :] = d_values.astype(BF16)
        return carry

    lax.fori_loop(0, groups, group, 0)
    out_ref[...] = dot(att[...].T, merge_ref[...], 1, 0).astype(BF16)
    d_first = dot(dmix[...].T, wt_ref[...], 1, 0)
    pair = place[1]
    mine = dmix[pl.ds(pl.multiple_of(pair * 2 * rows, 2 * rows), 2 * rows), :]
    mine_att = att[pl.ds(pl.multiple_of(pair * 6 * HD, 6 * HD), 6 * HD), :]
    hb_ref[0] = dot(jnp.ones((8, SEQ), BF16), mine, 1, 1)
    step = pl.program_id(0)

    @pl.when(step == 0)
    def _():
        acc[...] = jnp.zeros_like(acc)

    acc[:, : 2 * rows] += dot(n1.T, mine, 1, 1)
    acc[:, 2 * rows :] += dot(g.T, mine_att, 1, 1)

    @pl.when(step == pl.num_programs(0) - 1)
    def _():
        share_out(place, acc, held, made, pieces)

    rows_ref[0] = jnp.concatenate(
        [
            jnp.sum(d_first * hat, axis=0, keepdims=True),
            jnp.sum(d_first, axis=0, keepdims=True),
            jnp.sum(g.astype(F32), axis=0, keepdims=True),
            jnp.zeros((5, x.shape[1]), F32),
        ],
        axis=0,
    )
    din_ref[...] = norm_back(d_first, hat, scale, gain).astype(BF16)


def gelu_parts(h):
    near = 0.7071067811865476 * jnp.abs(h)
    below = 1.0 + 0.3275911 * near
    t = pl.reciprocal(below, approx=True)
    t = t * (2.0 - below * t)
    bell = jnp.exp(-0.5 * h * h)
    series = 1.061405429 * t - 1.453152027
    series = series * t + 1.421413741
    series = series * t - 0.284496736
    series = series * t + 0.254829592
    tail = 0.5 * series * t * bell
    phi = jnp.where(h >= 0, 1.0 - tail, tail)
    return h * phi, phi + h * bell * 0.3989422804014327


def feed_kernel(
    place, x_ref, g_ref, bias_ref, vec_ref, aout_ref, din_ref, *refs, pieces, earlier, at, phases,
):
    opens, closes = phases[0] == 0, phases[-1] == 1
    weights, refs = refs[:pieces], refs[pieces:]
    sides = min(pieces, 2)
    held, refs = refs[: sides * earlier], refs[sides * earlier :]
    begun, refs = refs[: 1 - opens], refs[1 - opens :]
    rows_ref, main_ref = refs[:2]
    made, refs = refs[2 : 2 + sides * opens], refs[2 + sides * opens :]
    n2, turned, n2t, gt, up, down, extra, part_s, acc, load_sem, held_sem, extra_sem, out_sem = refs
    chunk = weights[0].shape[1]
    ff = up.shape[2] // 2
    loads = {step: [] for step in phases}
    for step in phases:
        for index, ref in enumerate(weights):
            rows = piece_rows(place, index, pieces, chunk)
            for side in range(2):
                spot = slice(side * ff, (side + 1) * ff)
                for kind, target in enumerate((up, down)):
                    copy = pltpu.make_async_copy(
                        ref.at[2 * step + side, :, kind * ff : (kind + 1) * ff],
                        target.at[step, rows, spot],
                        load_sem.at[step, index, side, kind],
                    )
                    copy.start()
                    loads[step].append(copy)
    fetched = [
        pltpu.make_async_copy(held[k], part_s.at[k], held_sem.at[k])
        for k in range(sides * earlier)
    ]
    fetched += [
        pltpu.make_async_copy(ref.at[at * SEQ : (at + 1) * SEQ], extra.at[k], extra_sem.at[k])
        for k, ref in enumerate((aout_ref, din_ref))
    ]
    for copy in fetched:
        copy.start()

    gain, shift = vec_ref[0, 6:7, :], vec_ref[0, 7:8, :]
    hat, scale = normalise(x_ref[...].astype(F32))
    n2[...] = (hat * gain + shift).astype(BF16)
    if opens:
        for source, target in ((n2, n2t), (g_ref, gt)):
            turned[...] = source[...].T
            for index in range(pieces):
                rows = piece_rows(place, index, pieces, chunk)
                target[index * chunk : (index + 1) * chunk, :] = turned[rows, :]
    rows_ref[...] = jnp.zeros_like(rows_ref)
    stores = [pltpu.make_async_copy(part_s.at[k], made[k], out_sem.at[k]) for k in range(len(made))]

    def keep_gradients(activated, d_hidden):
        for copy in fetched[: sides * earlier]:
            copy.wait()
        for left, right, spot in ((n2t, d_hidden, 0), (gt, activated, 2 * ff)):
            fresh = dot(left[...], right, 1, 0)
            for index in range(pieces):
                value = fresh[index * chunk : (index + 1) * chunk, :]
                spots = (index % 2, index // 2, slice(None), slice(spot, spot + 2 * ff))
                if earlier:
                    value = value + part_s[spots].astype(F32)
                part_s[spots] = value.astype(BF16)
        for copy in stores:
            copy.start()
        sums = jnp.sum(d_hidden.astype(F32), axis=0, keepdims=True)
        rows_ref[2:3, :] = sums[:, :ff]
        rows_ref[3:4, :] = sums[:, ff:]

    def pair_of_groups(step, carry):
        for index, ref in enumerate(weights):
            for side in range(2):
                for kind, target in enumerate((up, down)):
                    pltpu.make_async_copy(
                        ref.at[side, :, :ff],
                        target.at[step, pl.ds(0, chunk), :ff],
                        load_sem.at[step, index, side, kind],
                    ).wait()
        which, parity = place[1] ^ step, place[2] % 2
        bias = jnp.concatenate(
            [bias_ref[2 * which + parity, 1:2, :], bias_ref[2 * which + 1 - parity, 1:2, :]],
            axis=1,
        )
        activated, slope = gelu_parts(dot(n2[...], up[step], 1, 0) + bias)
        activated = activated.astype(BF16)
        d_hidden = (dot(g_ref[...], down[step], 1, 0) * slope).astype(BF16)
        acc[0] += dot(activated, down[step], 1, 1)
        acc[1] += dot(d_hidden, up[step], 1, 1)
        if opens:
            pl.when(step == 0)(functools.partial(keep_gradients, activated, d_hidden))
        return carry

    acc[...] = begun[0][...] if begun else jnp.zeros_like(acc)
    lax.fori_loop(phases[0], phases[-1] + 1, pair_of_groups, 0)
    for copy in fetched[sides * earlier :]:
        copy.wait()
    if closes:
        d_second = acc[1]
        base = x_ref[...].astype(F32) + extra[0].astype(F32)
        base = base + vec_ref[0, 2:3, :] + vec_ref[0, 3:4, :]
        main_ref[0] = (acc[0] + base).astype(BF16)
        total = norm_back(d_second, hat, scale, gain) + extra[1].astype(F32)
        main_ref[1] = total.astype(BF16)
        rows_ref[0:1, :] = jnp.sum(d_second * hat, axis=0, keepdims=True)
        rows_ref[1:2, :] = jnp.sum(d_second, axis=0, keepdims=True)
    else:
        main_ref[...] = acc[...]
    for copy in stores:
        copy.wait()


def params(*kinds):
    return pltpu.CompilerParams(dimension_semantics=kinds, vmem_limit_bytes=VMEM)


def whole(shape):
    zeros = (0,) * len(shape)
    return pl.BlockSpec(shape, lambda *_: zeros)


def attention(place, x, g, wt, merge, bias, vecs, cosine, sine, count, pieces, earlier):
    width = x.shape[1]
    rows = 9 * HD
    columns = 2 * rows + 6 * HD
    given = pl.BlockSpec((SEQ, width), lambda i, place: (place[0] + i, 0))
    taken = pl.BlockSpec((SEQ, width), lambda i, place: (i, 0))

    def per(a, b):
        return pl.BlockSpec((1, a, b), lambda i, place: (i, 0, 0))

    sides = min(pieces, 2)
    part = (pieces // sides, width // pieces, columns)
    return pl.pallas_call(
        functools.partial(attention_kernel, pieces=pieces, earlier=1 if earlier else 0),
        grid_spec=pltpu.PrefetchScalarGridSpec(
            num_scalar_prefetch=1,
            grid=(count,),
            in_specs=[
                given, given, whole(wt.shape), whole(merge.shape), whole(bias.shape),
                whole((1, 8, width)), whole(cosine.shape), whole(sine.shape),
            ]
            + [whole(part)] * len(earlier),
            out_specs=[taken, taken, per(8, width), per(8, 2 * rows)]
            + [whole(part)] * sides,
            scratch_shapes=[
                pltpu.VMEM((width, SEQ), BF16),
                pltpu.VMEM((width, SEQ), BF16),
                pltpu.VMEM((wt.shape[0], SEQ), BF16),
                pltpu.VMEM((width, columns), F32),
            ],
        ),
        out_shape=[
            jax.ShapeDtypeStruct((count * SEQ, width), BF16),
            jax.ShapeDtypeStruct((count * SEQ, width), BF16),
            jax.ShapeDtypeStruct((count, 8, width), F32),
            jax.ShapeDtypeStruct((count, 8, 2 * rows), F32),
        ]
        + [jax.ShapeDtypeStruct(part, BF16)] * sides,
        compiler_params=params("arbitrary"),
        name="attention",
        cost_estimate=pl.CostEstimate(
            flops=count * 16_000_000_000, bytes_accessed=count * 12_000_000, transcendentals=0
        ),
    )(place, x, g, wt, merge, bias, vecs, cosine, sine, *earlier)


def feed(place, x, g, vecs, aout, din, at, weights, earlier, phases=(0, 1), begun=()):
    width = x.shape[1]
    groups, chunk, columns = weights[0].shape
    ff = columns // 2
    pieces = len(weights)
    sides = min(pieces, 2)
    given = pl.BlockSpec((SEQ, width), lambda s, place: (place[0], 0))
    part = (pieces // sides, chunk, 2 * columns)
    anywhere = pl.BlockSpec(memory_space=pl.ANY)
    first = 7 + pieces
    kept = 0 if begun else sides
    return pl.pallas_call(
        functools.partial(
            feed_kernel, pieces=pieces, earlier=1 if earlier else 0, at=at, phases=phases
        ),
        grid_spec=pltpu.PrefetchScalarGridSpec(
            num_scalar_prefetch=1,
            grid=(1,),
            in_specs=[given, given, whole(vecs.shape), whole((1, 8, width))]
            + [anywhere] * (2 + pieces + len(earlier))
            + [whole((2, SEQ, width))] * len(begun),
            out_specs=[whole((8, width)), whole((2, SEQ, width))] + [anywhere] * kept,
            scratch_shapes=[
                pltpu.VMEM((SEQ, width), BF16),
                pltpu.VMEM((width, SEQ), BF16),
                pltpu.VMEM((width, SEQ), BF16),
                pltpu.VMEM((width, SEQ), BF16),
                pltpu.VMEM((2, width, columns), BF16),
                pltpu.VMEM((2, width, columns), BF16),
                pltpu.VMEM((2, SEQ, width), BF16),
                pltpu.VMEM((sides, *part), BF16),
                pltpu.VMEM((2, SEQ, width), F32),
                pltpu.SemaphoreType.DMA((2, pieces, 2, 2)),
                pltpu.SemaphoreType.DMA((2,)),
                pltpu.SemaphoreType.DMA((2,)),
                pltpu.SemaphoreType.DMA((2,)),
            ],
        ),
        out_shape=[
            jax.ShapeDtypeStruct((8, width), F32),
            jax.ShapeDtypeStruct((2, SEQ, width), BF16 if phases[-1] == 1 else F32),
        ]
        + [jax.ShapeDtypeStruct(part, BF16)] * kept,
        input_output_aliases={first + k: 2 + k for k in range(len(earlier))},
        compiler_params=params("arbitrary"),
        name="feed",
        cost_estimate=pl.CostEstimate(
            flops=8_000_000_000 * len(phases), bytes_accessed=9_000_000, transcendentals=0
        ),
    )(place, x, g, vecs, vecs, aout, din, *weights, *earlier, *begun)


def prepare(place, weights, part):
    groups, chunk, columns = weights[0].shape
    pieces = len(weights)
    width = pieces * chunk
    rows = 9 * HD
    return pl.pallas_call(
        functools.partial(prepare_kernel, part=part),
        grid_spec=pltpu.PrefetchScalarGridSpec(
            num_scalar_prefetch=1,
            grid=(groups,),
            in_specs=[
                pl.BlockSpec((1, chunk, columns), lambda t, place: (t ^ place[2], 0, 0))
            ]
            * pieces,
            out_specs=[
                pl.BlockSpec((rows, width), lambda t, place: (t, 0)),
                pl.BlockSpec((3 * HD, width), lambda t, place: (t, 0)),
                pl.BlockSpec((1, 8, width), lambda t, place: (t, 0, 0)),
                pl.BlockSpec((1, 8, rows), lambda t, place: (t, 0, 0)),
            ],
            scratch_shapes=[pltpu.VMEM((width, columns), BF16)],
        ),
        out_shape=[
            jax.ShapeDtypeStruct((groups * rows, width), BF16),
            jax.ShapeDtypeStruct((groups * 3 * HD, width), BF16),
            jax.ShapeDtypeStruct((groups, 8, width), F32),
            jax.ShapeDtypeStruct((groups, 8, rows), F32),
        ],
        compiler_params=params("arbitrary"),
        name="prepare",
    )(place, *weights)


def trade(array, axis, mask):
    size = lax.axis_size(axis)
    return lax.ppermute(array, axis, [(i, i ^ mask) for i in range(size)])


def along(block):
    near, middle = trade(block, "tensor", 1), trade(block, "tensor", 2)
    return jnp.stack([block, near, middle, trade(tie(block, near), "tensor", 3)])


def across(block):
    return [block] + [trade(block, "dp", mask) for mask in (2, 4, 6)]


def both_cores(blocks):
    return [item for block in blocks for item in (block, trade(block, "dp", 1))]


def tie(array, after):
    return lax.optimization_barrier((array, after))[0]


def gather_both(early, late):
    own = early[None]
    others = [trade(early, "tensor", mask) for mask in (1, 2, 3)]
    own = across(own)
    others = jnp.stack(tie(others, own))
    late = along(tie(late, others))
    others = across(others)
    early = [jnp.concatenate(pair) for pair in zip(own, others)]
    ahead = late
    late = across(tie(late, early))
    early = both_cores([tie(item, ahead) for item in early])
    return early, late


def reduce_cores(kept, away):
    return kept.astype(F32) + trade(away, "dp", 1).astype(F32)


def exchange_across(pieces):
    return [pieces[0]] + [trade(pieces[k], "dp", 2 * k) for k in (1, 2, 3)]


def add_up(items):
    return sum(item.astype(F32) for item in items)


def body(
    block_input, cotangent, heads_weight, heads_bias, merge_weight, merge_bias, up_weight, up_bias,
    down_weight, down_bias, first_gain, first_shift, second_gain, second_shift,
):
    chunk = heads_weight.shape[0]
    owners = lax.axis_size("dp")
    groups = lax.axis_size("tensor")
    width = block_input.shape[1]
    spot = lax.axis_index("tensor")
    odd, pair = spot % 2, spot // 2
    total = block_input.shape[0] // SEQ
    count = total // 2
    fast = owners == 8 and groups == 4
    if fast:
        me = lax.axis_index("dp")
        facts = [odd * count, pair, spot, me // 2, me % 2]
    else:
        facts = [odd * count, pair, spot] + [jnp.zeros_like(spot)] * 2
    place = jnp.stack(facts).astype(jnp.int32)

    bias_part = heads_bias.shape[0]
    vectors = jnp.stack(
        [
            jnp.pad(heads_bias, (0, chunk - bias_part)), up_bias, merge_bias, down_bias,
            first_gain, first_shift, second_gain, second_shift,
        ],
        axis=1,
    )
    early = jnp.concatenate(
        [heads_weight, merge_weight.T, jnp.pad(vectors, ((0, 0), (0, 120)))], axis=1
    )
    late = jnp.concatenate([up_weight, down_weight.T], axis=1)
    if fast:
        early, late = gather_both(early, late)
    else:
        early, late = (
            lax.all_gather(item, ("tensor", "dp"), axis=0, tiled=True).reshape(groups, width, -1)
            for item in (early, late)
        )
        early, late = ([item[spot ^ jnp.arange(groups)]] for item in (early, late))
    rows = 9 * HD
    wt, merge, vecs, hbias = prepare(place, early, bias_part)
    if not fast:
        hbias = vecs[:, 0].reshape(groups, owners, chunk)[:, :, :bias_part]
        hbias = jnp.broadcast_to(hbias.reshape(groups, 1, rows), (groups, 8, rows))
    ff = up_weight.shape[1]
    cosine, sine = rotary_tables()
    swap = [(i, i ^ 1) for i in range(groups)]
    def shifted(i):
        return place.at[0].add(i)

    def attend(i, number, earlier, after):
        return attention(
            tie(shifted(i), after), block_input, cotangent, wt, merge, hbias, vecs, cosine, sine,
            number, len(early), earlier,
        )

    def advance(i, source, at, done, after):
        common = tie(shifted(i), after), block_input, cotangent, vecs, *source[:2], at, late
        sums, rows16, *grads = feed(*common, done[2:])
        return [rows16, sums, *grads], trade(rows16, "tensor", 1)

    lead = count - 1
    first = attend(0, lead, [], ())
    if fast:
        late = both_cores(tie(late, first[0]))
    second = attend(lead, 1, first[4:], late[0])
    done, others, totals = [], [], []
    wait = second[2]
    for i in range(count):
        source, at = (first, i) if i < lead else (second, 0)
        done, other = advance(i, source, at, done, wait)
        others.append((done[0], other))
        totals.append(done[1])
        if i == 0 and fast:
            heads_part = reduce_cores(*second[4:]).astype(BF16)
            wait = heads_part
        if i == 1:
            wait = others[0]
            if fast:
                heads_items = exchange_across(heads_part)
                wait = wait, heads_items
    if fast:
        heads_cols = add_up(tie(heads_items, done[1])).astype(BF16)
    else:
        heads_cols = lax.psum_scatter(second[4][0], "dp", scatter_dimension=0, tiled=True)

    rows_a = first[2].sum(0) + second[2].sum(0)
    hb = (first[3].sum(0) + second[3].sum(0))[0]
    rows_f = sum(totals)
    hb = jnp.pad(hb.reshape(2, owners, bias_part), ((0, 0), (0, 0), (0, chunk - bias_part)))
    small = jnp.concatenate(
        [
            rows_a[0:2], rows_f[0:2], rows_a[2:3], rows_f[2:4], hb.reshape(2, width),
            jnp.zeros((3, width), F32),
        ],
        axis=0,
    )
    if fast:
        kept, away = done[2:]
        kept = reduce_cores(kept, away).astype(BF16)
        small = (small + trade(small, "dp", 1)).reshape(-1, 4 * ff)
        tail = small.shape[0]
        small = jnp.pad(small, ((0, 8 - tail), (0, 0))).astype(BF16)
        kept = tie(kept, others[-2][1])
        ready = kept
        feed_cols = add_up(exchange_across([jnp.concatenate([item, small]) for item in kept]))
        small = feed_cols[chunk : chunk + tail].reshape(-1, width)
        small = lax.dynamic_slice(small, (0, me * chunk), (small.shape[0], chunk))
        feed_cols = feed_cols[:chunk].astype(BF16)
    else:
        ready = done[1]
        feed_cols = lax.psum_scatter(done[2][0], "dp", scatter_dimension=0, tiled=True)
        small = lax.psum_scatter(small, "dp", scatter_dimension=1, tiled=True)

    def settle(mine, other):
        return mine.astype(F32) + trade(other, "tensor", 1).astype(F32)

    small = small + trade(
        jnp.concatenate([small[:5], small[6:7], small[5:6], small[7:]], axis=0), "tensor", 1
    )
    feed_sum = settle(
        *(
            jnp.concatenate([feed_cols[:, k : k + ff], feed_cols[:, k + 2 * ff : k + 3 * ff]], axis=1)
            for k in (0, ff)
        )
    )
    wide = 2 * rows
    heads_cols = jnp.concatenate(
        [
            heads_cols[:, :rows], heads_cols[:, wide : wide + 3 * HD],
            heads_cols[:, rows:wide], heads_cols[:, wide + 3 * HD :],
        ],
        axis=1,
    )
    heads_cols = tie(heads_cols, ready)
    half = rows + 3 * HD
    left, right = heads_cols[:, :half], heads_cols[:, half:]
    heads_sum = settle(jnp.where(odd == 0, left, right), jnp.where(odd == 0, right, left))

    layer_output = tie(jnp.zeros(block_input.shape, BF16), done[1])
    input_grad = tie(jnp.zeros(block_input.shape, F32), ready)
    others = [(own, tie(other, ready)) for own, other in others]
    parts = [(own, odd, i) for i, (own, _) in enumerate(others)]
    parts += [(other, 1 - odd, i) for i, (_, other) in enumerate(others)]
    for item, base, i in parts:
        at = (base * count + i) * SEQ
        layer_output = lax.dynamic_update_slice(layer_output, item[0], (at, 0))
        given = lax.dynamic_slice(cotangent, (at, 0), (SEQ, width))
        input_grad = lax.dynamic_update_slice(
            input_grad, item[1].astype(F32) + given.astype(F32), (at, 0)
        )
    return (
        layer_output,
        input_grad,
        heads_sum[:, :rows],
        jnp.where(odd == 0, small[7], small[8])[:bias_part],
        heads_sum[:, rows:].T,
        small[4],
        feed_sum[:, :ff],
        small[5],
        feed_sum[:, ff:].T,
        small[4],
        small[0],
        small[1],
        small[2],
        small[3],
    )


def solution(mesh):
    placed = (
        P("dp", None),
        P("dp", None),
        P("dp", "tensor"),
        P(("tensor", "dp")),
        P("tensor", "dp"),
        P("dp"),
        P("dp", "tensor"),
        P(("tensor", "dp")),
        P("tensor", "dp"),
        P("dp"),
        P("dp"),
        P("dp"),
        P("dp"),
        P("dp"),
    )
    return jax.shard_map(
        body,
        mesh=mesh,
        in_specs=placed,
        out_specs=placed,
        check_vma=False,
    )
```

```python
import functools
import math

import jax
import jax.numpy as jnp
import numpy as np
from jax import lax
from jax.experimental import pallas as pl
from jax.experimental.pallas import tpu as pltpu
from jax.sharding import PartitionSpec as P

HD = 64
ROT = 16
SEQ = 512
EPS = 1e-05
VMEM = 60 * 1024 * 1024
F32 = jnp.float32
BF16 = jnp.bfloat16


def dot(left, right, left_dim, right_dim):
    return lax.dot_general(
        left, right, (((left_dim,), (right_dim,)), ((), ())), preferred_element_type=F32
    )


def normalise(values):
    average = jnp.mean(values, axis=-1, keepdims=True)
    centred = values - average
    spread = jnp.mean(centred * centred, axis=-1, keepdims=True)
    scale = lax.rsqrt(spread + EPS)
    return centred * scale, scale


def norm_back(d, hat, scale, gain):
    dg = d * gain
    first = jnp.mean(dg, axis=-1, keepdims=True)
    second = jnp.mean(dg * hat, axis=-1, keepdims=True)
    return (dg - first - hat * second) * scale


def rotary_tables():
    half = ROT // 2
    rates = 10000.0 ** (-(2.0 * np.arange(half)) / ROT)
    angles = rates[:, None] * np.arange(SEQ)[None, :]
    return np.cos(angles).astype(np.float32), np.sin(angles).astype(np.float32)


def rotate(values, cosine, sine):
    half = ROT // 2
    first, second = values[:half], values[half:ROT]
    return jnp.concatenate(
        [first * cosine - second * sine, second * cosine + first * sine, values[ROT:]], axis=0
    )


def piece_rows(place, index, pieces, chunk):
    if pieces == 1:
        return pl.ds(0, chunk)
    across, core = index // 2, index % 2
    owner = (across ^ place[3]) * 2 + (core ^ place[4])
    return pl.ds(pl.multiple_of(owner * chunk, 16), chunk)


def assemble(place, refs, target):
    chunk = refs[0].shape[1]
    for index, ref in enumerate(refs):
        target[piece_rows(place, index, len(refs), chunk), :] = ref[0]


def share_out(place, source, held, made, pieces):
    for index in range(pieces):
        value = source[piece_rows(place, index, pieces, made[0].shape[1]), :]
        if held:
            value = value + held[index % 2][index // 2].astype(F32)
        made[index % 2][index // 2] = value.astype(BF16)


def prepare_kernel(place, *refs, part):
    *pieces, wt_ref, merge_ref, vec_ref, bias_ref, full = refs
    assemble(place, pieces, full)
    rows = wt_ref.shape[0]
    end = rows + merge_ref.shape[0]
    wt_ref[...] = full[:, :rows].T
    merge_ref[...] = full[:, rows:end].T
    vectors = full[:, end:].astype(F32)
    vec_ref[0] = vectors.T[: vec_ref.shape[1]]
    chunk = pieces[0].shape[1]
    if len(pieces) > 1:
        packed = [vectors[at : at + part] for at in range(0, vectors.shape[0], chunk)]
        bias_ref[0] = jnp.concatenate(packed, axis=0).T[: bias_ref.shape[1]]
    else:
        bias_ref[...] = jnp.zeros_like(bias_ref)


def attention_kernel(
    place, x_ref, g_ref, wt_ref, merge_ref, bias_ref, vec_ref, cos_ref, sin_ref, *refs,
    pieces, earlier,
):
    sides = min(pieces, 2)
    held, refs = refs[: sides * earlier], refs[sides * earlier :]
    out_ref, din_ref, rows_ref, hb_ref = refs[:4]
    made = refs[4 : 4 + sides]
    datt, att, dmix, acc = refs[4 + sides :]
    groups = wt_ref.shape[0] // (9 * HD)
    rows = 9 * HD
    half = SEQ // 2
    scaling = 1.0 / math.sqrt(HD)
    x = x_ref[...].astype(F32)
    g = g_ref[...]
    gain, shift = vec_ref[0, 4:5, :], vec_ref[0, 5:6, :]
    hat, scale = normalise(x)
    n1 = (hat * gain + shift).astype(BF16)
    datt[...] = dot(merge_ref[...], g, 1, 1).astype(BF16)
    cosine, sine = cos_ref[...], sin_ref[...]
    below = lax.broadcasted_iota(jnp.int32, (half, half), 0) <= lax.broadcasted_iota(
        jnp.int32, (half, half), 1
    )

    def raise_columns(scores):
        raised = jnp.exp(scores - jnp.max(scores, axis=0, keepdims=True))
        return raised, jnp.sum(raised, axis=0, keepdims=True)

    def group(index, carry):
        base = pl.multiple_of(index * rows, rows)
        part = dot(wt_ref[pl.ds(base, rows), :], n1, 1, 1)
        part = part + bias_ref[index].T[:, 0:1]
        for head in range(3):
            at = head * 3 * HD
            query = (rotate(part[at : at + HD], cosine, sine) * scaling).astype(BF16)
            keys = rotate(part[at + HD : at + 2 * HD], cosine, sine).astype(BF16)
            values = part[at + 2 * HD : at + 3 * HD].astype(BF16)
            spot = pl.multiple_of(index * 3 * HD + head * HD, HD)
            given = datt[pl.ds(spot, HD), :].astype(F32)
            keys_t, values_t = keys.T, values.T
            s0 = dot(keys_t[:half], query[:, :half], 1, 0)
            s1a = dot(keys_t[:half], query[:, half:], 1, 0)
            s1b = dot(keys_t[half:], query[:, half:], 1, 0)
            e0, l0 = raise_columns(jnp.where(below, s0, -1e30))
            e1, l1 = raise_columns(
                jnp.concatenate([s1a, jnp.where(below, s1b, -1e30)], axis=0)
            )
            w0, w1 = e0.astype(BF16), e1.astype(BF16)
            share = 1.0 / jnp.concatenate([l0, l1], axis=1)
            attended = share * jnp.concatenate(
                [dot(values[:, :half], w0, 1, 0), dot(values, w1, 1, 0)], axis=1
            )
            att[pl.ds(spot, HD), :] = attended.astype(BF16)
            given = (given * share).astype(BF16)
            level = jnp.sum(given.astype(F32) * attended, axis=0, keepdims=True)
            q0 = dot(values_t[:half], given[:, :half], 1, 0)
            q1 = dot(values_t, given[:, half:], 1, 0)
            d0 = (e0 * (q0 - level[:, :half])).astype(BF16)
            d1 = (e1 * (q1 - level[:, half:])).astype(BF16)
            d_values = dot(given[:, half:], w1, 1, 1)
            d_values = jnp.concatenate(
                [d_values[:, :half] + dot(given[:, :half], w0, 1, 1), d_values[:, half:]], axis=1
            )
            d_keys = dot(query[:, half:], d1, 1, 1)
            d_keys = jnp.concatenate(
                [d_keys[:, :half] + dot(query[:, :half], d0, 1, 1), d_keys[:, half:]], axis=1
            )
            d_query = jnp.concatenate(
                [dot(keys[:, :half], d0, 1, 0), dot(keys, d1, 1, 0)], axis=1
            ) * scaling
            to = pl.multiple_of(base + at, HD)
            dmix[pl.ds(to, HD), :] = rotate(d_query, cosine, -sine).astype(BF16)
            dmix[pl.ds(to + HD, HD), :] = rotate(d_keys, cosine, -sine).astype(BF16)
            dmix[pl.ds(to + 2 * HD, HD), :] = d_values.astype(BF16)
        return carry

    lax.fori_loop(0, groups, group, 0)
    out_ref[...] = dot(att[...].T, merge_ref[...], 1, 0).astype(BF16)
    d_first = dot(dmix[...].T, wt_ref[...], 1, 0)
    pair = place[1]
    mine = dmix[pl.ds(pl.multiple_of(pair * 2 * rows, 2 * rows), 2 * rows), :]
    mine_att = att[pl.ds(pl.multiple_of(pair * 6 * HD, 6 * HD), 6 * HD), :]
    hb_ref[0] = dot(jnp.ones((8, SEQ), BF16), mine, 1, 1)
    step = pl.program_id(0)

    @pl.when(step == 0)
    def _():
        acc[...] = jnp.zeros_like(acc)

    acc[:, : 2 * rows] += dot(n1.T, mine, 1, 1)
    acc[:, 2 * rows :] += dot(g.T, mine_att, 1, 1)

    @pl.when(step == pl.num_programs(0) - 1)
    def _():
        share_out(place, acc, held, made, pieces)

    rows_ref[0] = jnp.concatenate(
        [
            jnp.sum(d_first * hat, axis=0, keepdims=True),
            jnp.sum(d_first, axis=0, keepdims=True),
            jnp.sum(g.astype(F32), axis=0, keepdims=True),
            jnp.zeros((5, x.shape[1]), F32),
        ],
        axis=0,
    )
    din_ref[...] = norm_back(d_first, hat, scale, gain).astype(BF16)


def gelu_parts(h):
    near = 0.7071067811865476 * jnp.abs(h)
    below = 1.0 + 0.3275911 * near
    t = pl.reciprocal(below, approx=True)
    t = t * (2.0 - below * t)
    bell = jnp.exp(-0.5 * h * h)
    series = 1.061405429 * t - 1.453152027
    series = series * t + 1.421413741
    series = series * t - 0.284496736
    series = series * t + 0.254829592
    tail = 0.5 * series * t * bell
    phi = jnp.where(h >= 0, 1.0 - tail, tail)
    return h * phi, phi + h * bell * 0.3989422804014327


def feed_kernel(
    place, x_ref, g_ref, bias_ref, vec_ref, aout_ref, din_ref, *refs, pieces, earlier, at, phases,
):
    opens, closes = phases[0] == 0, phases[-1] == 1
    weights, refs = refs[:pieces], refs[pieces:]
    sides = min(pieces, 2)
    held, refs = refs[: sides * earlier], refs[sides * earlier :]
    begun, refs = refs[: 1 - opens], refs[1 - opens :]
    rows_ref, main_ref = refs[:2]
    made, refs = refs[2 : 2 + sides * opens], refs[2 + sides * opens :]
    n2, turned, n2t, gt, up, down, extra, part_s, acc, load_sem, held_sem, extra_sem, out_sem = refs
    chunk = weights[0].shape[1]
    ff = up.shape[2] // 2
    loads = {step: [] for step in phases}
    for step in phases:
        for index, ref in enumerate(weights):
            rows = piece_rows(place, index, pieces, chunk)
            for side in range(2):
                spot = slice(side * ff, (side + 1) * ff)
                for kind, target in enumerate((up, down)):
                    copy = pltpu.make_async_copy(
                        ref.at[2 * step + side, :, kind * ff : (kind + 1) * ff],
                        target.at[step, rows, spot],
                        load_sem.at[step, index, side, kind],
                    )
                    copy.start()
                    loads[step].append(copy)
    fetched = [
        pltpu.make_async_copy(held[k], part_s.at[k], held_sem.at[k])
        for k in range(sides * earlier)
    ]
    fetched += [
        pltpu.make_async_copy(ref.at[at * SEQ : (at + 1) * SEQ], extra.at[k], extra_sem.at[k])
        for k, ref in enumerate((aout_ref, din_ref))
    ]
    for copy in fetched:
        copy.start()

    gain, shift = vec_ref[0, 6:7, :], vec_ref[0, 7:8, :]
    hat, scale = normalise(x_ref[...].astype(F32))
    n2[...] = (hat * gain + shift).astype(BF16)
    if opens:
        for source, target in ((n2, n2t), (g_ref, gt)):
            turned[...] = source[...].T
            for index in range(pieces):
                rows = piece_rows(place, index, pieces, chunk)
                target[index * chunk : (index + 1) * chunk, :] = turned[rows, :]
    rows_ref[...] = jnp.zeros_like(rows_ref)
    stores = [pltpu.make_async_copy(part_s.at[k], made[k], out_sem.at[k]) for k in range(len(made))]

    def keep_gradients(activated, d_hidden):
        for copy in fetched[: sides * earlier]:
            copy.wait()
        for left, right, spot in ((n2t, d_hidden, 0), (gt, activated, 2 * ff)):
            fresh = dot(left[...], right, 1, 0)
            for index in range(pieces):
                value = fresh[index * chunk : (index + 1) * chunk, :]
                spots = (index % 2, index // 2, slice(None), slice(spot, spot + 2 * ff))
                if earlier:
                    value = value + part_s[spots].astype(F32)
                part_s[spots] = value.astype(BF16)
        for copy in stores:
            copy.start()
        sums = jnp.sum(d_hidden.astype(F32), axis=0, keepdims=True)
        rows_ref[2:3, :] = sums[:, :ff]
        rows_ref[3:4, :] = sums[:, ff:]

    def pair_of_groups(step, carry):
        for index, ref in enumerate(weights):
            for side in range(2):
                for kind, target in enumerate((up, down)):
                    pltpu.make_async_copy(
                        ref.at[side, :, :ff],
                        target.at[step, pl.ds(0, chunk), :ff],
                        load_sem.at[step, index, side, kind],
                    ).wait()
        which, parity = place[1] ^ step, place[2] % 2
        bias = jnp.concatenate(
            [bias_ref[2 * which + parity, 1:2, :], bias_ref[2 * which + 1 - parity, 1:2, :]],
            axis=1,
        )
        activated, slope = gelu_parts(dot(n2[...], up[step], 1, 0) + bias)
        activated = activated.astype(BF16)
        d_hidden = (dot(g_ref[...], down[step], 1, 0) * slope).astype(BF16)
        acc[0] += dot(activated, down[step], 1, 1)
        acc[1] += dot(d_hidden, up[step], 1, 1)
        if opens:
            pl.when(step == 0)(functools.partial(keep_gradients, activated, d_hidden))
        return carry

    acc[...] = begun[0][...] if begun else jnp.zeros_like(acc)
    lax.fori_loop(phases[0], phases[-1] + 1, pair_of_groups, 0)
    for copy in fetched[sides * earlier :]:
        copy.wait()
    if closes:
        d_second = acc[1]
        base = x_ref[...].astype(F32) + extra[0].astype(F32)
        base = base + vec_ref[0, 2:3, :] + vec_ref[0, 3:4, :]
        main_ref[0] = (acc[0] + base).astype(BF16)
        total = norm_back(d_second, hat, scale, gain) + extra[1].astype(F32)
        main_ref[1] = total.astype(BF16)
        rows_ref[0:1, :] = jnp.sum(d_second * hat, axis=0, keepdims=True)
        rows_ref[1:2, :] = jnp.sum(d_second, axis=0, keepdims=True)
    else:
        main_ref[...] = acc[...]
    for copy in stores:
        copy.wait()


def params(*kinds):
    return pltpu.CompilerParams(dimension_semantics=kinds, vmem_limit_bytes=VMEM)


def whole(shape):
    zeros = (0,) * len(shape)
    return pl.BlockSpec(shape, lambda *_: zeros)


def attention(place, x, g, wt, merge, bias, vecs, cosine, sine, count, pieces, earlier):
    width = x.shape[1]
    rows = 9 * HD
    columns = 2 * rows + 6 * HD
    given = pl.BlockSpec((SEQ, width), lambda i, place: (place[0] + i, 0))
    taken = pl.BlockSpec((SEQ, width), lambda i, place: (i, 0))

    def per(a, b):
        return pl.BlockSpec((1, a, b), lambda i, place: (i, 0, 0))

    sides = min(pieces, 2)
    part = (pieces // sides, width // pieces, columns)
    return pl.pallas_call(
        functools.partial(attention_kernel, pieces=pieces, earlier=1 if earlier else 0),
        grid_spec=pltpu.PrefetchScalarGridSpec(
            num_scalar_prefetch=1,
            grid=(count,),
            in_specs=[
                given, given, whole(wt.shape), whole(merge.shape), whole(bias.shape),
                whole((1, 8, width)), whole(cosine.shape), whole(sine.shape),
            ]
            + [whole(part)] * len(earlier),
            out_specs=[taken, taken, per(8, width), per(8, 2 * rows)]
            + [whole(part)] * sides,
            scratch_shapes=[
                pltpu.VMEM((width, SEQ), BF16),
                pltpu.VMEM((width, SEQ), BF16),
                pltpu.VMEM((wt.shape[0], SEQ), BF16),
                pltpu.VMEM((width, columns), F32),
            ],
        ),
        out_shape=[
            jax.ShapeDtypeStruct((count * SEQ, width), BF16),
            jax.ShapeDtypeStruct((count * SEQ, width), BF16),
            jax.ShapeDtypeStruct((count, 8, width), F32),
            jax.ShapeDtypeStruct((count, 8, 2 * rows), F32),
        ]
        + [jax.ShapeDtypeStruct(part, BF16)] * sides,
        compiler_params=params("arbitrary"),
        name="attention",
        cost_estimate=pl.CostEstimate(
            flops=count * 16_000_000_000, bytes_accessed=count * 12_000_000, transcendentals=0
        ),
    )(place, x, g, wt, merge, bias, vecs, cosine, sine, *earlier)


def feed(place, x, g, vecs, aout, din, at, weights, earlier, phases=(0, 1), begun=()):
    width = x.shape[1]
    groups, chunk, columns = weights[0].shape
    ff = columns // 2
    pieces = len(weights)
    sides = min(pieces, 2)
    given = pl.BlockSpec((SEQ, width), lambda s, place: (place[0], 0))
    part = (pieces // sides, chunk, 2 * columns)
    anywhere = pl.BlockSpec(memory_space=pl.ANY)
    first = 7 + pieces
    kept = 0 if begun else sides
    return pl.pallas_call(
        functools.partial(
            feed_kernel, pieces=pieces, earlier=1 if earlier else 0, at=at, phases=phases
        ),
        grid_spec=pltpu.PrefetchScalarGridSpec(
            num_scalar_prefetch=1,
            grid=(1,),
            in_specs=[given, given, whole(vecs.shape), whole((1, 8, width))]
            + [anywhere] * (2 + pieces + len(earlier))
            + [whole((2, SEQ, width))] * len(begun),
            out_specs=[whole((8, width)), whole((2, SEQ, width))] + [anywhere] * kept,
            scratch_shapes=[
                pltpu.VMEM((SEQ, width), BF16),
                pltpu.VMEM((width, SEQ), BF16),
                pltpu.VMEM((width, SEQ), BF16),
                pltpu.VMEM((width, SEQ), BF16),
                pltpu.VMEM((2, width, columns), BF16),
                pltpu.VMEM((2, width, columns), BF16),
                pltpu.VMEM((2, SEQ, width), BF16),
                pltpu.VMEM((sides, *part), BF16),
                pltpu.VMEM((2, SEQ, width), F32),
                pltpu.SemaphoreType.DMA((2, pieces, 2, 2)),
                pltpu.SemaphoreType.DMA((2,)),
                pltpu.SemaphoreType.DMA((2,)),
                pltpu.SemaphoreType.DMA((2,)),
            ],
        ),
        out_shape=[
            jax.ShapeDtypeStruct((8, width), F32),
            jax.ShapeDtypeStruct((2, SEQ, width), BF16 if phases[-1] == 1 else F32),
        ]
        + [jax.ShapeDtypeStruct(part, BF16)] * kept,
        input_output_aliases={first + k: 2 + k for k in range(len(earlier))},
        compiler_params=params("arbitrary"),
        name="feed",
        cost_estimate=pl.CostEstimate(
            flops=8_000_000_000 * len(phases), bytes_accessed=9_000_000, transcendentals=0
        ),
    )(place, x, g, vecs, vecs, aout, din, *weights, *earlier, *begun)


def prepare(place, weights, part):
    groups, chunk, columns = weights[0].shape
    pieces = len(weights)
    width = pieces * chunk
    rows = 9 * HD
    return pl.pallas_call(
        functools.partial(prepare_kernel, part=part),
        grid_spec=pltpu.PrefetchScalarGridSpec(
            num_scalar_prefetch=1,
            grid=(groups,),
            in_specs=[
                pl.BlockSpec((1, chunk, columns), lambda t, place: (t ^ place[2], 0, 0))
            ]
            * pieces,
            out_specs=[
                pl.BlockSpec((rows, width), lambda t, place: (t, 0)),
                pl.BlockSpec((3 * HD, width), lambda t, place: (t, 0)),
                pl.BlockSpec((1, 8, width), lambda t, place: (t, 0, 0)),
                pl.BlockSpec((1, 8, rows), lambda t, place: (t, 0, 0)),
            ],
            scratch_shapes=[pltpu.VMEM((width, columns), BF16)],
        ),
        out_shape=[
            jax.ShapeDtypeStruct((groups * rows, width), BF16),
            jax.ShapeDtypeStruct((groups * 3 * HD, width), BF16),
            jax.ShapeDtypeStruct((groups, 8, width), F32),
            jax.ShapeDtypeStruct((groups, 8, rows), F32),
        ],
        compiler_params=params("arbitrary"),
        name="prepare",
    )(place, *weights)


def trade(array, axis, mask):
    size = lax.axis_size(axis)
    return lax.ppermute(array, axis, [(i, i ^ mask) for i in range(size)])


def along(block):
    near, middle = trade(block, "tensor", 1), trade(block, "tensor", 2)
    return jnp.stack([block, near, middle, trade(tie(block, near), "tensor", 3)])


def across(block):
    return [block] + [trade(block, "dp", mask) for mask in (2, 4, 6)]


def both_cores(blocks):
    return [item for block in blocks for item in (block, trade(block, "dp", 1))]


def tie(array, after):
    return lax.optimization_barrier((array, after))[0]


def gather_both(early, late):
    own = early[None]
    others = [trade(early, "tensor", mask) for mask in (1, 2, 3)]
    own = across(own)
    others = jnp.stack(tie(others, own))
    late = along(tie(late, others))
    others = across(others)
    early = [jnp.concatenate(pair) for pair in zip(own, others)]
    ahead = late
    late = across(tie(late, early))
    early = both_cores([tie(item, ahead) for item in early])
    return early, late


def reduce_cores(kept, away):
    return kept.astype(F32) + trade(away, "dp", 1).astype(F32)


def exchange_across(pieces):
    return [pieces[0]] + [trade(pieces[k], "dp", 2 * k) for k in (1, 2, 3)]


def add_up(items):
    return sum(item.astype(F32) for item in items)


def body(
    block_input, cotangent, heads_weight, heads_bias, merge_weight, merge_bias, up_weight, up_bias,
    down_weight, down_bias, first_gain, first_shift, second_gain, second_shift,
):
    chunk = heads_weight.shape[0]
    owners = lax.axis_size("dp")
    groups = lax.axis_size("tensor")
    width = block_input.shape[1]
    spot = lax.axis_index("tensor")
    odd, pair = spot % 2, spot // 2
    total = block_input.shape[0] // SEQ
    count = total // 2
    fast = owners == 8 and groups == 4
    if fast:
        me = lax.axis_index("dp")
        facts = [odd * count, pair, spot, me // 2, me % 2]
    else:
        facts = [odd * count, pair, spot] + [jnp.zeros_like(spot)] * 2
    place = jnp.stack(facts).astype(jnp.int32)

    bias_part = heads_bias.shape[0]
    vectors = jnp.stack(
        [
            jnp.pad(heads_bias, (0, chunk - bias_part)), up_bias, merge_bias, down_bias,
            first_gain, first_shift, second_gain, second_shift,
        ],
        axis=1,
    )
    early = jnp.concatenate(
        [heads_weight, merge_weight.T, jnp.pad(vectors, ((0, 0), (0, 120)))], axis=1
    )
    late = jnp.concatenate([up_weight, down_weight.T], axis=1)
    if fast:
        early, late = gather_both(early, late)
    else:
        early, late = (
            lax.all_gather(item, ("tensor", "dp"), axis=0, tiled=True).reshape(groups, width, -1)
            for item in (early, late)
        )
        early, late = ([item[spot ^ jnp.arange(groups)]] for item in (early, late))
    rows = 9 * HD
    wt, merge, vecs, hbias = prepare(place, early, bias_part)
    if not fast:
        hbias = vecs[:, 0].reshape(groups, owners, chunk)[:, :, :bias_part]
        hbias = jnp.broadcast_to(hbias.reshape(groups, 1, rows), (groups, 8, rows))
    ff = up_weight.shape[1]
    cosine, sine = rotary_tables()
    swap = [(i, i ^ 1) for i in range(groups)]
    def shifted(i):
        return place.at[0].add(i)

    def attend(i, number, earlier, after):
        return attention(
            tie(shifted(i), after), block_input, cotangent, wt, merge, hbias, vecs, cosine, sine,
            number, len(early), earlier,
        )

    def advance(i, source, at, done, after):
        common = tie(shifted(i), after), block_input, cotangent, vecs, *source[:2], at, late
        sums, rows16, *grads = feed(*common, done[2:])
        return [rows16, sums, *grads], trade(rows16, "tensor", 1)

    lead = count - 1
    first = attend(0, lead, [], ())
    if fast:
        late = both_cores(tie(late, first[0]))
    second = attend(lead, 1, first[4:], late[0])
    done, others, totals = [], [], []
    wait = second[2]
    for i in range(count):
        source, at = (first, i) if i < lead else (second, 0)
        done, other = advance(i, source, at, done, wait)
        others.append((done[0], other))
        totals.append(done[1])
        if i == 0 and fast:
            heads_part = reduce_cores(*second[4:]).astype(BF16)
            wait = heads_part
        if i == 1:
            wait = others[0]
            if fast:
                heads_items = exchange_across(heads_part)
                wait = wait, heads_items
    if fast:
        heads_cols = add_up(tie(heads_items, done[1])).astype(BF16)
    else:
        heads_cols = lax.psum_scatter(second[4][0], "dp", scatter_dimension=0, tiled=True)

    rows_a = first[2].sum(0) + second[2].sum(0)
    hb = (first[3].sum(0) + second[3].sum(0))[0]
    rows_f = sum(totals)
    hb = jnp.pad(hb.reshape(2, owners, bias_part), ((0, 0), (0, 0), (0, chunk - bias_part)))
    small = jnp.concatenate(
        [
            rows_a[0:2], rows_f[0:2], rows_a[2:3], rows_f[2:4], hb.reshape(2, width),
            jnp.zeros((3, width), F32),
        ],
        axis=0,
    )
    if fast:
        kept, away = done[2:]
        kept = reduce_cores(kept, away).astype(BF16)
        small = (small + trade(small, "dp", 1)).reshape(-1, 4 * ff)
        tail = small.shape[0]
        small = jnp.pad(small, ((0, 8 - tail), (0, 0))).astype(BF16)
        kept = tie(kept, others[-2][1])
        ready = kept
        feed_cols = add_up(exchange_across([jnp.concatenate([item, small]) for item in kept]))
        small = feed_cols[chunk : chunk + tail].reshape(-1, width)
        small = lax.dynamic_slice(small, (0, me * chunk), (small.shape[0], chunk))
        feed_cols = feed_cols[:chunk].astype(BF16)
    else:
        ready = done[1]
        feed_cols = lax.psum_scatter(done[2][0], "dp", scatter_dimension=0, tiled=True)
        small = lax.psum_scatter(small, "dp", scatter_dimension=1, tiled=True)

    def settle(mine, other):
        return mine.astype(F32) + trade(other, "tensor", 1).astype(F32)

    small = small + trade(
        jnp.concatenate([small[:5], small[6:7], small[5:6], small[7:]], axis=0), "tensor", 1
    )
    feed_sum = settle(
        *(
            jnp.concatenate([feed_cols[:, k : k + ff], feed_cols[:, k + 2 * ff : k + 3 * ff]], axis=1)
            for k in (0, ff)
        )
    )
    wide = 2 * rows
    heads_cols = jnp.concatenate(
        [
            heads_cols[:, :rows], heads_cols[:, wide : wide + 3 * HD],
            heads_cols[:, rows:wide], heads_cols[:, wide + 3 * HD :],
        ],
        axis=1,
    )
    heads_cols = tie(heads_cols, ready)
    others[-1] = others[-1][0], tie(others[-1][1], ready)
    half = rows + 3 * HD
    left, right = heads_cols[:, :half], heads_cols[:, half:]
    heads_sum = settle(jnp.where(odd == 0, left, right), jnp.where(odd == 0, right, left))

    layer_output = tie(jnp.zeros(block_input.shape, BF16), done[1])
    input_grad = tie(jnp.zeros(block_input.shape, F32), ready)
    for i, both in enumerate(others):
        for item, base in zip(both, (odd, 1 - odd)):
            at = (base * count + i) * SEQ
            layer_output = lax.dynamic_update_slice(layer_output, item[0], (at, 0))
            given = lax.dynamic_slice(cotangent, (at, 0), (SEQ, width))
            input_grad = lax.dynamic_update_slice(
                input_grad, item[1].astype(F32) + given.astype(F32), (at, 0)
            )
    return (
        layer_output,
        input_grad,
        heads_sum[:, :rows],
        jnp.where(odd == 0, small[7], small[8])[:bias_part],
        heads_sum[:, rows:].T,
        small[4],
        feed_sum[:, :ff],
        small[5],
        feed_sum[:, ff:].T,
        small[4],
        small[0],
        small[1],
        small[2],
        small[3],
    )


def solution(mesh):
    placed = (
        P("dp", None),
        P("dp", None),
        P("dp", "tensor"),
        P(("tensor", "dp")),
        P("tensor", "dp"),
        P("dp"),
        P("dp", "tensor"),
        P(("tensor", "dp")),
        P("tensor", "dp"),
        P("dp"),
        P("dp"),
        P("dp"),
        P("dp"),
        P("dp"),
    )
    return jax.shard_map(
        body,
        mesh=mesh,
        in_specs=placed,
        out_specs=placed,
        check_vma=False,
    )
```

```python
import functools
import math

import jax
import jax.numpy as jnp
import numpy as np
from jax import lax
from jax.experimental import pallas as pl
from jax.experimental.pallas import tpu as pltpu
from jax.sharding import PartitionSpec as P

HD = 64
ROT = 16
SEQ = 512
EPS = 1e-05
VMEM = 60 * 1024 * 1024
F32 = jnp.float32
BF16 = jnp.bfloat16


def dot(left, right, left_dim, right_dim):
    return lax.dot_general(
        left, right, (((left_dim,), (right_dim,)), ((), ())), preferred_element_type=F32
    )


def normalise(values):
    average = jnp.mean(values, axis=-1, keepdims=True)
    centred = values - average
    spread = jnp.mean(centred * centred, axis=-1, keepdims=True)
    scale = lax.rsqrt(spread + EPS)
    return centred * scale, scale


def norm_back(d, hat, scale, gain):
    dg = d * gain
    first = jnp.mean(dg, axis=-1, keepdims=True)
    second = jnp.mean(dg * hat, axis=-1, keepdims=True)
    return (dg - first - hat * second) * scale


def rotary_tables():
    half = ROT // 2
    rates = 10000.0 ** (-(2.0 * np.arange(half)) / ROT)
    angles = rates[:, None] * np.arange(SEQ)[None, :]
    return np.cos(angles).astype(np.float32), np.sin(angles).astype(np.float32)


def rotate(values, cosine, sine):
    half = ROT // 2
    first, second = values[:half], values[half:ROT]
    return jnp.concatenate(
        [first * cosine - second * sine, second * cosine + first * sine, values[ROT:]], axis=0
    )


def piece_rows(place, index, pieces, chunk):
    if pieces == 1:
        return pl.ds(0, chunk)
    across, core = index // 2, index % 2
    owner = (across ^ place[3]) * 2 + (core ^ place[4])
    return pl.ds(pl.multiple_of(owner * chunk, 16), chunk)


def assemble(place, refs, target):
    chunk = refs[0].shape[1]
    for index, ref in enumerate(refs):
        target[piece_rows(place, index, len(refs), chunk), :] = ref[0]


def share_out(place, source, held, made, pieces):
    for index in range(pieces):
        value = source[piece_rows(place, index, pieces, made[0].shape[1]), :]
        if held:
            value = value + held[index % 2][index // 2].astype(F32)
        made[index % 2][index // 2] = value.astype(BF16)


def prepare_kernel(place, *refs, part):
    *pieces, wt_ref, merge_ref, vec_ref, bias_ref, full = refs
    assemble(place, pieces, full)
    rows = wt_ref.shape[0]
    end = rows + merge_ref.shape[0]
    wt_ref[...] = full[:, :rows].T
    merge_ref[...] = full[:, rows:end].T
    vectors = full[:, end:].astype(F32)
    vec_ref[0] = vectors.T[: vec_ref.shape[1]]
    chunk = pieces[0].shape[1]
    if len(pieces) > 1:
        packed = [vectors[at : at + part] for at in range(0, vectors.shape[0], chunk)]
        bias_ref[0] = jnp.concatenate(packed, axis=0).T[: bias_ref.shape[1]]
    else:
        bias_ref[...] = jnp.zeros_like(bias_ref)


def attention_kernel(
    place, x_ref, g_ref, wt_ref, merge_ref, bias_ref, vec_ref, cos_ref, sin_ref, *refs,
    pieces, earlier,
):
    sides = min(pieces, 2)
    held, refs = refs[: sides * earlier], refs[sides * earlier :]
    out_ref, din_ref, rows_ref, hb_ref = refs[:4]
    made = refs[4 : 4 + sides]
    datt, att, dmix, acc = refs[4 + sides :]
    groups = wt_ref.shape[0] // (9 * HD)
    rows = 9 * HD
    half = SEQ // 2
    scaling = 1.0 / math.sqrt(HD)
    x = x_ref[...].astype(F32)
    g = g_ref[...]
    gain, shift = vec_ref[0, 4:5, :], vec_ref[0, 5:6, :]
    hat, scale = normalise(x)
    n1 = (hat * gain + shift).astype(BF16)
    datt[...] = dot(merge_ref[...], g, 1, 1).astype(BF16)
    cosine, sine = cos_ref[...], sin_ref[...]
    below = lax.broadcasted_iota(jnp.int32, (half, half), 0) <= lax.broadcasted_iota(
        jnp.int32, (half, half), 1
    )

    def raise_columns(scores):
        raised = jnp.exp(scores - jnp.max(scores, axis=0, keepdims=True))
        return raised, jnp.sum(raised, axis=0, keepdims=True)

    def group(index, carry):
        base = pl.multiple_of(index * rows, rows)
        part = dot(wt_ref[pl.ds(base, rows), :], n1, 1, 1)
        part = part + bias_ref[index].T[:, 0:1]
        for head in range(3):
            at = head * 3 * HD
            query = (rotate(part[at : at + HD], cosine, sine) * scaling).astype(BF16)
            keys = rotate(part[at + HD : at + 2 * HD], cosine, sine).astype(BF16)
            values = part[at + 2 * HD : at + 3 * HD].astype(BF16)
            spot = pl.multiple_of(index * 3 * HD + head * HD, HD)
            given = datt[pl.ds(spot, HD), :].astype(F32)
            keys_t, values_t = keys.T, values.T
            s0 = dot(keys_t[:half], query[:, :half], 1, 0)
            s1a = dot(keys_t[:half], query[:, half:], 1, 0)
            s1b = dot(keys_t[half:], query[:, half:], 1, 0)
            e0, l0 = raise_columns(jnp.where(below, s0, -1e30))
            e1, l1 = raise_columns(
                jnp.concatenate([s1a, jnp.where(below, s1b, -1e30)], axis=0)
            )
            w0, w1 = e0.astype(BF16), e1.astype(BF16)
            share = 1.0 / jnp.concatenate([l0, l1], axis=1)
            attended = share * jnp.concatenate(
                [dot(values[:, :half], w0, 1, 0), dot(values, w1, 1, 0)], axis=1
            )
            att[pl.ds(spot, HD), :] = attended.astype(BF16)
            given = (given * share).astype(BF16)
            level = jnp.sum(given.astype(F32) * attended, axis=0, keepdims=True)
            q0 = dot(values_t[:half], given[:, :half], 1, 0)
            q1 = dot(values_t, given[:, half:], 1, 0)
            d0 = (e0 * (q0 - level[:, :half])).astype(BF16)
            d1 = (e1 * (q1 - level[:, half:])).astype(BF16)
            d_values = dot(given[:, half:], w1, 1, 1)
            d_values = jnp.concatenate(
                [d_values[:, :half] + dot(given[:, :half], w0, 1, 1), d_values[:, half:]], axis=1
            )
            d_keys = dot(query[:, half:], d1, 1, 1)
            d_keys = jnp.concatenate(
                [d_keys[:, :half] + dot(query[:, :half], d0, 1, 1), d_keys[:, half:]], axis=1
            )
            d_query = jnp.concatenate(
                [dot(keys[:, :half], d0, 1, 0), dot(keys, d1, 1, 0)], axis=1
            ) * scaling
            to = pl.multiple_of(base + at, HD)
            dmix[pl.ds(to, HD), :] = rotate(d_query, cosine, -sine).astype(BF16)
            dmix[pl.ds(to + HD, HD), :] = rotate(d_keys, cosine, -sine).astype(BF16)
            dmix[pl.ds(to + 2 * HD, HD), :] = d_values.astype(BF16)
        return carry

    lax.fori_loop(0, groups, group, 0)
    out_ref[...] = dot(att[...].T, merge_ref[...], 1, 0).astype(BF16)
    d_first = dot(dmix[...].T, wt_ref[...], 1, 0)
    pair = place[1]
    mine = dmix[pl.ds(pl.multiple_of(pair * 2 * rows, 2 * rows), 2 * rows), :]
    mine_att = att[pl.ds(pl.multiple_of(pair * 6 * HD, 6 * HD), 6 * HD), :]
    hb_ref[0] = dot(jnp.ones((8, SEQ), BF16), mine, 1, 1)
    step = pl.program_id(0)

    @pl.when(step == 0)
    def _():
        acc[...] = jnp.zeros_like(acc)

    acc[:, : 2 * rows] += dot(n1.T, mine, 1, 1)
    acc[:, 2 * rows :] += dot(g.T, mine_att, 1, 1)

    @pl.when(step == pl.num_programs(0) - 1)
    def _():
        share_out(place, acc, held, made, pieces)

    rows_ref[0] = jnp.concatenate(
        [
            jnp.sum(d_first * hat, axis=0, keepdims=True),
            jnp.sum(d_first, axis=0, keepdims=True),
            jnp.sum(g.astype(F32), axis=0, keepdims=True),
            jnp.zeros((5, x.shape[1]), F32),
        ],
        axis=0,
    )
    din_ref[...] = norm_back(d_first, hat, scale, gain).astype(BF16)


def gelu_parts(h):
    near = 0.7071067811865476 * jnp.abs(h)
    below = 1.0 + 0.3275911 * near
    t = pl.reciprocal(below, approx=True)
    t = t * (2.0 - below * t)
    bell = jnp.exp(-0.5 * h * h)
    series = 1.061405429 * t - 1.453152027
    series = series * t + 1.421413741
    series = series * t - 0.284496736
    series = series * t + 0.254829592
    tail = 0.5 * series * t * bell
    phi = jnp.where(h >= 0, 1.0 - tail, tail)
    return h * phi, phi + h * bell * 0.3989422804014327


def feed_kernel(
    place, x_ref, g_ref, bias_ref, vec_ref, aout_ref, din_ref, *refs, pieces, earlier, at, phases,
):
    opens, closes = phases[0] == 0, phases[-1] == 1
    weights, refs = refs[:pieces], refs[pieces:]
    sides = min(pieces, 2)
    held, refs = refs[: sides * earlier], refs[sides * earlier :]
    begun, refs = refs[: 1 - opens], refs[1 - opens :]
    rows_ref, main_ref = refs[:2]
    made, refs = refs[2 : 2 + sides * opens], refs[2 + sides * opens :]
    n2, turned, n2t, gt, up, down, extra, part_s, acc, load_sem, held_sem, extra_sem, out_sem = refs
    chunk = weights[0].shape[1]
    ff = up.shape[2] // 2
    loads = {step: [] for step in phases}
    for step in phases:
        for index, ref in enumerate(weights):
            rows = piece_rows(place, index, pieces, chunk)
            for side in range(2):
                spot = slice(side * ff, (side + 1) * ff)
                for kind, target in enumerate((up, down)):
                    copy = pltpu.make_async_copy(
                        ref.at[2 * step + side, :, kind * ff : (kind + 1) * ff],
                        target.at[step, rows, spot],
                        load_sem.at[step, index, side, kind],
                    )
                    copy.start()
                    loads[step].append(copy)
    fetched = [
        pltpu.make_async_copy(held[k], part_s.at[k], held_sem.at[k])
        for k in range(sides * earlier)
    ]
    fetched += [
        pltpu.make_async_copy(ref.at[at * SEQ : (at + 1) * SEQ], extra.at[k], extra_sem.at[k])
        for k, ref in enumerate((aout_ref, din_ref))
    ]
    for copy in fetched:
        copy.start()

    gain, shift = vec_ref[0, 6:7, :], vec_ref[0, 7:8, :]
    hat, scale = normalise(x_ref[...].astype(F32))
    n2[...] = (hat * gain + shift).astype(BF16)
    if opens:
        for source, target in ((n2, n2t), (g_ref, gt)):
            turned[...] = source[...].T
            for index in range(pieces):
                rows = piece_rows(place, index, pieces, chunk)
                target[index * chunk : (index + 1) * chunk, :] = turned[rows, :]
    rows_ref[...] = jnp.zeros_like(rows_ref)
    stores = [pltpu.make_async_copy(part_s.at[k], made[k], out_sem.at[k]) for k in range(len(made))]

    def keep_gradients(activated, d_hidden):
        for copy in fetched[: sides * earlier]:
            copy.wait()
        for left, right, spot in ((n2t, d_hidden, 0), (gt, activated, 2 * ff)):
            fresh = dot(left[...], right, 1, 0)
            for index in range(pieces):
                value = fresh[index * chunk : (index + 1) * chunk, :]
                spots = (index % 2, index // 2, slice(None), slice(spot, spot + 2 * ff))
                if earlier:
                    value = value + part_s[spots].astype(F32)
                part_s[spots] = value.astype(BF16)
        for copy in stores:
            copy.start()
        sums = jnp.sum(d_hidden.astype(F32), axis=0, keepdims=True)
        rows_ref[2:3, :] = sums[:, :ff]
        rows_ref[3:4, :] = sums[:, ff:]

    def pair_of_groups(step, carry):
        for index, ref in enumerate(weights):
            for side in range(2):
                for kind, target in enumerate((up, down)):
                    pltpu.make_async_copy(
                        ref.at[side, :, :ff],
                        target.at[step, pl.ds(0, chunk), :ff],
                        load_sem.at[step, index, side, kind],
                    ).wait()
        which, parity = place[1] ^ step, place[2] % 2
        bias = jnp.concatenate(
            [bias_ref[2 * which + parity, 1:2, :], bias_ref[2 * which + 1 - parity, 1:2, :]],
            axis=1,
        )
        activated, slope = gelu_parts(dot(n2[...], up[step], 1, 0) + bias)
        activated = activated.astype(BF16)
        d_hidden = (dot(g_ref[...], down[step], 1, 0) * slope).astype(BF16)
        acc[0] += dot(activated, down[step], 1, 1)
        acc[1] += dot(d_hidden, up[step], 1, 1)
        if opens:
            pl.when(step == 0)(functools.partial(keep_gradients, activated, d_hidden))
        return carry

    acc[...] = begun[0][...] if begun else jnp.zeros_like(acc)
    lax.fori_loop(phases[0], phases[-1] + 1, pair_of_groups, 0)
    for copy in fetched[sides * earlier :]:
        copy.wait()
    if closes:
        d_second = acc[1]
        base = x_ref[...].astype(F32) + extra[0].astype(F32)
        base = base + vec_ref[0, 2:3, :] + vec_ref[0, 3:4, :]
        main_ref[0] = (acc[0] + base).astype(BF16)
        total = norm_back(d_second, hat, scale, gain) + extra[1].astype(F32)
        main_ref[1] = total.astype(BF16)
        rows_ref[0:1, :] = jnp.sum(d_second * hat, axis=0, keepdims=True)
        rows_ref[1:2, :] = jnp.sum(d_second, axis=0, keepdims=True)
    else:
        main_ref[...] = acc[...]
    for copy in stores:
        copy.wait()


def params(*kinds):
    return pltpu.CompilerParams(dimension_semantics=kinds, vmem_limit_bytes=VMEM)


def whole(shape):
    zeros = (0,) * len(shape)
    return pl.BlockSpec(shape, lambda *_: zeros)


def attention(place, x, g, wt, merge, bias, vecs, cosine, sine, count, pieces, earlier):
    width = x.shape[1]
    rows = 9 * HD
    columns = 2 * rows + 6 * HD
    given = pl.BlockSpec((SEQ, width), lambda i, place: (place[0] + i, 0))
    taken = pl.BlockSpec((SEQ, width), lambda i, place: (i, 0))

    def per(a, b):
        return pl.BlockSpec((1, a, b), lambda i, place: (i, 0, 0))

    sides = min(pieces, 2)
    part = (pieces // sides, width // pieces, columns)
    return pl.pallas_call(
        functools.partial(attention_kernel, pieces=pieces, earlier=1 if earlier else 0),
        grid_spec=pltpu.PrefetchScalarGridSpec(
            num_scalar_prefetch=1,
            grid=(count,),
            in_specs=[
                given, given, whole(wt.shape), whole(merge.shape), whole(bias.shape),
                whole((1, 8, width)), whole(cosine.shape), whole(sine.shape),
            ]
            + [whole(part)] * len(earlier),
            out_specs=[taken, taken, per(8, width), per(8, 2 * rows)]
            + [whole(part)] * sides,
            scratch_shapes=[
                pltpu.VMEM((width, SEQ), BF16),
                pltpu.VMEM((width, SEQ), BF16),
                pltpu.VMEM((wt.shape[0], SEQ), BF16),
                pltpu.VMEM((width, columns), F32),
            ],
        ),
        out_shape=[
            jax.ShapeDtypeStruct((count * SEQ, width), BF16),
            jax.ShapeDtypeStruct((count * SEQ, width), BF16),
            jax.ShapeDtypeStruct((count, 8, width), F32),
            jax.ShapeDtypeStruct((count, 8, 2 * rows), F32),
        ]
        + [jax.ShapeDtypeStruct(part, BF16)] * sides,
        compiler_params=params("arbitrary"),
        name="attention",
        cost_estimate=pl.CostEstimate(
            flops=count * 16_000_000_000, bytes_accessed=count * 12_000_000, transcendentals=0
        ),
    )(place, x, g, wt, merge, bias, vecs, cosine, sine, *earlier)


def feed(place, x, g, vecs, aout, din, at, weights, earlier, phases=(0, 1), begun=()):
    width = x.shape[1]
    groups, chunk, columns = weights[0].shape
    ff = columns // 2
    pieces = len(weights)
    sides = min(pieces, 2)
    given = pl.BlockSpec((SEQ, width), lambda s, place: (place[0], 0))
    part = (pieces // sides, chunk, 2 * columns)
    anywhere = pl.BlockSpec(memory_space=pl.ANY)
    first = 7 + pieces
    kept = 0 if begun else sides
    return pl.pallas_call(
        functools.partial(
            feed_kernel, pieces=pieces, earlier=1 if earlier else 0, at=at, phases=phases
        ),
        grid_spec=pltpu.PrefetchScalarGridSpec(
            num_scalar_prefetch=1,
            grid=(1,),
            in_specs=[given, given, whole(vecs.shape), whole((1, 8, width))]
            + [anywhere] * (2 + pieces + len(earlier))
            + [whole((2, SEQ, width))] * len(begun),
            out_specs=[whole((8, width)), whole((2, SEQ, width))] + [anywhere] * kept,
            scratch_shapes=[
                pltpu.VMEM((SEQ, width), BF16),
                pltpu.VMEM((width, SEQ), BF16),
                pltpu.VMEM((width, SEQ), BF16),
                pltpu.VMEM((width, SEQ), BF16),
                pltpu.VMEM((2, width, columns), BF16),
                pltpu.VMEM((2, width, columns), BF16),
                pltpu.VMEM((2, SEQ, width), BF16),
                pltpu.VMEM((sides, *part), BF16),
                pltpu.VMEM((2, SEQ, width), F32),
                pltpu.SemaphoreType.DMA((2, pieces, 2, 2)),
                pltpu.SemaphoreType.DMA((2,)),
                pltpu.SemaphoreType.DMA((2,)),
                pltpu.SemaphoreType.DMA((2,)),
            ],
        ),
        out_shape=[
            jax.ShapeDtypeStruct((8, width), F32),
            jax.ShapeDtypeStruct((2, SEQ, width), BF16 if phases[-1] == 1 else F32),
        ]
        + [jax.ShapeDtypeStruct(part, BF16)] * kept,
        input_output_aliases={first + k: 2 + k for k in range(len(earlier))},
        compiler_params=params("arbitrary"),
        name="feed",
        cost_estimate=pl.CostEstimate(
            flops=8_000_000_000 * len(phases), bytes_accessed=9_000_000, transcendentals=0
        ),
    )(place, x, g, vecs, vecs, aout, din, *weights, *earlier, *begun)


def prepare(place, weights, part):
    groups, chunk, columns = weights[0].shape
    pieces = len(weights)
    width = pieces * chunk
    rows = 9 * HD
    return pl.pallas_call(
        functools.partial(prepare_kernel, part=part),
        grid_spec=pltpu.PrefetchScalarGridSpec(
            num_scalar_prefetch=1,
            grid=(groups,),
            in_specs=[
                pl.BlockSpec((1, chunk, columns), lambda t, place: (t ^ place[2], 0, 0))
            ]
            * pieces,
            out_specs=[
                pl.BlockSpec((rows, width), lambda t, place: (t, 0)),
                pl.BlockSpec((3 * HD, width), lambda t, place: (t, 0)),
                pl.BlockSpec((1, 8, width), lambda t, place: (t, 0, 0)),
                pl.BlockSpec((1, 8, rows), lambda t, place: (t, 0, 0)),
            ],
            scratch_shapes=[pltpu.VMEM((width, columns), BF16)],
        ),
        out_shape=[
            jax.ShapeDtypeStruct((groups * rows, width), BF16),
            jax.ShapeDtypeStruct((groups * 3 * HD, width), BF16),
            jax.ShapeDtypeStruct((groups, 8, width), F32),
            jax.ShapeDtypeStruct((groups, 8, rows), F32),
        ],
        compiler_params=params("arbitrary"),
        name="prepare",
    )(place, *weights)


def trade(array, axis, mask):
    size = lax.axis_size(axis)
    return lax.ppermute(array, axis, [(i, i ^ mask) for i in range(size)])


def along(block):
    near, middle = trade(block, "tensor", 1), trade(block, "tensor", 2)
    return jnp.stack([block, near, middle, trade(tie(block, near), "tensor", 3)])


def across(block):
    return [block] + [trade(block, "dp", mask) for mask in (2, 4, 6)]


def both_cores(blocks):
    return [item for block in blocks for item in (block, trade(block, "dp", 1))]


def tie(array, after):
    return lax.optimization_barrier((array, after))[0]


def gather_both(early, late):
    own = early[None]
    others = [trade(early, "tensor", mask) for mask in (1, 2, 3)]
    own = across(own)
    others = jnp.stack(tie(others, own))
    late = along(tie(late, others))
    others = across(others)
    early = [jnp.concatenate(pair) for pair in zip(own, others)]
    ahead = late
    late = across(tie(late, early))
    early = both_cores([tie(item, ahead) for item in early])
    return early, late


def reduce_cores(kept, away):
    return kept.astype(F32) + trade(away, "dp", 1).astype(F32)


def exchange_across(pieces):
    return [pieces[0]] + [trade(pieces[k], "dp", 2 * k) for k in (1, 2, 3)]


def add_up(items):
    return sum(item.astype(F32) for item in items)


def body(
    block_input, cotangent, heads_weight, heads_bias, merge_weight, merge_bias, up_weight, up_bias,
    down_weight, down_bias, first_gain, first_shift, second_gain, second_shift,
):
    chunk = heads_weight.shape[0]
    owners = lax.axis_size("dp")
    groups = lax.axis_size("tensor")
    width = block_input.shape[1]
    spot = lax.axis_index("tensor")
    odd, pair = spot % 2, spot // 2
    total = block_input.shape[0] // SEQ
    count = total // 2
    fast = owners == 8 and groups == 4
    if fast:
        me = lax.axis_index("dp")
        facts = [odd * count, pair, spot, me // 2, me % 2]
    else:
        facts = [odd * count, pair, spot] + [jnp.zeros_like(spot)] * 2
    place = jnp.stack(facts).astype(jnp.int32)

    bias_part = heads_bias.shape[0]
    vectors = jnp.stack(
        [
            jnp.pad(heads_bias, (0, chunk - bias_part)), up_bias, merge_bias, down_bias,
            first_gain, first_shift, second_gain, second_shift,
        ],
        axis=1,
    )
    early = jnp.concatenate(
        [heads_weight, merge_weight.T, jnp.pad(vectors, ((0, 0), (0, 120)))], axis=1
    )
    late = jnp.concatenate([up_weight, down_weight.T], axis=1)
    if fast:
        early, late = gather_both(early, late)
    else:
        early, late = (
            lax.all_gather(item, ("tensor", "dp"), axis=0, tiled=True).reshape(groups, width, -1)
            for item in (early, late)
        )
        early, late = ([item[spot ^ jnp.arange(groups)]] for item in (early, late))
    rows = 9 * HD
    wt, merge, vecs, hbias = prepare(place, early, bias_part)
    if not fast:
        hbias = vecs[:, 0].reshape(groups, owners, chunk)[:, :, :bias_part]
        hbias = jnp.broadcast_to(hbias.reshape(groups, 1, rows), (groups, 8, rows))
    ff = up_weight.shape[1]
    cosine, sine = rotary_tables()
    swap = [(i, i ^ 1) for i in range(groups)]
    def shifted(i):
        return place.at[0].add(i)

    def attend(i, number, earlier, after):
        return attention(
            tie(shifted(i), after), block_input, cotangent, wt, merge, hbias, vecs, cosine, sine,
            number, len(early), earlier,
        )

    def advance(i, source, at, done, after):
        common = tie(shifted(i), after), block_input, cotangent, vecs, *source[:2], at, late
        sums, rows16, *grads = feed(*common, done[2:])
        return [rows16, sums, *grads], trade(rows16, "tensor", 1)

    lead = count - 1
    first = attend(0, lead, [], ())
    if fast:
        late = both_cores(tie(late, first[0]))
    second = attend(lead, 1, first[4:], late[0])
    done, others, totals = [], [], []
    wait = second[2]
    for i in range(count):
        source, at = (first, i) if i < lead else (second, 0)
        done, other = advance(i, source, at, done, wait)
        others.append((done[0], other))
        totals.append(done[1])
        if i == 0 and fast:
            heads_part = reduce_cores(*second[4:]).astype(BF16)
            wait = heads_part
        if i == 1:
            wait = others[0]
            if fast:
                heads_items = exchange_across(heads_part)
                wait = wait, heads_items
            blank = jnp.zeros(block_input.shape, BF16), jnp.zeros(block_input.shape, F32)
            blank = tie(blank, done[1])
            wait = wait, blank
    if fast:
        heads_cols = add_up(tie(heads_items, done[1])).astype(BF16)
    else:
        heads_cols = lax.psum_scatter(second[4][0], "dp", scatter_dimension=0, tiled=True)

    rows_a = first[2].sum(0) + second[2].sum(0)
    hb = (first[3].sum(0) + second[3].sum(0))[0]
    rows_f = sum(totals)
    hb = jnp.pad(hb.reshape(2, owners, bias_part), ((0, 0), (0, 0), (0, chunk - bias_part)))
    small = jnp.concatenate(
        [
            rows_a[0:2], rows_f[0:2], rows_a[2:3], rows_f[2:4], hb.reshape(2, width),
            jnp.zeros((3, width), F32),
        ],
        axis=0,
    )
    if fast:
        kept, away = done[2:]
        kept = reduce_cores(kept, away).astype(BF16)
        small = (small + trade(small, "dp", 1)).reshape(-1, 4 * ff)
        tail = small.shape[0]
        small = jnp.pad(small, ((0, 8 - tail), (0, 0))).astype(BF16)
        kept = tie(kept, others[-2][1])
        ready = kept
        feed_cols = add_up(exchange_across([jnp.concatenate([item, small]) for item in kept]))
        small = feed_cols[chunk : chunk + tail].reshape(-1, width)
        small = lax.dynamic_slice(small, (0, me * chunk), (small.shape[0], chunk))
        feed_cols = feed_cols[:chunk].astype(BF16)
    else:
        ready = done[1]
        feed_cols = lax.psum_scatter(done[2][0], "dp", scatter_dimension=0, tiled=True)
        small = lax.psum_scatter(small, "dp", scatter_dimension=1, tiled=True)

    def settle(mine, other):
        return mine.astype(F32) + trade(other, "tensor", 1).astype(F32)

    small = small + trade(
        jnp.concatenate([small[:5], small[6:7], small[5:6], small[7:]], axis=0), "tensor", 1
    )
    feed_sum = settle(
        *(
            jnp.concatenate([feed_cols[:, k : k + ff], feed_cols[:, k + 2 * ff : k + 3 * ff]], axis=1)
            for k in (0, ff)
        )
    )
    wide = 2 * rows
    heads_cols = jnp.concatenate(
        [
            heads_cols[:, :rows], heads_cols[:, wide : wide + 3 * HD],
            heads_cols[:, rows:wide], heads_cols[:, wide + 3 * HD :],
        ],
        axis=1,
    )
    heads_cols = tie(heads_cols, ready)
    others[-1] = others[-1][0], tie(others[-1][1], ready)
    half = rows + 3 * HD
    left, right = heads_cols[:, :half], heads_cols[:, half:]
    heads_sum = settle(jnp.where(odd == 0, left, right), jnp.where(odd == 0, right, left))

    layer_output, input_grad = tie(blank[0], done[1]), tie(blank[1], ready)
    for i, both in enumerate(others):
        for item, base in zip(both, (odd, 1 - odd)):
            at = (base * count + i) * SEQ
            layer_output = lax.dynamic_update_slice(layer_output, item[0], (at, 0))
            given = lax.dynamic_slice(cotangent, (at, 0), (SEQ, width))
            input_grad = lax.dynamic_update_slice(
                input_grad, item[1].astype(F32) + given.astype(F32), (at, 0)
            )
    return (
        layer_output,
        input_grad,
        heads_sum[:, :rows],
        jnp.where(odd == 0, small[7], small[8])[:bias_part],
        heads_sum[:, rows:].T,
        small[4],
        feed_sum[:, :ff],
        small[5],
        feed_sum[:, ff:].T,
        small[4],
        small[0],
        small[1],
        small[2],
        small[3],
    )


def solution(mesh):
    placed = (
        P("dp", None),
        P("dp", None),
        P("dp", "tensor"),
        P(("tensor", "dp")),
        P("tensor", "dp"),
        P("dp"),
        P("dp", "tensor"),
        P(("tensor", "dp")),
        P("tensor", "dp"),
        P("dp"),
        P("dp"),
        P("dp"),
        P("dp"),
        P("dp"),
    )
    return jax.shard_map(
        body,
        mesh=mesh,
        in_specs=placed,
        out_specs=placed,
        check_vma=False,
    )
```
